32 devices in a mesh: gz: 4 (over y, x), gy: 8 (over z, core).
Axes of the slice: x: 2, y: 2, z: 4, core: 2. Of those that a mesh axis runs over, the one named last changes fastest.
Arguments:
- velocity_x: bfloat16 [8, 128, 2048], P('gz', 'gy'), may hold values from -1.5 to 1.5
- velocity_y: bfloat16 [8, 128, 2048], P('gz', 'gy'), may hold values from -1.5 to 1.5
- velocity_z: bfloat16 [8, 128, 2048], P('gz', 'gy'), may hold values from -1.5 to 1.5
- owners: int32 [64, 1], replicated, may hold values from 0 to 7; in each aligned block of 64 rows (0 to 63, 64 to 127, ...) at most 16 rows name the same one
- coupling_below: float32 [8], replicated, may hold values from 0.5 to 2
- coupling_above: float32 [8], replicated, may hold values from 0.5 to 2
- metric: float32 [8], replicated, may hold values from 0.25 to 1
Outputs:
- pressure: float32 [8, 16, 2, 8, 128], P('gy', None, None, 'gz')
The draws below stay inside these ranges and needn't reach their ends.
Inputs may be any that keep to these rules, and one draw needn't show every extreme that they name: owners[m, 0] is the owner of retained mode kx = m; no owner has more than 16 modes, and some owner has exactly 16.
All inputs are finite; a program needn't handle non-finite values.
Results may differ from the reference program's by a relative error of at most 0.0003.
Values may be sent and summed in bfloat16 or wider, within the bound.
No kernel may reach another device: no remote copies, remote signals or barrier semaphores. Data moves between devices by JAX's collectives and lax.ppermute only.
A program may use at most 64 MiB of HBM per device.

```python
import math
import jax
import jax.numpy as jnp
import numpy as np
from jax import lax

NX = 2048
NY = 128
NZ = 8
KXR = 64
KYR = 128
CAP = 16
N_GY = 8


def levels(stream_key, extent, shards, low, top_value):
    def one(dim, shards_of):
        steps = jax.random.uniform(jax.random.fold_in(jax.random.fold_in(stream_key, 6), dim), (shards_of,), jnp.float32, low / len(shards), top_value / len(shards))
        return jnp.repeat(jnp.exp(steps), extent[dim] // shards_of).reshape((-1,) + (1,) * (len(extent) - dim - 1))

    level = one(*shards[0])
    for cut in shards[1:]:
        level = level * one(*cut)
    return level


def deal_out(stream_key, own, number, rows, number_of, top, bound, lean):
    order = jax.random.permutation(stream_key, number_of)
    crowded, ordinary = load_shares(number_of, rows * top, bound, lean, True), load_shares(number_of, rows * top, bound, lean, False)
    places = jnp.arange(number_of)

    def named(tallies, rotation):
        used = int((tallies > 0).sum())
        fixed = max(1, used // 4)
        shifted = fixed + (places - fixed + rotation * (used - fixed)) % max(1, number_of - fixed)
        return jnp.zeros((number_of,), jnp.int32).at[order[jnp.where(places < fixed, places, shifted)]].set(jnp.asarray(tallies, jnp.int32))

    tallies = jnp.where(number % 4 == 0, named(crowded, number // 4), named(ordinary, number - number // 4 - 1))
    mixed = jax.random.permutation(jax.random.fold_in(own, 3), number_of)
    source_of, receiver = mixed[0:number_of // 2 * 2:2], mixed[1:number_of // 2 * 2:2]
    margin = jnp.minimum(tallies[source_of] - 1, bound - tallies[receiver]) // 2
    margin = jnp.where((source_of == order[0]) | (receiver == order[0]) | (tallies[receiver] == 0), 0, jnp.maximum(margin, 0))
    shifted = jax.random.randint(jax.random.fold_in(own, 4), (number_of // 2,), 0, 1 << 20) % (margin + 1)
    tallies = tallies.at[source_of].add(-shifted).at[receiver].add(shifted)
    labels = jnp.searchsorted(jnp.cumsum(tallies), jnp.arange(rows * top), side="right").astype(jnp.int32)
    listing = labels.reshape(top, rows).T
    listing = listing[jax.random.permutation(jax.random.fold_in(own, 1), rows)]
    rotation = jax.random.randint(jax.random.fold_in(own, 2), (rows, 1), 0, top)
    return jnp.take_along_axis(listing, (jnp.arange(top)[None, :] + rotation) % top, axis=1)


def load_shares(count, total, bound, skew, full):
    portions = [(1 << 20) // math.isqrt(standing ** skew) + 1 for standing in range(1, count + 1)]
    largest = bound if full else min(bound, max(-(-total // count), total * portions[0] // sum(portions)))
    least = 1 if total - largest >= count - 1 else 0
    holding, surplus = [largest] + [least] * (count - 1), total - largest - least * (count - 1)
    while surplus > 0:
        movable = [i for i in range(1, count) if holding[i] < largest] or [i for i in range(1, count) if holding[i] < bound]
        whole, budget = sum([portions[i] for i in movable]), surplus
        for i in movable:
            more = min(bound - holding[i], max(1, budget * portions[i] // whole), surplus)
            holding[i] = holding[i] + more
            surplus = surplus - more
    return np.array(holding)


def gaussian(key, dims, width, bound, pieces=(), kind=jnp.bfloat16):
    values = jax.random.normal(key, dims, jnp.float32) * width
    if len(pieces) > 0:
        values = levels(key, dims, pieces, -0.22, 0.18) * values
    return jnp.clip(values, min=-bound, max=bound).astype(kind)


def setup_inputs(seed: int = 0) -> dict:
    streams_of = jax.random.split(jax.random.key(seed), 8)
    velocity_x = gaussian(streams_of[0], (NZ, NY, NX), 0.25, 1.5, ((0, 4), (1, 8)))
    velocity_y = gaussian(streams_of[1], (NZ, NY, NX), 0.25, 1.5, ((0, 4), (1, 8)))
    velocity_z = gaussian(streams_of[2], (NZ, NY, NX), 0.25, 1.5, ((0, 4), (1, 8)))
    owners_keys = jax.random.split(jax.random.fold_in(streams_of[3], 1), KXR // KXR)
    owners_turns = jax.random.permutation(jax.random.fold_in(streams_of[3], 3), KXR // KXR)
    owners = jax.vmap(lambda own, number: deal_out(jax.random.fold_in(streams_of[3], 2), own, number, KXR, N_GY, 1, CAP, 1))(owners_keys, owners_turns).reshape((KXR, 1))
    coupling_below = jnp.clip(jnp.exp(jax.random.uniform(streams_of[4], (NZ,), jnp.float32, math.log(0.5), math.log(2.0))), 0.5, 2.0)
    coupling_above = jnp.clip(jnp.exp(jax.random.uniform(streams_of[5], (NZ,), jnp.float32, math.log(0.5), math.log(2.0))), 0.5, 2.0)
    metric = jnp.clip(jnp.exp(jax.random.uniform(streams_of[6], (NZ,), jnp.float32, math.log(0.25), math.log(1.0))), 0.25, 1.0)
    return {"velocity_x": velocity_x, "velocity_y": velocity_y, "velocity_z": velocity_z, "owners": owners, "coupling_below": coupling_below, "coupling_above": coupling_above, "metric": metric}


SMAG_COEF = 0.12
STRAIN_FLOOR = 0.01
BASE_SHIFT = 0.004
MODE_SHIFT = 0.02

def shrink(field):
    return field[1:-1, 1:-1]

def centred_x(field):
    return (jnp.roll(field, -1, 2) - jnp.roll(field, 1, 2)) * 0.5

def slope_x(field):
    return shrink(centred_x(field))

def slope_y(field):
    return (field[1:-1, 2:] - field[1:-1, :-2]) * 0.5

def slope_z(field):
    return (field[2:, 1:-1] - field[:-2, 1:-1]) * 0.5

def second_x(field):
    return shrink(jnp.roll(field, -1, 2) + jnp.roll(field, 1, 2) - 2.0 * field)

def second_y(field):
    return field[1:-1, 2:] + field[1:-1, :-2] - 2.0 * shrink(field)

def second_z(field):
    return field[2:, 1:-1] + field[:-2, 1:-1] - 2.0 * shrink(field)

def mixed_yz(field):
    return 0.25 * (field[2:, 2:] - field[2:, :-2] - field[:-2, 2:] + field[:-2, :-2])

def pressure_source(extended):
    slopes = (slope_x, slope_y, slope_z)
    gradient = [[slopes[axis_two](extended[axis_one]) for axis_two in range(3)] for axis_one in range(3)]
    strain = {}
    for axis_one in range(3):
        for axis_two in range(axis_one, 3):
            strain[axis_one, axis_two] = 0.5 * (gradient[axis_one][axis_two] + gradient[axis_two][axis_one])
    squared = 2.0 * (strain[0, 0] * strain[0, 0] + strain[1, 1] * strain[1, 1] + strain[2, 2] * strain[2, 2])
    squared = squared + 4.0 * (strain[0, 1] * strain[0, 1] + strain[0, 2] * strain[0, 2] + strain[1, 2] * strain[1, 2])
    viscous = 2.0 * SMAG_COEF * jnp.sqrt(squared + STRAIN_FLOOR)
    stress = {}
    for pair_key in strain:
        stress[pair_key] = viscous * strain[pair_key]
    divergence = shrink(gradient[0][0] + gradient[1][1] + gradient[2][2])
    forcing = second_x(stress[0, 0]) + second_y(stress[1, 1]) + second_z(stress[2, 2])
    crossed = slope_y(centred_x(stress[0, 1])) + slope_z(centred_x(stress[0, 2])) + mixed_yz(stress[1, 2])
    return divergence + forcing + 2.0 * crossed

def slot_table(owners, groups, capacity):
    owner_of = owners[:, 0]
    one_hot = (owner_of[:, None] == jnp.arange(groups, dtype=jnp.int32)[None, :]).astype(jnp.int32)
    before = jnp.cumsum(one_hot, axis=0) - one_hot
    rank_in = lax.optimization_barrier(jnp.sum(before * one_hot, axis=1))
    slot_of = owner_of * capacity + rank_in
    matches = slot_of[None, :] == jnp.arange(groups * capacity, dtype=jnp.int32)[:, None]
    mode_ids = jnp.arange(owner_of.shape[0], dtype=jnp.int32)
    slot_mode = lax.optimization_barrier(jnp.sum(jnp.where(matches, mode_ids[None, :], 0), axis=1)).astype(jnp.int32)
    return (slot_mode, jnp.any(matches, axis=1))

def reference(velocity_x, velocity_y, velocity_z, owners, coupling_below, coupling_above, metric):
    stacked = jnp.stack([velocity_x, velocity_y, velocity_z])
    padded = jnp.pad(stacked, ((0, 0), (2, 2), (0, 0), (0, 0)))
    norm_factor = 1.0 / math.sqrt(NX * NY)
    ky_all = jnp.arange(KYR, dtype=jnp.int32) - KXR
    kx_all = jnp.arange(KXR, dtype=jnp.int32)
    ky_rows = jnp.mod(ky_all, NY)
    radius = ky_all[:, None] * ky_all[:, None] + kx_all[None, :] * kx_all[None, :]
    inside = radius <= KXR * KXR

    def one_level(layer_pos):
        slab_data = lax.dynamic_slice_in_dim(padded, layer_pos, 5, 1).astype(jnp.float32)
        slab_data = jnp.pad(slab_data, ((0, 0), (0, 0), (2, 2), (0, 0)))
        source = pressure_source(slab_data)[0]
        spectrum = jnp.fft.rfft(source, axis=1)[:, :KXR]
        spectrum = jnp.fft.fft(spectrum, axis=0)[ky_rows] * norm_factor
        spectrum = jnp.where(inside, spectrum, 0.0)
        return jnp.stack([jnp.real(spectrum), jnp.imag(spectrum)]).astype(jnp.float32)
    spectra = lax.map(one_level, jnp.arange(NZ, dtype=jnp.int32))
    kappa = radius.astype(jnp.float32) / float(KXR * KXR)
    pivots = []
    carried = []
    for layer_pos in range(NZ):
        diagonal = -(coupling_below[layer_pos] + coupling_above[layer_pos] + metric[layer_pos] * (BASE_SHIFT + MODE_SHIFT * kappa))
        rhs_now = spectra[layer_pos]
        if layer_pos == 0:
            pivot = diagonal
            value = rhs_now
        else:
            pivot = diagonal - coupling_below[layer_pos] * coupling_above[layer_pos - 1] / pivots[-1]
            value = rhs_now - coupling_below[layer_pos] * carried[-1] / pivots[-1]
        pivots.append(pivot)
        carried.append(value)
    solution = [None] * NZ
    current = carried[NZ - 1] / pivots[NZ - 1]
    solution[NZ - 1] = current
    for layer_pos in range(NZ - 2, -1, -1):
        current = (carried[layer_pos] - coupling_above[layer_pos] * current) / pivots[layer_pos]
        solution[layer_pos] = current
    field = jnp.stack(solution)
    slot_mode, slot_ok = slot_table(owners, N_GY, CAP)
    picked = jnp.take(field, slot_mode, axis=3)
    picked = jnp.transpose(picked, (3, 1, 0, 2)) * slot_ok[:, None, None, None].astype(jnp.float32)
    return picked.reshape(N_GY, CAP, 2, NZ, KYR)
```

```python
import functools
import math

import jax
import jax.numpy as jnp
import numpy as np
from jax import lax
from jax.experimental import pallas as pl
from jax.experimental.pallas import tpu as pltpu
from jax.sharding import PartitionSpec as P

CAP = 16
SMAG_COEF = 0.12
STRAIN_FLOOR = 0.01
BASE_SHIFT = 0.004
MODE_SHIFT = 0.02

CHUNK = 256
PAD_ROWS = 24
VMEM = pl.BlockSpec(memory_space=pltpu.VMEM)
SMEM = pl.BlockSpec(memory_space=pltpu.SMEM)


def split(value):
    high = value.astype(jnp.bfloat16)
    low = (value - high.astype(jnp.float32)).astype(jnp.bfloat16)
    return high, low


def split_table(table):
    high = table.astype(jnp.bfloat16)
    low = (table - high.astype(np.float64)).astype(jnp.bfloat16)
    return high, low


def matmul(left, right):
    return jnp.dot(left, right, preferred_element_type=jnp.float32)


def x_tables(width, kxr, grid_rows):
    norm = 1.0 / math.sqrt(width * grid_rows)
    phase = (np.arange(width)[:, None] * np.arange(kxr)[None, :] % width) * (2.0 * np.pi / width)
    table = np.stack([np.cos(phase) * norm, -np.sin(phase) * norm], axis=2)
    high, low = split_table(table.reshape(width, 2 * kxr))
    angle = np.arange(kxr) * (2.0 * np.pi / width)
    turn = np.stack([-np.sin(angle), np.sin(angle)], axis=1).reshape(2 * kxr) * 0.5
    second = np.repeat(-4.0 * np.sin(angle * 0.5) ** 2, 2)
    return np.concatenate([high, low], axis=1), np.stack([turn, second]).astype(np.float32)


def y_tables(rows, groups, kyr):
    grid_rows = rows * groups
    offset = np.concatenate([np.arange(rows), [-1, rows]])
    cells = (np.arange(groups)[:, None] * rows + offset[None, :]).reshape(-1)
    ky = np.arange(kyr) - kyr // 2
    phase = (ky[:, None] * cells[None, :] % grid_rows) * (2.0 * np.pi / grid_rows)
    valid = (cells >= 0) & (cells < grid_rows)
    table = np.concatenate([np.cos(phase), np.sin(phase)], axis=0) * valid[None, :]
    return split_table(table)


def mode_kernel(groups, capacity, kyr, levels, depth, own_ref, below, above, metric, pick, green):
    kxr = own_ref.shape[0]
    places, gy = lax.axis_index("gz"), lax.axis_index("gy")
    owner = jnp.broadcast_to(own_ref[...], (kxr, kxr))
    mode = lax.broadcasted_iota(jnp.int32, (kxr, kxr), 0)
    other = lax.broadcasted_iota(jnp.int32, (kxr, kxr), 1)
    owner_f = owner.astype(jnp.float32)
    same = (owner_f == owner_f.T) & (other < mode)
    rank = jnp.sum(jnp.where(same, 1.0, 0.0), axis=1, keepdims=True)
    slot = own_ref[...].astype(jnp.float32) * capacity + rank

    row = lax.broadcasted_iota(jnp.int32, (2 * kxr, groups * capacity * 2), 0)
    column = lax.broadcasted_iota(jnp.int32, (2 * kxr, groups * capacity * 2), 1)
    again = jnp.where(
        lax.broadcasted_iota(jnp.int32, (2 * kxr, kxr), 0) // 2
        == lax.broadcasted_iota(jnp.int32, (2 * kxr, kxr), 1),
        1.0,
        0.0,
    )
    slot_row = jnp.broadcast_to(slot, (kxr, kxr)).T[:1]
    slot_two = jnp.sum(again * slot_row, axis=1, keepdims=True).astype(jnp.int32)
    match = (slot_two * 2 + row % 2) == column
    pick[...] = jnp.where(match, 1.0, 0.0).astype(jnp.bfloat16)

    lane = lax.broadcasted_iota(jnp.int32, (kxr, 128), 1)
    here = gy * capacity + lane % (2 * capacity) // 2
    owned = slot.astype(jnp.int32) == here
    mode_id = lax.broadcasted_iota(jnp.int32, (kxr, 128), 0).astype(jnp.float32)
    kx = jnp.sum(jnp.where(owned, mode_id, 0.0), axis=0, keepdims=True)
    filled = jnp.sum(jnp.where(owned, 1.0, 0.0), axis=0, keepdims=True)

    at = lax.broadcasted_iota(jnp.int32, (8, 128), 1) // (2 * capacity)

    def turn(step, carry):
        start = pl.multiple_of(step * 8, 8)
        ky = (lax.broadcasted_iota(jnp.int32, (8, 128), 0) + (start - kyr // 2)).astype(jnp.float32)
        radius = kx * kx + ky * ky
        inside = jnp.where(radius <= float(kxr * kxr), filled, 0.0)
        shift = BASE_SHIFT + MODE_SHIFT * (radius / float(kxr * kxr))
        inverse = []
        for k in range(levels):
            pivot = -(below[k] + above[k] + metric[k] * shift)
            if k > 0:
                pivot = pivot - below[k] * above[k - 1] * inverse[-1]
            inverse.append(1.0 / pivot)
        for k in range(depth):
            target = places * depth + k
            forward = []
            for pos in range(levels):
                unit = jnp.where(target == pos, 1.0, 0.0)
                value = inside * unit
                if pos > 0:
                    value = value - above[pos - 1] * inverse[pos - 1] * forward[-1]
                forward.append(value)
            weights = [None] * levels
            for pos in range(levels - 1, -1, -1):
                value = forward[pos]
                if pos < levels - 1:
                    value = value - below[pos + 1] * weights[pos + 1]
                weights[pos] = value * inverse[pos]
            for block in range(levels // depth):
                total = jnp.zeros((8, 128), jnp.float32)
                for j in range(depth + 2):
                    pos = block * depth - 1 + j
                    if 0 <= pos < levels:
                        total = jnp.where(at == j, weights[pos], total)
                green[k, block, pl.ds(start, 8), :] = total
        return carry

    lax.fori_loop(0, kyr // 8, turn, 0)


def source_kernel(
    groups, planes, capacity,
    vx, vy, vz, z_low, z_high, y_low, y_high, table, factors, pick,
    out, total, lines,
):
    depth, rows, width = vx.shape
    modes = factors.shape[1]
    gz, gy = lax.axis_index("gz"), lax.axis_index("gy")
    first = jnp.where(gz == 0, 1.0, 0.0)
    last = jnp.where(gz == planes - 1, 1.0, 0.0)
    sub = lax.broadcasted_iota(jnp.int32, (8, CHUNK), 0)
    at_top, at_bottom = sub == 0, sub == 7
    ghost_rows = jnp.where(at_top & (gy == groups - 1) | at_bottom & (gy == 0), SMAG_COEF, 0.0)
    empty = jnp.zeros((8, CHUNK), jnp.float32)
    velocity = (vx, vy, vz)

    def up(field):
        return pltpu.roll(field, PAD_ROWS - 1, 0)

    def down(field):
        return pltpu.roll(field, 1, 0)

    def padded(field):
        return jnp.concatenate([field, empty], axis=0)

    def turn(step, carry):
        here = pl.multiple_of(step * CHUNK, CHUNK)
        before = pl.multiple_of(jnp.where(step == 0, width - 128, here - 128), 128)
        after = pl.multiple_of(jnp.where(step == width // CHUNK - 1, 0, here + CHUNK), 128)
        cells = pl.ds(here, CHUNK)
        rim_low = y_low[:, cells].astype(jnp.float32)
        rim_high = y_high[:, cells].astype(jnp.float32)

        own = [[velocity[i][k, :, cells].astype(jnp.float32) for k in range(depth)] for i in range(3)]
        below = [z_low[i, :, cells].astype(jnp.float32) for i in range(3)]
        above = [z_high[i, :, cells].astype(jnp.float32) for i in range(3)]

        def slope_x(i, k):
            window = jnp.concatenate(
                [
                    velocity[i][k, :, pl.ds(before, 128)].astype(jnp.float32),
                    own[i][k],
                    velocity[i][k, :, pl.ds(after, 128)].astype(jnp.float32),
                ],
                axis=1,
            )
            wide = CHUNK + 256
            difference = pltpu.roll(window, wide - 1, 1) - pltpu.roll(window, 1, 1)
            return difference[:, 128 : 128 + CHUNK]

        def slope_y(i, k):
            at = i * depth + k
            rim = jnp.where(
                at_top, rim_high[at : at + 1], jnp.where(at_bottom, rim_low[at : at + 1], 0.0)
            )
            field = jnp.concatenate([own[i][k], rim], axis=0)
            difference = up(field) - down(field)
            return difference[:rows], difference[rows:]

        def slope_z(i, k):
            lower = below[i] if k == 0 else own[i][k - 1]
            upper = above[i] if k == depth - 1 else own[i][k + 1]
            return upper - lower

        stress = []
        for k in range(depth):
            x = [slope_x(i, k) for i in range(3)]
            y, rim = zip(*[slope_y(i, k) for i in range(3)])
            z = [slope_z(i, k) for i in range(3)]
            e01, e02, e12 = y[0] + x[1], z[0] + x[2], z[1] + y[2]
            squared = 0.5 * (x[0] * x[0] + y[1] * y[1] + z[2] * z[2])
            squared = squared + 0.25 * (e01 * e01 + e02 * e02 + e12 * e12)
            viscous = SMAG_COEF * jnp.sqrt(squared + STRAIN_FLOOR)
            rim_squared = 0.5 * (rim[1] * rim[1]) + 0.25 * (rim[0] * rim[0] + rim[2] * rim[2])
            rim_viscous = ghost_rows * jnp.sqrt(rim_squared + STRAIN_FLOOR)
            s00, s11, s22 = viscous * x[0], viscous * y[1], viscous * z[2]
            t02 = viscous * e02
            t01 = jnp.concatenate([viscous * e01, rim_viscous * rim[0]], axis=0)
            p11 = jnp.concatenate([s11, rim_viscous * rim[1]], axis=0)
            t12 = jnp.concatenate([viscous * e12, rim_viscous * rim[2]], axis=0)
            divergence = 0.5 * (x[0] + y[1] + z[2])
            local = up(p11) + down(p11) + padded(divergence - 2.0 * (s11 + s22))
            cross = 0.25 * (up(t12) - down(t12))
            turned = up(t01) - down(t01)
            stress.append((s00, s22, t02, local, cross, turned))

        rim_u, rim_v, rim_w = [first * own[i][0] - last * own[i][depth - 1] for i in range(3)]
        squared = 0.5 * (rim_w * rim_w) + 0.25 * (rim_u * rim_u + rim_v * rim_v)
        viscous = SMAG_COEF * jnp.sqrt(squared + STRAIN_FLOOR)
        g22, g02, g12 = viscous * rim_w, viscous * rim_u, padded(viscous * rim_v)
        g_cross = 0.25 * (up(g12) - down(g12))
        g22 = padded(g22)

        plain = [None] * (depth + 2)
        turned = [None] * (depth + 2)
        plain[0] = padded(stress[0][1]) + stress[0][4]
        turned[0] = stress[0][2]
        for k in range(depth):
            plain[k + 1] = stress[k][3]
            turned[k + 1] = stress[k][5]
            if k > 0:
                plain[k + 1] = plain[k + 1] + padded(stress[k - 1][1]) - stress[k - 1][4]
                turned[k + 1] = turned[k + 1] - padded(stress[k - 1][2])
            if k < depth - 1:
                plain[k + 1] = plain[k + 1] + padded(stress[k + 1][1]) + stress[k + 1][4]
                turned[k + 1] = turned[k + 1] + padded(stress[k + 1][2])
        plain[1] = plain[1] + first * (g22 - g_cross)
        turned[1] = turned[1] - padded(first * g02)
        plain[depth] = plain[depth] + last * (g22 + g_cross)
        turned[depth] = turned[depth] + padded(last * g02)
        plain[depth + 1] = padded(stress[depth - 1][1]) - stress[depth - 1][4]
        turned[depth + 1] = -stress[depth - 1][2]

        fields = plain + turned + [stress[k][0] for k in range(depth)]
        half = lines.shape[0] // 2
        start = 0
        for field in fields:
            high, low = split(field)
            size = field.shape[0]
            lines[start : start + size, :] = high
            lines[half + start : half + start + size, :] = low
            start += size
        product = matmul(lines[...], table[cells, :])
        total[...] += product[:half] + product[half:]
        return carry

    total[...] = jnp.zeros_like(total)
    lax.fori_loop(0, width // CHUNK, turn, 0)

    summed = total[:, :modes] + total[:, modes:]
    even = lax.broadcasted_iota(jnp.int32, (1, modes), 1) % 2 == 0
    turn_factor, second_factor = factors[0:1], factors[1:2]

    def swapped(field):
        return jnp.where(even, pltpu.roll(field, modes - 1, 1), pltpu.roll(field, 1, 1))

    count = depth + 2
    spectrum = [summed[PAD_ROWS * j : PAD_ROWS * (j + 1)] for j in range(count)]
    start = PAD_ROWS * count
    zero_rows = jnp.zeros((PAD_ROWS - rows, modes), jnp.float32)
    for j in range(count):
        size = rows if j in (0, count - 1) else PAD_ROWS
        field = summed[start : start + size]
        if size == rows:
            field = jnp.concatenate([field, zero_rows], axis=0)
        spectrum[j] = spectrum[j] + turn_factor * swapped(field)
        start += size
    for k in range(depth):
        field = jnp.concatenate([summed[start : start + rows], zero_rows], axis=0)
        spectrum[k + 1] = spectrum[k + 1] + second_factor * field
        start += rows

    stacked = jnp.concatenate(spectrum, axis=0)
    high = stacked.astype(jnp.bfloat16)
    rest = stacked - high.astype(jnp.float32)
    middle, low = split(rest)
    selected = matmul(jnp.concatenate([high, middle, low], axis=0), pick[...])
    size = count * PAD_ROWS
    selected = selected[:size] + selected[size : 2 * size] + selected[2 * size :]

    lane = lax.broadcasted_iota(jnp.int32, (PAD_ROWS, 128), 1)
    share = 2 * capacity
    for half in range(groups * share // 128):
        pieces = [
            selected[PAD_ROWS * j : PAD_ROWS * (j + 1), 128 * half : 128 * (half + 1)]
            for j in range(count)
        ]
        for place in range(128 // share):
            block = jnp.zeros((PAD_ROWS, 128), jnp.float32)
            for j in range(count):
                distance = (share * (j - place)) % 128
                moved = pltpu.roll(pieces[j], distance, 1) if distance else pieces[j]
                block = jnp.where(lane // share == j, moved, block)
            rim = pltpu.roll(block[rows:], 1, 0)
            for plane in range(planes):
                base = (plane * groups + half * (128 // share) + place) * (rows + 2)
                out[base : base + rows, :] = block[:rows]
                out[base + rows : base + rows + 2, :] = rim[:2]


def solve_kernel(kyr, depth, capacity, received, basis_high, basis_low, green, out):
    planes = green.shape[1]
    reach = received.shape[0] // planes
    cosine = [jnp.zeros((kyr, 128), jnp.float32) for _ in range(depth)]
    sine = [jnp.zeros((kyr, 128), jnp.float32) for _ in range(depth)]
    for block in range(planes):
        high, low = split(received[block * reach : (block + 1) * reach, :])
        product = matmul(basis_high[...], high) + matmul(basis_high[...], low)
        product = product + matmul(basis_low[...], high)
        for k in range(depth):
            cosine[k] = cosine[k] + green[k, block] * product[:kyr]
            sine[k] = sine[k] + green[k, block] * product[kyr:]
    lane = lax.broadcasted_iota(jnp.int32, (kyr, 128), 1)
    share = 2 * capacity

    def gathered(field):
        distance = 64
        while distance >= share:
            field = field + pltpu.roll(field, distance, 1)
            distance //= 2
        return field

    result = jnp.zeros((kyr, 128), jnp.float32)
    for k in range(depth):
        real = gathered(cosine[k])
        turned = gathered(sine[k])
        turned = jnp.where(lane % 2 == 0, pltpu.roll(turned, 127, 1), -pltpu.roll(turned, 1, 1))
        result = jnp.where(lane // share == k, real + turned, result)
    flipped = result.T
    for k in range(depth):
        out[:, k, :] = flipped[k * share : (k + 1) * share]


def per_device(groups, planes, velocity_x, velocity_y, velocity_z, owners, below, above, metric):
    depth, rows, width = velocity_x.shape
    kxr = owners.shape[0]
    kyr = 2 * kxr
    levels = below.shape[0]
    limit = pltpu.CompilerParams(vmem_limit_bytes=32 * 1024 * 1024)
    fields = (velocity_x, velocity_y, velocity_z)

    upward = [(i, i + 1) for i in range(planes - 1)]
    sideways = [(i, i + 1) for i in range(groups - 1)]
    back = lambda pairs: [(j, i) for i, j in pairs]
    top = jnp.stack([field[depth - 1] for field in fields])
    bottom = jnp.stack([field[0] for field in fields])
    z_low = lax.ppermute(top, "gz", upward)
    z_high = lax.ppermute(bottom, "gz", back(upward))
    far = jnp.stack([field[:, rows - 1] for field in fields]).reshape(3 * depth, width)
    near = jnp.stack([field[:, 0] for field in fields]).reshape(3 * depth, width)
    y_low = lax.ppermute(far, "gy", sideways)
    y_high = lax.ppermute(near, "gy", back(sideways))

    columns = groups * CAP * 2
    pick, green = pl.pallas_call(
        functools.partial(mode_kernel, groups, CAP, kyr, levels, depth),
        out_shape=(
            jax.ShapeDtypeStruct((2 * kxr, columns), jnp.bfloat16),
            jax.ShapeDtypeStruct((depth, planes, kyr, 128), jnp.float32),
        ),
        in_specs=[VMEM, SMEM, SMEM, SMEM],
        out_specs=(VMEM, VMEM),
        compiler_params=limit,
    )(owners, below, above, metric)

    table, factors = x_tables(width, kxr, rows * groups)
    count = (depth + 2) * PAD_ROWS + depth * PAD_ROWS + (2 + depth) * rows
    reach = rows + 2
    outgoing = pl.pallas_call(
        functools.partial(source_kernel, groups, planes, CAP),
        out_shape=jax.ShapeDtypeStruct((planes * groups * reach, 128), jnp.float32),
        in_specs=[VMEM] * 10,
        out_specs=VMEM,
        scratch_shapes=[
            pltpu.VMEM((count, table.shape[1]), jnp.float32),
            pltpu.VMEM((2 * count, CHUNK), jnp.bfloat16),
        ],
        compiler_params=limit,
    )(*fields, z_low, z_high, y_low, y_high, jnp.asarray(table), jnp.asarray(factors), pick)

    outgoing = outgoing.reshape(planes * groups, reach // 2, 2, 128)
    received = lax.all_to_all(outgoing, ("gz", "gy"), split_axis=0, concat_axis=0, tiled=True)
    received = received.reshape(planes * groups * reach, 128)

    basis_high, basis_low = y_tables(rows, groups, kyr)
    solved = pl.pallas_call(
        functools.partial(solve_kernel, kyr, depth, CAP),
        out_shape=jax.ShapeDtypeStruct((CAP * 2, depth, kyr), jnp.float32),
        in_specs=[VMEM] * 4,
        out_specs=VMEM,
        compiler_params=limit,
    )(received, jnp.asarray(basis_high), jnp.asarray(basis_low), green)
    return solved.reshape(1, CAP, 2, depth, kyr)


def solution(mesh):
    placed = (P("gz", "gy", None), P("gz", "gy", None), P("gz", "gy", None), P(), P(), P(), P())
    return jax.shard_map(
        functools.partial(per_device, mesh.shape["gy"], mesh.shape["gz"]),
        mesh=mesh,
        in_specs=placed,
        out_specs=P("gy", None, None, "gz", None),
        check_vma=False,
    )
```

```python
import functools
import math

import jax
import jax.numpy as jnp
import numpy as np
from jax import lax
from jax.experimental import pallas as pl
from jax.experimental.pallas import tpu as pltpu
from jax.sharding import PartitionSpec as P

CAP = 16
SMAG_COEF = 0.12
STRAIN_FLOOR = 0.01
BASE_SHIFT = 0.004
MODE_SHIFT = 0.02

CHUNK = 256
PAD_ROWS = 24
VMEM = pl.BlockSpec(memory_space=pltpu.VMEM)
SMEM = pl.BlockSpec(memory_space=pltpu.SMEM)


def split(value):
    high = value.astype(jnp.bfloat16)
    low = (value - high.astype(jnp.float32)).astype(jnp.bfloat16)
    return high, low


def split_table(table):
    high = table.astype(jnp.bfloat16)
    low = (table - high.astype(np.float64)).astype(jnp.bfloat16)
    return high, low


def matmul(left, right):
    return jnp.dot(left, right, preferred_element_type=jnp.float32)


def x_tables(width, kxr, grid_rows):
    norm = 1.0 / math.sqrt(width * grid_rows)
    phase = (np.arange(width)[:, None] * np.arange(kxr)[None, :] % width) * (2.0 * np.pi / width)
    table = np.stack([np.cos(phase) * norm, -np.sin(phase) * norm], axis=2)
    high, low = split_table(table.reshape(width, 2 * kxr))
    angle = np.arange(kxr) * (2.0 * np.pi / width)
    turn = np.stack([-np.sin(angle), np.sin(angle)], axis=1).reshape(2 * kxr) * 0.5
    second = np.repeat(-4.0 * np.sin(angle * 0.5) ** 2, 2)
    return np.concatenate([high, low], axis=1), np.stack([turn, second]).astype(np.float32)


def y_tables(rows, groups, kyr):
    grid_rows = rows * groups
    offset = np.concatenate([np.arange(rows), [-1, rows]])
    cells = (np.arange(groups)[:, None] * rows + offset[None, :]).reshape(-1)
    ky = np.arange(kyr) - kyr // 2
    phase = (ky[:, None] * cells[None, :] % grid_rows) * (2.0 * np.pi / grid_rows)
    valid = (cells >= 0) & (cells < grid_rows)
    table = np.concatenate([np.cos(phase), np.sin(phase)], axis=0) * valid[None, :]
    return split_table(table)


def mode_kernel(
    groups, capacity, kyr, levels, depth,
    own_ref, below, above, metric, table, pick, green, held, arrived,
):
    copies = []
    part = table.shape[0] // arrived.shape[0]
    for i in range(arrived.shape[0]):
        at = pl.ds(i * part, part)
        copies.append(pltpu.make_async_copy(table.at[at], held.at[at], arrived.at[i]))
        copies[i].start()
    kxr = own_ref.shape[0]
    places, gy = lax.axis_index("gz"), lax.axis_index("gy")
    owner = jnp.broadcast_to(own_ref[...], (kxr, kxr))
    mode = lax.broadcasted_iota(jnp.int32, (kxr, kxr), 0)
    other = lax.broadcasted_iota(jnp.int32, (kxr, kxr), 1)
    owner_f = owner.astype(jnp.float32)
    same = (owner_f == owner_f.T) & (other < mode)
    rank = jnp.sum(jnp.where(same, 1.0, 0.0), axis=1, keepdims=True)
    slot = own_ref[...].astype(jnp.float32) * capacity + rank

    row = lax.broadcasted_iota(jnp.int32, (2 * kxr, groups * capacity * 2), 0)
    column = lax.broadcasted_iota(jnp.int32, (2 * kxr, groups * capacity * 2), 1)
    again = jnp.where(
        lax.broadcasted_iota(jnp.int32, (2 * kxr, kxr), 0) // 2
        == lax.broadcasted_iota(jnp.int32, (2 * kxr, kxr), 1),
        1.0,
        0.0,
    )
    slot_row = jnp.broadcast_to(slot, (kxr, kxr)).T[:1]
    slot_two = jnp.sum(again * slot_row, axis=1, keepdims=True).astype(jnp.int32)
    match = (slot_two * 2 + row % 2) == column
    pick[...] = jnp.where(match, 1.0, 0.0).astype(jnp.bfloat16)

    lane = lax.broadcasted_iota(jnp.int32, (kxr, 128), 1)
    here = gy * capacity + lane % (2 * capacity) // 2
    owned = slot.astype(jnp.int32) == here
    mode_id = lax.broadcasted_iota(jnp.int32, (kxr, 128), 0).astype(jnp.float32)
    kx = jnp.sum(jnp.where(owned, mode_id, 0.0), axis=0, keepdims=True)
    filled = jnp.sum(jnp.where(owned, 1.0, 0.0), axis=0, keepdims=True)

    size = 64
    at = lax.broadcasted_iota(jnp.int32, (size, 128), 1) // (2 * capacity)

    def turn(step, carry):
        start = pl.multiple_of(step * size, size)
        ky = lax.broadcasted_iota(jnp.int32, (size, 128), 0) + (start - kyr // 2)
        ky = ky.astype(jnp.float32)
        radius = kx * kx + ky * ky
        inside = jnp.where(radius <= float(kxr * kxr), filled, 0.0)
        shift = BASE_SHIFT + MODE_SHIFT * (radius / float(kxr * kxr))
        inverse = []
        for k in range(levels):
            pivot = -(below[k] + above[k] + metric[k] * shift)
            if k > 0:
                pivot = pivot - below[k] * above[k - 1] * inverse[-1]
            inverse.append(1.0 / pivot)
        for k in range(depth):
            target = places * depth + k
            forward = []
            for pos in range(levels):
                unit = jnp.where(target == pos, 1.0, 0.0)
                value = inside * unit
                if pos > 0:
                    value = value - above[pos - 1] * inverse[pos - 1] * forward[-1]
                forward.append(value)
            weights = [None] * levels
            for pos in range(levels - 1, -1, -1):
                value = forward[pos]
                if pos < levels - 1:
                    value = value - below[pos + 1] * weights[pos + 1]
                weights[pos] = value * inverse[pos]
            for block in range(levels // depth):
                total = jnp.zeros((size, 128), jnp.float32)
                for j in range(depth + 2):
                    pos = block * depth - 1 + j
                    if 0 <= pos < levels:
                        total = jnp.where(at == j, weights[pos], total)
                green[k, block, pl.ds(start, size), :] = total
        return carry

    lax.fori_loop(0, kyr // size, turn, 0)
    for copy in copies:
        copy.wait()


def pack_kernel(vx, vy, vz, plane_one, plane_two, row_one, row_two, held, arrived):
    rows = vx.shape[1]
    odd, odd_row = lax.axis_index("gz") % 2, lax.axis_index("gy") % 2
    copies = []
    for i, field in enumerate((vx, vy, vz)):
        for k in range(2):
            copies.append(pltpu.make_async_copy(field.at[k], held.at[i, k], arrived.at[i, k]))
    for copy in copies:
        copy.start()
    sub = lax.broadcasted_iota(jnp.int32, (8, vx.shape[2]), 0)
    bottom = jnp.zeros((8, vx.shape[2]), jnp.float32)
    top = bottom
    for i in range(3):
        copies[2 * i].wait()
        copies[2 * i + 1].wait()
        plane_one[i] = held[i, 1 - odd]
        plane_two[i] = held[i, odd]
        for k, level in enumerate((1 - odd, odd)):
            field = held[i, level].astype(jnp.float32)
            bottom = jnp.where(sub == 2 * i + k, field[0:1], bottom)
            top = jnp.where(sub == 2 * i + k, field[rows - 1 : rows], top)
    row_one[...] = jnp.where(odd_row == 0, top, bottom).astype(jnp.bfloat16)
    row_two[...] = jnp.where(odd_row == 0, bottom, top).astype(jnp.bfloat16)


def level_kernel(
    groups, planes, capacity, second,
    vx, vy, vz, plane, row_one, row_two, table, factors, *rest,
):
    if second:
        earlier, pick, out, lines = rest
    else:
        out, lines = rest
    depth, rows, width = vx.shape
    modes = factors.shape[1]
    gz, gy = lax.axis_index("gz"), lax.axis_index("gy")
    first = jnp.where(gz == 0, 1.0, 0.0)
    last = jnp.where(gz == planes - 1, 1.0, 0.0)
    odd, odd_row = gz % 2, gy % 2
    level = odd if second else 1 - odd
    upward = jnp.where(level == 1, 1.0, -1.0)
    sub = lax.broadcasted_iota(jnp.int32, (8, CHUNK), 0)
    at_top, at_bottom = sub == 0, sub == 7
    rim_one = at_top & (odd_row == 0) | at_bottom & (odd_row == 1)
    rim_two = at_top & (odd_row == 1) | at_bottom & (odd_row == 0)
    ghost_rows = jnp.where(at_top & (gy == groups - 1) | at_bottom & (gy == 0), SMAG_COEF, 0.0)
    empty = jnp.zeros((8, CHUNK), jnp.float32)
    velocity = (vx, vy, vz)

    def up(field):
        return pltpu.roll(field, PAD_ROWS - 1, 0)

    def down(field):
        return pltpu.roll(field, 1, 0)

    def padded(field):
        return jnp.concatenate([field, empty], axis=0)

    def turn(step):
        here = step * CHUNK
        before, after = (here - 128) % width, (here + CHUNK) % width
        cells = pl.ds(here, CHUNK)
        rows_one = row_one[:, cells].astype(jnp.float32)
        rows_two = row_two[:, cells].astype(jnp.float32)
        own = [velocity[i][level, :, cells].astype(jnp.float32) for i in range(3)]
        other = [velocity[i][1 - level, :, cells].astype(jnp.float32) for i in range(3)]

        def slope_x(i):
            window = jnp.concatenate(
                [
                    velocity[i][level, :, pl.ds(before, 128)].astype(jnp.float32),
                    own[i],
                    velocity[i][level, :, pl.ds(after, 128)].astype(jnp.float32),
                ],
                axis=1,
            )
            wide = CHUNK + 256
            difference = pltpu.roll(window, wide - 1, 1) - pltpu.roll(window, 1, 1)
            return difference[:, 128 : 128 + CHUNK]

        def slope_y(i):
            at = 2 * i + (1 if second else 0)
            rim = jnp.where(
                rim_one, rows_one[at : at + 1], jnp.where(rim_two, rows_two[at : at + 1], 0.0)
            )
            field = jnp.concatenate([own[i], rim], axis=0)
            difference = up(field) - down(field)
            return difference[:rows], difference[rows:]

        x = [slope_x(i) for i in range(3)]
        y, rim = zip(*[slope_y(i) for i in range(3)])
        z = [upward * (plane[i, :, cells].astype(jnp.float32) - other[i]) for i in range(3)]
        e01, e02, e12 = y[0] + x[1], z[0] + x[2], z[1] + y[2]
        squared = 0.5 * (x[0] * x[0] + y[1] * y[1] + z[2] * z[2])
        squared = squared + 0.25 * (e01 * e01 + e02 * e02 + e12 * e12)
        viscous = SMAG_COEF * jnp.sqrt(squared + STRAIN_FLOOR)
        rim_squared = 0.5 * (rim[1] * rim[1]) + 0.25 * (rim[0] * rim[0] + rim[2] * rim[2])
        rim_viscous = ghost_rows * jnp.sqrt(rim_squared + STRAIN_FLOOR)
        s00, s11, s22 = viscous * x[0], viscous * y[1], viscous * z[2]
        t02 = viscous * e02
        t01 = jnp.concatenate([viscous * e01, rim_viscous * rim[0]], axis=0)
        p11 = jnp.concatenate([s11, rim_viscous * rim[1]], axis=0)
        t12 = jnp.concatenate([viscous * e12, rim_viscous * rim[2]], axis=0)
        divergence = 0.5 * (x[0] + y[1] + z[2])
        local = up(p11) + down(p11) + padded(divergence - 2.0 * (s11 + s22))
        cross = 0.25 * (up(t12) - down(t12))
        turned = up(t01) - down(t01)
        fields = [local, cross, turned, s22, t02, s00]

        if not second:
            edge = first - last
            ghost = [edge * other[i] for i in range(3)]
            squared = 0.5 * (ghost[2] * ghost[2])
            squared = squared + 0.25 * (ghost[0] * ghost[0] + ghost[1] * ghost[1])
            viscous = SMAG_COEF * jnp.sqrt(squared + STRAIN_FLOOR)
            t12 = padded(viscous * ghost[1])
            cross = 0.25 * (up(t12) - down(t12))
            fields = fields + [cross, viscous * ghost[2], viscous * ghost[0]]

        half = lines.shape[0] // 2
        start = 0
        for field in fields:
            high, low = split(field)
            size = field.shape[0]
            lines[start : start + size, cells] = high
            lines[half + start : half + start + size, cells] = low
            start += size

    for step in range(width // CHUNK):
        turn(step)
    half = lines.shape[0] // 2
    product = matmul(lines[...], table[...])
    product = product[:half] + product[half:]
    summed = product[:, :modes] + product[:, modes:]
    even = lax.broadcasted_iota(jnp.int32, (1, modes), 1) % 2 == 0
    zero_rows = jnp.zeros((PAD_ROWS - rows, modes), jnp.float32)

    def slope(field):
        moved = jnp.where(even, pltpu.roll(field, modes - 1, 1), pltpu.roll(field, 1, 1))
        return factors[0:1] * moved

    def taken(start, size):
        field = summed[start : start + size]
        return jnp.concatenate([field, zero_rows], axis=0) if size == rows else field

    local, cross, turned = [taken(PAD_ROWS * i, PAD_ROWS) for i in range(3)]
    s22, t02, s00 = [taken(3 * PAD_ROWS + rows * i, rows) for i in range(3)]
    middle = local + slope(turned) + factors[1:2] * s00
    cross = cross + slope(t02)
    parts = [s22 + cross, middle, s22 - cross]
    if not second:
        start = 3 * PAD_ROWS + 3 * rows
        cross = taken(start, PAD_ROWS) + slope(taken(start + PAD_ROWS + rows, rows))
        parts.append(taken(start + PAD_ROWS, rows) + (last - first) * cross)
        for i, part in enumerate(parts):
            out[PAD_ROWS * i : PAD_ROWS * (i + 1), :] = part
        return

    before = [earlier[PAD_ROWS * i : PAD_ROWS * (i + 1), :] for i in range(4)]
    ghost = before.pop()
    lower = [jnp.where(odd == 1, p, q) for p, q in zip(before, parts)]
    upper = [jnp.where(odd == 1, q, p) for p, q in zip(before, parts)]
    spectrum = [
        lower[0],
        lower[1] + upper[0] + first * ghost,
        lower[2] + upper[1] + last * ghost,
        upper[2],
    ]
    count = len(spectrum)

    stacked = jnp.concatenate(spectrum, axis=0)
    high = stacked.astype(jnp.bfloat16)
    middle, low = split(stacked - high.astype(jnp.float32))
    selected = matmul(jnp.concatenate([high, middle, low], axis=0), pick[...])
    size = count * PAD_ROWS
    selected = selected[:size] + selected[size : 2 * size] + selected[2 * size :]

    lane = lax.broadcasted_iota(jnp.int32, (PAD_ROWS, 128), 1)
    share = 2 * capacity
    for half in range(groups * share // 128):
        pieces = [
            selected[PAD_ROWS * j : PAD_ROWS * (j + 1), 128 * half : 128 * (half + 1)]
            for j in range(count)
        ]
        for place in range(128 // share):
            block = jnp.zeros((PAD_ROWS, 128), jnp.float32)
            for j in range(count):
                distance = (share * (j - place)) % 128
                moved = pltpu.roll(pieces[j], distance, 1) if distance else pieces[j]
                block = jnp.where(lane // share == j, moved, block)
            rim = pltpu.roll(block[rows:], 1, 0)
            for side in range(planes):
                base = (side * groups + half * (128 // share) + place) * (rows + 2)
                out[base : base + rows, :] = block[:rows]
                out[base + rows : base + rows + 2, :] = rim[:2]


def solve_kernel(kyr, depth, capacity, received, basis_high, basis_low, green, out):
    planes = green.shape[1]
    reach = received.shape[0] // planes
    cosine = [jnp.zeros((kyr, 128), jnp.float32) for _ in range(depth)]
    sine = [jnp.zeros((kyr, 128), jnp.float32) for _ in range(depth)]
    for block in range(planes):
        high, low = split(received[block * reach : (block + 1) * reach, :])
        product = matmul(basis_high[...], high) + matmul(basis_high[...], low)
        product = product + matmul(basis_low[...], high)
        for k in range(depth):
            cosine[k] = cosine[k] + green[k, block] * product[:kyr]
            sine[k] = sine[k] + green[k, block] * product[kyr:]
    lane = lax.broadcasted_iota(jnp.int32, (kyr, 128), 1)
    share = 2 * capacity

    def gathered(field):
        distance = 64
        while distance >= share:
            field = field + pltpu.roll(field, distance, 1)
            distance //= 2
        return field

    result = jnp.zeros((kyr, 128), jnp.float32)
    for k in range(depth):
        real = gathered(cosine[k])
        turned = gathered(sine[k])
        turned = jnp.where(lane % 2 == 0, pltpu.roll(turned, 127, 1), -pltpu.roll(turned, 1, 1))
        result = jnp.where(lane // share == k, real + turned, result)
    flipped = result.T
    for k in range(depth):
        out[:, k, :] = flipped[k * share : (k + 1) * share]


def exchange(array, axis, size, shifted):
    pairs = [(i, i + 1) for i in range(shifted, size - 1, 2)]
    return lax.ppermute(array, axis, pairs + [(j, i) for i, j in pairs])


def per_device(groups, planes, velocity_x, velocity_y, velocity_z, owners, below, above, metric):
    depth, rows, width = velocity_x.shape
    kxr = owners.shape[0]
    kyr = 2 * kxr
    levels = below.shape[0]
    limit = pltpu.CompilerParams(vmem_limit_bytes=32 * 1024 * 1024)
    fields = (velocity_x, velocity_y, velocity_z)

    plane_shape = jax.ShapeDtypeStruct((3, rows, width), jnp.bfloat16)
    row_shape = jax.ShapeDtypeStruct((8, width), jnp.bfloat16)
    plane_one, plane_two, row_one, row_two = pl.pallas_call(
        pack_kernel,
        out_shape=(plane_shape, plane_shape, row_shape, row_shape),
        in_specs=[pl.BlockSpec(memory_space=pltpu.HBM)] * 3,
        out_specs=(VMEM,) * 4,
        scratch_shapes=[
            pltpu.VMEM((3, depth, rows, width), jnp.bfloat16),
            pltpu.SemaphoreType.DMA((3, depth)),
        ],
        compiler_params=limit,
    )(*[pltpu.with_memory_space_constraint(field, pltpu.HBM) for field in fields])
    plane_one = exchange(plane_one, "gz", planes, 0)
    plane_two = exchange(plane_two, "gz", planes, 1)
    row_one = exchange(row_one, "gy", groups, 0)
    row_two = exchange(row_two, "gy", groups, 1)

    columns = groups * CAP * 2
    table, factors = [jnp.asarray(array) for array in x_tables(width, kxr, rows * groups)]
    pick, green, table = pl.pallas_call(
        functools.partial(mode_kernel, groups, CAP, kyr, levels, depth),
        out_shape=(
            jax.ShapeDtypeStruct((2 * kxr, columns), jnp.bfloat16),
            jax.ShapeDtypeStruct((depth, planes, kyr, 128), jnp.float32),
            jax.ShapeDtypeStruct(table.shape, table.dtype),
        ),
        in_specs=[VMEM, SMEM, SMEM, SMEM, pl.BlockSpec(memory_space=pltpu.HBM)],
        out_specs=(VMEM, VMEM, VMEM),
        scratch_shapes=[pltpu.SemaphoreType.DMA((4,))],
        compiler_params=limit,
    )(owners, below, above, metric, pltpu.with_memory_space_constraint(table, pltpu.HBM))

    reach = rows + 2

    def level(second, plane, *rest):
        count = 3 * (PAD_ROWS + rows) + (0 if second else PAD_ROWS + 2 * rows)
        out_rows = planes * groups * reach if second else 4 * PAD_ROWS
        return pl.pallas_call(
            functools.partial(level_kernel, groups, planes, CAP, second),
            out_shape=jax.ShapeDtypeStruct((out_rows, 128 if second else 2 * kxr), jnp.float32),
            in_specs=[VMEM] * (8 + len(rest)),
            out_specs=VMEM,
            scratch_shapes=[
                pltpu.VMEM((2 * count, width), jnp.bfloat16),
            ],
            compiler_params=limit,
            cost_estimate=pl.CostEstimate(flops=10**8, bytes_accessed=10**6, transcendentals=0),
        )(*fields, plane, row_one, row_two, table, factors, *rest)

    earlier = level(False, plane_one)
    outgoing = level(True, plane_two, earlier, pick)
    outgoing = outgoing.reshape(planes * groups, reach // 2, 2, 128)
    received = lax.all_to_all(outgoing, ("gz", "gy"), split_axis=0, concat_axis=0, tiled=True)
    received = received.reshape(planes * groups * reach, 128)

    basis_high, basis_low = y_tables(rows, groups, kyr)
    solved = pl.pallas_call(
        functools.partial(solve_kernel, kyr, depth, CAP),
        out_shape=jax.ShapeDtypeStruct((CAP * 2, depth, kyr), jnp.float32),
        in_specs=[VMEM] * 4,
        out_specs=VMEM,
        compiler_params=limit,
    )(received, jnp.asarray(basis_high), jnp.asarray(basis_low), green)
    return solved.reshape(1, CAP, 2, depth, kyr)


def solution(mesh):
    placed = (P("gz", "gy", None), P("gz", "gy", None), P("gz", "gy", None), P(), P(), P(), P())
    return jax.shard_map(
        functools.partial(per_device, mesh.shape["gy"], mesh.shape["gz"]),
        mesh=mesh,
        in_specs=placed,
        out_specs=P("gy", None, None, "gz", None),
        check_vma=False,
    )
```

```python
import functools
import math

import jax
import jax.numpy as jnp
import numpy as np
from jax import lax
from jax.experimental import pallas as pl
from jax.experimental.pallas import tpu as pltpu
from jax.sharding import PartitionSpec as P

CAP = 16
SMAG_COEF = 0.12
STRAIN_FLOOR = 0.01
BASE_SHIFT = 0.004
MODE_SHIFT = 0.02

CHUNK = 256
PAD_ROWS = 24
CODES = 32000.0
STEPS = 32.0
VMEM = pl.BlockSpec(memory_space=pltpu.VMEM)
SMEM = pl.BlockSpec(memory_space=pltpu.SMEM)


def split(value):
    high = value.astype(jnp.bfloat16)
    low = (value - high.astype(jnp.float32)).astype(jnp.bfloat16)
    return high, low


def split_table(table):
    high = table.astype(jnp.bfloat16)
    low = (table - high.astype(np.float64)).astype(jnp.bfloat16)
    return high, low


def matmul(left, right):
    return jnp.dot(left, right, preferred_element_type=jnp.float32)


def x_tables(width, kxr, grid_rows):
    norm = 1.0 / math.sqrt(width * grid_rows)
    phase = (np.arange(width)[:, None] * np.arange(kxr)[None, :] % width) * (2.0 * np.pi / width)
    table = np.stack([np.cos(phase) * norm, -np.sin(phase) * norm], axis=2)
    high, low = split_table(table.reshape(width, 2 * kxr))
    angle = np.arange(kxr) * (2.0 * np.pi / width)
    turn = np.stack([-np.sin(angle), np.sin(angle)], axis=1).reshape(2 * kxr) * 0.5
    second = np.repeat(-4.0 * np.sin(angle * 0.5) ** 2, 2)
    return np.concatenate([high, low], axis=1), np.stack([turn, second]).astype(np.float32)


def y_tables(rows, groups, kyr):
    grid_rows = rows * groups
    nowhere = -grid_rows
    offset = np.concatenate([np.arange(rows), [-1, rows, nowhere, nowhere]])
    cells = (np.arange(groups)[:, None] * rows + offset[None, :]).reshape(-1)
    ky = np.arange(kyr) - kyr // 2
    phase = (ky[:, None] * cells[None, :] % grid_rows) * (2.0 * np.pi / grid_rows)
    valid = (cells >= 0) & (cells < grid_rows)
    table = np.concatenate([np.cos(phase), np.sin(phase)], axis=0) * valid[None, :]
    return np.concatenate(split_table(table), axis=0)


def mode_kernel(
    groups, capacity, kyr, levels, depth,
    own_ref, below, above, metric, table, pick, green, held, arrived,
):
    copies = []
    part = table.shape[0] // arrived.shape[0]
    for i in range(arrived.shape[0]):
        at = pl.ds(i * part, part)
        copies.append(pltpu.make_async_copy(table.at[at], held.at[at], arrived.at[i]))
        copies[i].start()
    kxr = own_ref.shape[0]
    places, gy = lax.axis_index("gz"), lax.axis_index("gy")
    owner = jnp.broadcast_to(own_ref[...], (kxr, kxr))
    mode = lax.broadcasted_iota(jnp.int32, (kxr, kxr), 0)
    other = lax.broadcasted_iota(jnp.int32, (kxr, kxr), 1)
    owner_f = owner.astype(jnp.float32)
    same = (owner_f == owner_f.T) & (other < mode)
    rank = jnp.sum(jnp.where(same, 1.0, 0.0), axis=1, keepdims=True)
    slot = own_ref[...].astype(jnp.float32) * capacity + rank

    row = lax.broadcasted_iota(jnp.int32, (2 * kxr, groups * capacity * 2), 0)
    column = lax.broadcasted_iota(jnp.int32, (2 * kxr, groups * capacity * 2), 1)
    again = jnp.where(
        lax.broadcasted_iota(jnp.int32, (2 * kxr, kxr), 0) // 2
        == lax.broadcasted_iota(jnp.int32, (2 * kxr, kxr), 1),
        1.0,
        0.0,
    )
    slot_row = jnp.broadcast_to(slot, (kxr, kxr)).T[:1]
    slot_two = jnp.sum(again * slot_row, axis=1, keepdims=True).astype(jnp.int32)
    match = (slot_two * 2 + row % 2) == column
    pick[...] = jnp.where(match, 1.0, 0.0).astype(jnp.bfloat16)

    lane = lax.broadcasted_iota(jnp.int32, (kxr, 128), 1)
    here = gy * capacity + lane % (2 * capacity) // 2
    owned = slot.astype(jnp.int32) == here
    mode_id = lax.broadcasted_iota(jnp.int32, (kxr, 128), 0).astype(jnp.float32)
    kx = jnp.sum(jnp.where(owned, mode_id, 0.0), axis=0, keepdims=True)
    filled = jnp.sum(jnp.where(owned, 1.0, 0.0), axis=0, keepdims=True)

    size = 64
    at = lax.broadcasted_iota(jnp.int32, (size, 128), 1) // (2 * capacity)

    def turn(step, carry):
        start = pl.multiple_of(step * size, size)
        ky = lax.broadcasted_iota(jnp.int32, (size, 128), 0) + (start - kyr // 2)
        ky = ky.astype(jnp.float32)
        radius = kx * kx + ky * ky
        inside = jnp.where(radius <= float(kxr * kxr), filled, 0.0)
        shift = BASE_SHIFT + MODE_SHIFT * (radius / float(kxr * kxr))
        inverse = []
        for k in range(levels):
            pivot = -(below[k] + above[k] + metric[k] * shift)
            if k > 0:
                pivot = pivot - below[k] * above[k - 1] * inverse[-1]
            inverse.append(1.0 / pivot)
        for k in range(depth):
            target = places * depth + k
            forward = []
            for pos in range(levels):
                unit = jnp.where(target == pos, 1.0, 0.0)
                value = inside * unit
                if pos > 0:
                    value = value - above[pos - 1] * inverse[pos - 1] * forward[-1]
                forward.append(value)
            weights = [None] * levels
            for pos in range(levels - 1, -1, -1):
                value = forward[pos]
                if pos < levels - 1:
                    value = value - below[pos + 1] * weights[pos + 1]
                weights[pos] = value * inverse[pos]
            for block in range(levels // depth):
                total = jnp.zeros((size, 128), jnp.float32)
                for j in range(depth + 2):
                    pos = block * depth - 1 + j
                    if 0 <= pos < levels:
                        total = jnp.where(at == j, weights[pos], total)
                green[k, block, pl.ds(start, size), :] = total
        return carry

    lax.fori_loop(0, kyr // size, turn, 0)
    for copy in copies:
        copy.wait()


def pack_kernel(vx, vy, vz, plane_one, plane_two, row_one, row_two, held, arrived):
    rows = vx.shape[1]
    odd, odd_row = lax.axis_index("gz") % 2, lax.axis_index("gy") % 2
    copies = []
    for i, field in enumerate((vx, vy, vz)):
        for k in range(2):
            copies.append(pltpu.make_async_copy(field.at[k], held.at[i, k], arrived.at[i, k]))
    for copy in copies:
        copy.start()
    sub = lax.broadcasted_iota(jnp.int32, (8, vx.shape[2]), 0)
    bottom = jnp.zeros((8, vx.shape[2]), jnp.float32)
    top = bottom
    for i in range(3):
        copies[2 * i].wait()
        copies[2 * i + 1].wait()
        plane_one[i] = held[i, 1 - odd]
        plane_two[i] = held[i, odd]
        for k, level in enumerate((1 - odd, odd)):
            field = held[i, level].astype(jnp.float32)
            bottom = jnp.where(sub == 2 * i + k, field[0:1], bottom)
            top = jnp.where(sub == 2 * i + k, field[rows - 1 : rows], top)
    row_one[...] = jnp.where(odd_row == 0, top, bottom).astype(jnp.bfloat16)
    row_two[...] = jnp.where(odd_row == 0, bottom, top).astype(jnp.bfloat16)


def level_kernel(
    groups, planes, capacity, second,
    vx, vy, vz, plane, row_one, row_two, table, factors, *rest,
):
    if second:
        earlier, pick, out, lines, codes = rest
    else:
        out, lines = rest
    depth, rows, width = vx.shape
    modes = factors.shape[1]
    gz, gy = lax.axis_index("gz"), lax.axis_index("gy")
    first = jnp.where(gz == 0, 1.0, 0.0)
    last = jnp.where(gz == planes - 1, 1.0, 0.0)
    odd, odd_row = gz % 2, gy % 2
    level = odd if second else 1 - odd
    upward = jnp.where(level == 1, 1.0, -1.0)
    sub = lax.broadcasted_iota(jnp.int32, (8, CHUNK), 0)
    at_top, at_bottom = sub == 0, sub == 7
    rim_one = at_top & (odd_row == 0) | at_bottom & (odd_row == 1)
    rim_two = at_top & (odd_row == 1) | at_bottom & (odd_row == 0)
    ghost_rows = jnp.where(at_top & (gy == groups - 1) | at_bottom & (gy == 0), SMAG_COEF, 0.0)
    empty = jnp.zeros((8, CHUNK), jnp.float32)
    velocity = (vx, vy, vz)

    def up(field):
        return pltpu.roll(field, PAD_ROWS - 1, 0)

    def down(field):
        return pltpu.roll(field, 1, 0)

    def padded(field):
        return jnp.concatenate([field, empty], axis=0)

    def turn(step):
        here = step * CHUNK
        before, after = (here - 128) % width, (here + CHUNK) % width
        cells = pl.ds(here, CHUNK)
        rows_one = row_one[:, cells].astype(jnp.float32)
        rows_two = row_two[:, cells].astype(jnp.float32)
        own = [velocity[i][level, :, cells].astype(jnp.float32) for i in range(3)]
        other = [velocity[i][1 - level, :, cells].astype(jnp.float32) for i in range(3)]

        def slope_x(i):
            window = jnp.concatenate(
                [
                    velocity[i][level, :, pl.ds(before, 128)].astype(jnp.float32),
                    own[i],
                    velocity[i][level, :, pl.ds(after, 128)].astype(jnp.float32),
                ],
                axis=1,
            )
            wide = CHUNK + 256
            difference = pltpu.roll(window, wide - 1, 1) - pltpu.roll(window, 1, 1)
            return difference[:, 128 : 128 + CHUNK]

        def slope_y(i):
            at = 2 * i + (1 if second else 0)
            rim = jnp.where(
                rim_one, rows_one[at : at + 1], jnp.where(rim_two, rows_two[at : at + 1], 0.0)
            )
            field = jnp.concatenate([own[i], rim], axis=0)
            difference = up(field) - down(field)
            return difference[:rows], difference[rows:]

        x = [slope_x(i) for i in range(3)]
        y, rim = zip(*[slope_y(i) for i in range(3)])
        z = [upward * (plane[i, :, cells].astype(jnp.float32) - other[i]) for i in range(3)]
        e01, e02, e12 = y[0] + x[1], z[0] + x[2], z[1] + y[2]
        squared = 0.5 * (x[0] * x[0] + y[1] * y[1] + z[2] * z[2])
        squared = squared + 0.25 * (e01 * e01 + e02 * e02 + e12 * e12)
        viscous = SMAG_COEF * jnp.sqrt(squared + STRAIN_FLOOR)
        rim_squared = 0.5 * (rim[1] * rim[1]) + 0.25 * (rim[0] * rim[0] + rim[2] * rim[2])
        rim_viscous = ghost_rows * jnp.sqrt(rim_squared + STRAIN_FLOOR)
        s00, s11, s22 = viscous * x[0], viscous * y[1], viscous * z[2]
        t02 = viscous * e02
        t01 = jnp.concatenate([viscous * e01, rim_viscous * rim[0]], axis=0)
        p11 = jnp.concatenate([s11, rim_viscous * rim[1]], axis=0)
        t12 = jnp.concatenate([viscous * e12, rim_viscous * rim[2]], axis=0)
        divergence = 0.5 * (x[0] + y[1] + z[2])
        local = up(p11) + down(p11) + padded(divergence - 2.0 * (s11 + s22))
        cross = 0.25 * (up(t12) - down(t12))
        turned = up(t01) - down(t01)
        fields = [local, cross, turned, s22, t02, s00]

        if not second:
            edge = first - last
            ghost = [edge * other[i] for i in range(3)]
            squared = 0.5 * (ghost[2] * ghost[2])
            squared = squared + 0.25 * (ghost[0] * ghost[0] + ghost[1] * ghost[1])
            viscous = SMAG_COEF * jnp.sqrt(squared + STRAIN_FLOOR)
            t12 = padded(viscous * ghost[1])
            cross = 0.25 * (up(t12) - down(t12))
            fields = fields + [cross, viscous * ghost[2], viscous * ghost[0]]

        half = lines.shape[0] // 2
        start = 0
        for field in fields:
            high, low = split(field)
            size = field.shape[0]
            lines[start : start + size, cells] = high
            lines[half + start : half + start + size, cells] = low
            start += size

    for step in range(width // CHUNK):
        turn(step)
    half = lines.shape[0] // 2
    product = matmul(lines[...], table[...])
    product = product[:half] + product[half:]
    summed = product[:, :modes] + product[:, modes:]
    even = lax.broadcasted_iota(jnp.int32, (1, modes), 1) % 2 == 0
    zero_rows = jnp.zeros((PAD_ROWS - rows, modes), jnp.float32)

    def slope(field):
        moved = jnp.where(even, pltpu.roll(field, modes - 1, 1), pltpu.roll(field, 1, 1))
        return factors[0:1] * moved

    def taken(start, size):
        field = summed[start : start + size]
        return jnp.concatenate([field, zero_rows], axis=0) if size == rows else field

    local, cross, turned = [taken(PAD_ROWS * i, PAD_ROWS) for i in range(3)]
    s22, t02, s00 = [taken(3 * PAD_ROWS + rows * i, rows) for i in range(3)]
    middle = local + slope(turned) + factors[1:2] * s00
    cross = cross + slope(t02)
    parts = [s22 + cross, middle, s22 - cross]
    if not second:
        start = 3 * PAD_ROWS + 3 * rows
        cross = taken(start, PAD_ROWS) + slope(taken(start + PAD_ROWS + rows, rows))
        parts.append(taken(start + PAD_ROWS, rows) + (last - first) * cross)
        for i, part in enumerate(parts):
            out[PAD_ROWS * i : PAD_ROWS * (i + 1), :] = part
        return

    before = [earlier[PAD_ROWS * i : PAD_ROWS * (i + 1), :] for i in range(4)]
    ghost = before.pop()
    lower = [jnp.where(odd == 1, p, q) for p, q in zip(before, parts)]
    upper = [jnp.where(odd == 1, q, p) for p, q in zip(before, parts)]
    spectrum = [
        lower[0],
        lower[1] + upper[0] + first * ghost,
        lower[2] + upper[1] + last * ghost,
        upper[2],
    ]
    count = len(spectrum)

    stacked = jnp.concatenate(spectrum, axis=0)
    high = stacked.astype(jnp.bfloat16)
    middle, low = split(stacked - high.astype(jnp.float32))
    selected = matmul(jnp.concatenate([high, middle, low], axis=0), pick[...])
    size = count * PAD_ROWS
    selected = selected[:size] + selected[size : 2 * size] + selected[2 * size :]

    lane = lax.broadcasted_iota(jnp.int32, (PAD_ROWS, 128), 1)
    empty_block = jnp.zeros((PAD_ROWS, 128), jnp.float32)
    sub_lanes = lax.broadcasted_iota(jnp.int32, (8, 128), 0)
    share = 2 * capacity
    for half in range(groups * share // 128):
        pieces = [
            selected[PAD_ROWS * j : PAD_ROWS * (j + 1), 128 * half : 128 * (half + 1)]
            for j in range(count)
        ]
        for place in range(128 // share):
            block = empty_block
            for j in range(count):
                distance = (share * (j - place)) % 128
                moved = pltpu.roll(pieces[j], distance, 1) if distance else pieces[j]
                block = jnp.where(lane // share == j, moved, block)
            largest = jnp.max(jnp.abs(block), axis=0, keepdims=True)
            power = jnp.floor(jnp.log2(jnp.maximum(largest, 1e-35)) * STEPS) + 1.0
            block = jnp.floor(block * (CODES * jnp.exp2(power * (-1.0 / STEPS))) + 0.5)
            rim = pltpu.roll(block[rows:], 1, 0)
            rim = jnp.where(sub_lanes < 2, rim, jnp.where(sub_lanes == 2, power, 0.0))
            for side in range(planes):
                base = (side * groups + half * (128 // share) + place) * (rows + 4)
                codes[base : base + rows, :] = block[:rows]
                codes[base + rows : base + rows + 4, :] = rim[:4]
    out[...] = codes[...].astype(jnp.int32).astype(jnp.int16)


def solve_kernel(kyr, depth, capacity, reach, received, basis, green, out, codes):
    planes = green.shape[1]
    sources = received.shape[0] // reach
    codes[...] = received[...].astype(jnp.int32).astype(jnp.float32)
    power = codes[pl.ds(reach - 2, sources, stride=reach), :]
    scale = jnp.exp2(power * (1.0 / STEPS)) * (1.0 / CODES)
    row = lax.broadcasted_iota(jnp.int32, (2 * reach, 128), 0)
    values = []
    for pair in range(0, sources, 2):
        factor = jnp.where(row < reach, scale[pair : pair + 1], scale[pair + 1 : pair + 2])
        values.append(codes[pair * reach : (pair + 2) * reach, :] * factor)
    each = sources // planes // 2
    blocks = [jnp.concatenate(values[i * each : (i + 1) * each], axis=0) for i in range(planes)]
    high, low = split(jnp.concatenate(blocks, axis=1))
    product = matmul(basis[...], high)
    product = product[: 2 * kyr] + product[2 * kyr :] + matmul(basis[: 2 * kyr, :], low)
    cosine = [jnp.zeros((kyr, 128), jnp.float32) for _ in range(depth)]
    sine = [jnp.zeros((kyr, 128), jnp.float32) for _ in range(depth)]
    for block in range(planes):
        lanes = slice(block * 128, (block + 1) * 128)
        for k in range(depth):
            cosine[k] = cosine[k] + green[k, block] * product[:kyr, lanes]
            sine[k] = sine[k] + green[k, block] * product[kyr:, lanes]
    lane = lax.broadcasted_iota(jnp.int32, (kyr, 128), 1)
    share = 2 * capacity

    def gathered(field):
        distance = 64
        while distance >= share:
            field = field + pltpu.roll(field, distance, 1)
            distance //= 2
        return field

    result = jnp.zeros((kyr, 128), jnp.float32)
    for k in range(depth):
        real = gathered(cosine[k])
        turned = gathered(sine[k])
        turned = jnp.where(lane % 2 == 0, pltpu.roll(turned, 127, 1), -pltpu.roll(turned, 1, 1))
        result = jnp.where(lane // share == k, real + turned, result)
    flipped = result.T
    for k in range(depth):
        out[:, k, :] = flipped[k * share : (k + 1) * share]


def exchange(array, axis, size, shifted):
    pairs = [(i, i + 1) for i in range(shifted, size - 1, 2)]
    return lax.ppermute(array, axis, pairs + [(j, i) for i, j in pairs])


def per_device(groups, planes, velocity_x, velocity_y, velocity_z, owners, below, above, metric):
    depth, rows, width = velocity_x.shape
    kxr = owners.shape[0]
    kyr = 2 * kxr
    levels = below.shape[0]
    limit = pltpu.CompilerParams(vmem_limit_bytes=32 * 1024 * 1024)
    fields = (velocity_x, velocity_y, velocity_z)

    plane_shape = jax.ShapeDtypeStruct((3, rows, width), jnp.bfloat16)
    row_shape = jax.ShapeDtypeStruct((8, width), jnp.bfloat16)
    plane_one, plane_two, row_one, row_two = pl.pallas_call(
        pack_kernel,
        out_shape=(plane_shape, plane_shape, row_shape, row_shape),
        in_specs=[pl.BlockSpec(memory_space=pltpu.HBM)] * 3,
        out_specs=(VMEM,) * 4,
        scratch_shapes=[
            pltpu.VMEM((3, depth, rows, width), jnp.bfloat16),
            pltpu.SemaphoreType.DMA((3, depth)),
        ],
        compiler_params=limit,
    )(*[pltpu.with_memory_space_constraint(field, pltpu.HBM) for field in fields])
    plane_one = exchange(plane_one, "gz", planes, 0)
    plane_two = exchange(plane_two, "gz", planes, 1)
    row_one = exchange(row_one, "gy", groups, 0)
    row_two = exchange(row_two, "gy", groups, 1)

    columns = groups * CAP * 2
    table, factors = [jnp.asarray(array) for array in x_tables(width, kxr, rows * groups)]
    pick, green, table = pl.pallas_call(
        functools.partial(mode_kernel, groups, CAP, kyr, levels, depth),
        out_shape=(
            jax.ShapeDtypeStruct((2 * kxr, columns), jnp.bfloat16),
            jax.ShapeDtypeStruct((depth, planes, kyr, 128), jnp.float32),
            jax.ShapeDtypeStruct(table.shape, table.dtype),
        ),
        in_specs=[VMEM, SMEM, SMEM, SMEM, pl.BlockSpec(memory_space=pltpu.HBM)],
        out_specs=(VMEM, VMEM, VMEM),
        scratch_shapes=[pltpu.SemaphoreType.DMA((4,))],
        compiler_params=limit,
    )(owners, below, above, metric, pltpu.with_memory_space_constraint(table, pltpu.HBM))

    reach = rows + 4

    def level(second, plane, *rest):
        count = 3 * (PAD_ROWS + rows) + (0 if second else PAD_ROWS + 2 * rows)
        out_rows = planes * groups * reach if second else 4 * PAD_ROWS
        return pl.pallas_call(
            functools.partial(level_kernel, groups, planes, CAP, second),
            out_shape=jax.ShapeDtypeStruct(
                (out_rows, 128 if second else 2 * kxr), jnp.int16 if second else jnp.float32
            ),
            in_specs=[VMEM] * (8 + len(rest)),
            out_specs=VMEM,
            scratch_shapes=[pltpu.VMEM((2 * count, width), jnp.bfloat16)]
            + ([pltpu.VMEM((out_rows, 128), jnp.float32)] if second else []),
            compiler_params=limit,
            cost_estimate=pl.CostEstimate(flops=10**8, bytes_accessed=10**6, transcendentals=0),
        )(*fields, plane, row_one, row_two, table, factors, *rest)

    earlier = level(False, plane_one)
    outgoing = level(True, plane_two, earlier, pick)
    outgoing = outgoing.reshape(planes * groups, reach // 2, 2, 128)
    received = lax.all_to_all(outgoing, ("gz", "gy"), split_axis=0, concat_axis=0, tiled=True)
    received = received.reshape(planes * groups * reach, 128)

    basis = jnp.asarray(y_tables(rows, groups, kyr))
    solved = pl.pallas_call(
        functools.partial(solve_kernel, kyr, depth, CAP, reach),
        out_shape=jax.ShapeDtypeStruct((CAP * 2, depth, kyr), jnp.float32),
        in_specs=[VMEM] * 3,
        out_specs=VMEM,
        scratch_shapes=[pltpu.VMEM(received.shape, jnp.float32)],
        compiler_params=limit,
    )(received, basis, green)
    return solved.reshape(1, CAP, 2, depth, kyr)


def solution(mesh):
    placed = (P("gz", "gy", None), P("gz", "gy", None), P("gz", "gy", None), P(), P(), P(), P())
    return jax.shard_map(
        functools.partial(per_device, mesh.shape["gy"], mesh.shape["gz"]),
        mesh=mesh,
        in_specs=placed,
        out_specs=P("gy", None, None, "gz", None),
        check_vma=False,
    )
```

```python
import functools
import math

import jax
import jax.numpy as jnp
import numpy as np
from jax import lax
from jax.experimental import pallas as pl
from jax.experimental.pallas import tpu as pltpu
from jax.sharding import PartitionSpec as P

CAP = 16
SMAG_COEF = 0.12
STRAIN_FLOOR = 0.01
BASE_SHIFT = 0.004
MODE_SHIFT = 0.02

CHUNK = 256
PAD_ROWS = 24
COST = pl.CostEstimate(flops=10**9, bytes_accessed=10**7, transcendentals=0)
CODES = 32000.0
STEPS = 32.0
VMEM = pl.BlockSpec(memory_space=pltpu.VMEM)
HBM = pl.BlockSpec(memory_space=pltpu.HBM)
SMEM = pl.BlockSpec(memory_space=pltpu.SMEM)


def split(value):
    high = value.astype(jnp.bfloat16)
    low = (value - high.astype(jnp.float32)).astype(jnp.bfloat16)
    return high, low


def split_table(table, parts):
    pieces = []
    for _ in range(parts):
        pieces.append(table.astype(jnp.bfloat16))
        table = table - pieces[-1].astype(np.float64)
    return pieces


def matmul(left, right):
    return jnp.dot(left, right, preferred_element_type=jnp.float32)


def x_tables(width, kxr, grid_rows):
    norm = 1.0 / math.sqrt(width * grid_rows)
    phase = (np.arange(width)[:, None] * np.arange(kxr)[None, :] % width) * (2.0 * np.pi / width)
    table = np.stack([np.cos(phase) * norm, -np.sin(phase) * norm], axis=2)
    pieces = split_table(table.reshape(width, 2 * kxr), 2)
    angle = np.arange(kxr) * (2.0 * np.pi / width)
    turn = np.stack([-np.sin(angle), np.sin(angle)], axis=1).reshape(2 * kxr) * 0.5
    second = np.repeat(-4.0 * np.sin(angle * 0.5) ** 2, 2)
    return np.concatenate(pieces, axis=1), np.stack([turn, second]).astype(np.float32)


def y_tables(rows, groups, kyr):
    grid_rows = rows * groups
    nowhere = -grid_rows
    offset = np.concatenate([np.arange(rows), [-1, rows, nowhere, nowhere]])
    cells = (np.arange(groups)[:, None] * rows + offset[None, :]).reshape(-1)
    ky = np.arange(kyr) - kyr // 2
    phase = (ky[:, None] * cells[None, :] % grid_rows) * (2.0 * np.pi / grid_rows)
    valid = (cells >= 0) & (cells < grid_rows)
    table = np.concatenate([np.cos(phase), np.sin(phase)], axis=0) * valid[None, :]
    return np.concatenate(split_table(table, 2), axis=0)


def mode_kernel(
    groups, capacity, kyr, levels, depth,
    owners, columns, table_hbm, factors_hbm,
    pick, green, table, factors, arrived,
):
    copies = [pltpu.make_async_copy(factors_hbm, factors, arrived.at[0])]
    share = table.shape[0] // (arrived.shape[0] - 1)
    for i in range(1, arrived.shape[0]):
        at = pl.ds((i - 1) * share, share)
        copies.append(pltpu.make_async_copy(table_hbm.at[at], table.at[at], arrived.at[i]))
    for copy in copies:
        copy.start()
    kxr = owners.shape[1]
    below, above, metric = [
        [columns[i * levels + k : i * levels + k + 1, :] for k in range(levels)] for i in range(3)
    ]
    places, gy = lax.axis_index("gz"), lax.axis_index("gy")
    shape = (2 * kxr, kxr)
    mode = lax.broadcasted_iota(jnp.int32, shape, 0) // 2
    other = lax.broadcasted_iota(jnp.int32, shape, 1)
    named = owners[...].astype(jnp.float32)
    owner = jnp.sum(jnp.where(mode == other, named, 0.0), axis=1, keepdims=True)
    rank = jnp.sum(
        jnp.where((named == owner) & (other < mode), 1.0, 0.0), axis=1, keepdims=True
    )
    slot = (owner * capacity + rank).astype(jnp.int32)
    part = lax.broadcasted_iota(jnp.int32, (2 * kxr, 1), 0) % 2
    column = lax.broadcasted_iota(jnp.int32, (2 * kxr, groups * capacity * 2), 1)
    pick[...] = jnp.where(slot * 2 + part == column, 1.0, 0.0).astype(jnp.bfloat16)

    lane = lax.broadcasted_iota(jnp.int32, (2 * kxr, 128), 1)
    here = gy * capacity + lane % (2 * capacity) // 2
    owned = (slot == here) & (part == 0)
    mode_id = (lax.broadcasted_iota(jnp.int32, (2 * kxr, 128), 0) // 2).astype(jnp.float32)
    kx = jnp.sum(jnp.where(owned, mode_id, 0.0), axis=0, keepdims=True)
    filled = jnp.sum(jnp.where(owned, 1.0, 0.0), axis=0, keepdims=True)

    size = 64
    at = lax.broadcasted_iota(jnp.int32, (size, 128), 1) // (2 * capacity)

    def turn(step, carry):
        start = pl.multiple_of(step * size, size)
        ky = lax.broadcasted_iota(jnp.int32, (size, 128), 0) + (start - kyr // 2)
        ky = ky.astype(jnp.float32)
        radius = kx * kx + ky * ky
        inside = jnp.where(radius <= float(kxr * kxr), filled, 0.0)
        shift = BASE_SHIFT + MODE_SHIFT * (radius / float(kxr * kxr))
        inverse = []
        for k in range(levels):
            pivot = -(below[k] + above[k] + metric[k] * shift)
            if k > 0:
                pivot = pivot - below[k] * above[k - 1] * inverse[-1]
            inverse.append(1.0 / pivot)
        for k in range(depth):
            target = places * depth + k
            forward = []
            for pos in range(levels):
                unit = jnp.where(target == pos, 1.0, 0.0)
                value = inside * unit
                if pos > 0:
                    value = value - above[pos - 1] * inverse[pos - 1] * forward[-1]
                forward.append(value)
            weights = [None] * levels
            for pos in range(levels - 1, -1, -1):
                value = forward[pos]
                if pos < levels - 1:
                    value = value - below[pos + 1] * weights[pos + 1]
                weights[pos] = value * inverse[pos]
            for block in range(levels // depth):
                total = jnp.zeros((size, 128), jnp.float32)
                for j in range(depth + 2):
                    pos = block * depth - 1 + j
                    if 0 <= pos < levels:
                        total = jnp.where(at == j, weights[pos], total)
                green[k, block, pl.ds(start, size), :] = total
        return carry

    lax.fori_loop(0, kyr // size, turn, 0)
    for copy in copies:
        copy.wait()


def pack_kernel(
    vx, vy, vz, owners_hbm, below_hbm, above_hbm, metric_hbm,
    own_one, own_two, row_one, row_two, owners, columns, scalars, arrived, small,
):
    rows = vx.shape[1]
    odd, odd_row = lax.axis_index("gz") % 2, lax.axis_index("gy") % 2
    copies = []
    for i, field in enumerate((vx, vy, vz)):
        for k, plane in enumerate((own_one, own_two)):
            level = odd if k else 1 - odd
            copies.append(pltpu.make_async_copy(field.at[level], plane.at[i], arrived.at[i, k]))
    others = [pltpu.make_async_copy(owners_hbm, owners, small.at[3])]
    for i, array in enumerate((below_hbm, above_hbm, metric_hbm)):
        others.append(pltpu.make_async_copy(array, scalars.at[i], small.at[i]))
    for copy in copies + others:
        copy.start()
    sub = lax.broadcasted_iota(jnp.int32, (8, vx.shape[2]), 0)
    bottom = jnp.zeros((8, vx.shape[2]), jnp.float32)
    top = bottom
    for copy in others:
        copy.wait()
    levels = scalars.shape[1]
    for i in range(3):
        for k in range(levels):
            at = i * levels + k
            columns[at : at + 1, :] = jnp.full((1, 128), scalars[i, k], jnp.float32)
    for i in range(3):
        for k, plane in enumerate((own_one, own_two)):
            copies[2 * i + k].wait()
            field = plane[i].astype(jnp.float32)
            bottom = jnp.where(sub == 2 * i + k, field[0:1], bottom)
            top = jnp.where(sub == 2 * i + k, field[rows - 1 : rows], top)
    row_one[...] = jnp.where(odd_row == 0, top, bottom).astype(jnp.bfloat16)
    row_two[...] = jnp.where(odd_row == 0, bottom, top).astype(jnp.bfloat16)


def up(field):
    return pltpu.roll(field, PAD_ROWS - 1, 0)


def down(field):
    return pltpu.roll(field, 1, 0)


def padded(field):
    empty = jnp.zeros((PAD_ROWS - field.shape[0], field.shape[1]), field.dtype)
    return jnp.concatenate([field, empty], axis=0)


def magnitude(squared):
    return SMAG_COEF * (squared * lax.rsqrt(squared))


def put_lines(lines, cells, fields):
    count = lines.shape[0] // 2
    start = 0
    for field in fields:
        high, low = split(field)
        size = field.shape[0]
        lines[start : start + size, cells] = high
        lines[count + start : count + start + size, cells] = low
        start += size


def transformed(lines, table):
    count, modes = lines.shape[0] // 2, table.shape[1] // 2
    product = matmul(lines[...], table[...])
    product = product[:count] + product[count:]
    return product[:, :modes] + product[:, modes:]


def slope_of(factors, field):
    modes = field.shape[1]
    even = lax.broadcasted_iota(jnp.int32, (1, modes), 1) % 2 == 0
    moved = jnp.where(even, pltpu.roll(field, modes - 1, 1), pltpu.roll(field, 1, 1))
    return factors[0:1] * moved


def early_kernel(
    groups, planes,
    own_one, own_two, row_one, row_two, table, factors,
    strain, spectra, lines,
):
    rows, width = own_one.shape[1:]
    gz, gy = lax.axis_index("gz"), lax.axis_index("gy")
    first = jnp.where(gz == 0, 1.0, 0.0)
    last = jnp.where(gz == planes - 1, 1.0, 0.0)
    odd, odd_row = gz % 2, gy % 2
    sub = lax.broadcasted_iota(jnp.int32, (8, CHUNK), 0)
    at_top, at_bottom = sub == 0, sub == 7
    rim_one = at_top & (odd_row == 0) | at_bottom & (odd_row == 1)
    rim_two = at_top & (odd_row == 1) | at_bottom & (odd_row == 0)
    ghost_rows = jnp.where(at_top & (gy == groups - 1) | at_bottom & (gy == 0), 1.0, 0.0)

    for step in range(width // CHUNK):
        here = step * CHUNK
        before, after = (here - 128) % width, (here + CHUNK) % width
        cells = pl.ds(here, CHUNK)
        rows_one = row_one[:, cells].astype(jnp.float32)
        rows_two = row_two[:, cells].astype(jnp.float32)
        flat, rims = [], []
        for k, source in enumerate((own_one, own_two)):
            sign = jnp.where(odd == k, 1.0, -1.0)
            own = [source[i, :, cells].astype(jnp.float32) for i in range(3)]
            x, y, rim = [], [], []
            for i in range(3):
                window = jnp.concatenate(
                    [
                        source[i, :, pl.ds(before, 128)].astype(jnp.float32),
                        own[i],
                        source[i, :, pl.ds(after, 128)].astype(jnp.float32),
                    ],
                    axis=1,
                )
                difference = pltpu.roll(window, CHUNK + 255, 1) - pltpu.roll(window, 1, 1)
                x.append(difference[:, 128 : 128 + CHUNK])
                at = 2 * i + k
                edge = jnp.where(
                    rim_one, rows_one[at : at + 1], jnp.where(rim_two, rows_two[at : at + 1], 0.0)
                )
                field = jnp.concatenate([own[i], edge], axis=0)
                difference = up(field) - down(field)
                y.append(difference[:rows])
                rim.append(difference[rows:])
            e01 = y[0] + x[1]
            strain[k, 0, :, cells] = x[0]
            strain[k, 1, :, cells] = y[1]
            strain[k, 2, :, cells] = e01
            strain[k, 3, :, cells] = sign * x[2]
            strain[k, 4, :, cells] = sign * y[2]
            strain[k, 5, :, cells] = (
                0.5 * (x[0] * x[0] + y[1] * y[1]) + 0.25 * (e01 * e01) + STRAIN_FLOOR
            )
            squared = 0.5 * (rim[1] * rim[1]) + 0.25 * (rim[0] * rim[0] + rim[2] * rim[2])
            viscous = ghost_rows * magnitude(squared + STRAIN_FLOOR)
            rims += [viscous * rim[0], viscous * rim[1], viscous * (sign * rim[2])]
            flat.append(x[0] + y[1])

        ghost = [(first - last) * own_two[i, :, cells].astype(jnp.float32) for i in range(3)]
        squared = 0.5 * (ghost[2] * ghost[2])
        squared = squared + 0.25 * (ghost[0] * ghost[0] + ghost[1] * ghost[1])
        viscous = magnitude(squared + STRAIN_FLOOR)
        put_lines(lines, cells, flat + [viscous * ghost[i] for i in range(3)] + rims)

    total = transformed(lines, table)
    pieces = [padded(total[rows * i : rows * (i + 1)]) for i in range(5)]
    t02, t12, s22 = pieces[2:]
    cross = 0.25 * (up(t12) - down(t12)) + slope_of(factors, t02)
    pieces = pieces[:2] + [s22 + (last - first) * cross]
    for i, piece in enumerate(pieces + [total[5 * rows :]]):
        spectra[PAD_ROWS * i : PAD_ROWS * i + piece.shape[0], :] = piece


def late_kernel(
    planes, groups, capacity,
    own_one, own_two, plane_one, plane_two, strain, spectra, table, factors, pick,
    out, lines, codes,
):
    rows, width = own_one.shape[1:]
    gz = lax.axis_index("gz")
    first = jnp.where(gz == 0, 1.0, 0.0)
    last = jnp.where(gz == planes - 1, 1.0, 0.0)
    odd = gz % 2

    for step in range(width // CHUNK):
        cells = pl.ds(step * CHUNK, CHUNK)
        fields = []
        for k, plane, other in ((0, plane_one, own_two), (1, plane_two, own_one)):
            z = [
                plane[i, :, cells].astype(jnp.float32) - other[i, :, cells].astype(jnp.float32)
                for i in range(3)
            ]
            e02 = z[0] + strain[k, 3, :, cells]
            e12 = z[1] + strain[k, 4, :, cells]
            squared = strain[k, 5, :, cells] + 0.5 * (z[2] * z[2])
            squared = squared + 0.25 * (e02 * e02 + e12 * e12)
            viscous = magnitude(squared)
            fields += [viscous * strain[k, i, :, cells] for i in (2, 1)]
            fields += [viscous * e12, viscous * z[2], viscous * e02]
            fields += [viscous * strain[k, 0, :, cells], z[2]]
        put_lines(lines, cells, fields)

    total = transformed(lines, table)
    parts = []
    for k in range(2):
        sign = jnp.where(odd == k, 1.0, -1.0)
        pieces = [total[rows * i : rows * (i + 1)] for i in range(7 * k, 7 * k + 7)]
        for i in range(3):
            start = 3 * PAD_ROWS + 8 * (3 * k + i)
            pieces[i] = jnp.concatenate([pieces[i], spectra[start : start + 8, :]], axis=0)
        t01, p11, t12 = pieces[:3]
        s22, t02, s00, rise = [padded(piece) for piece in pieces[3:]]
        p11 = up(p11) + down(p11) - 2.0 * p11
        t01 = up(t01) - down(t01)
        t12 = 0.25 * (up(t12) - down(t12))
        flat = spectra[k * PAD_ROWS : (k + 1) * PAD_ROWS, :]
        s22, rise = sign * s22, sign * rise
        middle = p11 - 2.0 * s22 + 0.5 * (flat + rise)
        middle = middle + slope_of(factors, t01) + factors[1:2] * s00
        cross = sign * (t12 + slope_of(factors, t02))
        parts.append([s22 + cross, middle, s22 - cross])

    ghost = spectra[2 * PAD_ROWS : 3 * PAD_ROWS, :]
    lower = [jnp.where(odd == 1, p, q) for p, q in zip(*parts)]
    upper = [jnp.where(odd == 1, q, p) for p, q in zip(*parts)]
    spectrum = [
        lower[0],
        lower[1] + upper[0] + first * ghost,
        lower[2] + upper[1] + last * ghost,
        upper[2],
    ]
    count = len(spectrum)

    stacked = jnp.concatenate(spectrum, axis=0)
    selected = matmul(jnp.concatenate(split(stacked), axis=0), pick[...])
    size = count * PAD_ROWS
    selected = selected[:size] + selected[size:]

    lane = lax.broadcasted_iota(jnp.int32, (PAD_ROWS, 128), 1)
    empty_block = jnp.zeros((PAD_ROWS, 128), jnp.float32)
    sub_lanes = lax.broadcasted_iota(jnp.int32, (8, 128), 0)
    share = 2 * capacity
    for half in range(groups * share // 128):
        pieces = [
            selected[PAD_ROWS * j : PAD_ROWS * (j + 1), 128 * half : 128 * (half + 1)]
            for j in range(count)
        ]
        for place in range(128 // share):
            block = empty_block
            for j in range(count):
                distance = (share * (j - place)) % 128
                moved = pltpu.roll(pieces[j], distance, 1) if distance else pieces[j]
                block = jnp.where(lane // share == j, moved, block)
            largest = jnp.max(jnp.abs(block), axis=0, keepdims=True)
            power = jnp.floor(jnp.log2(jnp.maximum(largest, 1e-35)) * STEPS) + 1.0
            block = jnp.floor(block * (CODES * jnp.exp2(power * (-1.0 / STEPS))) + 0.5)
            rim = pltpu.roll(block[rows:], 1, 0)
            rim = jnp.where(sub_lanes < 2, rim, jnp.where(sub_lanes == 2, power, 0.0))
            base = (half * (128 // share) + place) * (rows + 4)
            codes[base : base + rows, :] = block[:rows]
            codes[base + rows : base + rows + 4, :] = rim[:4]
    packed = codes[...].astype(jnp.int32).astype(jnp.int16)
    for side in range(planes):
        out[side * packed.shape[0] : (side + 1) * packed.shape[0], :] = packed


def solve_kernel(kyr, depth, capacity, reach, received, basis, green, out, codes):
    planes = green.shape[1]
    sources = received.shape[0] // reach
    codes[...] = received[...].astype(jnp.int32).astype(jnp.float32)
    power = codes[pl.ds(reach - 2, sources, stride=reach), :]
    scale = jnp.exp2(power * (1.0 / STEPS)) * (1.0 / CODES)
    row = lax.broadcasted_iota(jnp.int32, (2 * reach, 128), 0)
    values = []
    for pair in range(0, sources, 2):
        factor = jnp.where(row < reach, scale[pair : pair + 1], scale[pair + 1 : pair + 2])
        values.append(codes[pair * reach : (pair + 2) * reach, :] * factor)
    each = sources // planes // 2
    blocks = [jnp.concatenate(values[i * each : (i + 1) * each], axis=0) for i in range(planes)]
    high, low = split(jnp.concatenate(blocks, axis=1))
    product = matmul(basis[...], high)
    product = product[: 2 * kyr] + product[2 * kyr :] + matmul(basis[: 2 * kyr, :], low)
    cosine = [jnp.zeros((kyr, 128), jnp.float32) for _ in range(depth)]
    sine = [jnp.zeros((kyr, 128), jnp.float32) for _ in range(depth)]
    for block in range(planes):
        lanes = slice(block * 128, (block + 1) * 128)
        for k in range(depth):
            cosine[k] = cosine[k] + green[k, block] * product[:kyr, lanes]
            sine[k] = sine[k] + green[k, block] * product[kyr:, lanes]
    lane = lax.broadcasted_iota(jnp.int32, (kyr, 128), 1)
    share = 2 * capacity

    def gathered(field):
        distance = 64
        while distance >= share:
            field = field + pltpu.roll(field, distance, 1)
            distance //= 2
        return field

    result = jnp.zeros((kyr, 128), jnp.float32)
    for k in range(depth):
        real = gathered(cosine[k])
        turned = gathered(sine[k])
        turned = jnp.where(lane % 2 == 0, pltpu.roll(turned, 127, 1), -pltpu.roll(turned, 1, 1))
        result = jnp.where(lane // share == k, real + turned, result)
    flipped = result.T
    for k in range(depth):
        out[:, k, :] = flipped[k * share : (k + 1) * share]


def exchange(array, axis, size, shifted):
    pairs = [(i, i + 1) for i in range(shifted, size - 1, 2)]
    return lax.ppermute(array, axis, pairs + [(j, i) for i, j in pairs])


def in_hbm(array):
    return pltpu.with_memory_space_constraint(array, pltpu.HBM)


def per_device(groups, planes, velocity_x, velocity_y, velocity_z, owners, below, above, metric):
    depth, rows, width = velocity_x.shape
    kxr = owners.shape[0]
    kyr = 2 * kxr
    levels = below.shape[0]
    limit = pltpu.CompilerParams(vmem_limit_bytes=32 * 1024 * 1024)
    fields = (velocity_x, velocity_y, velocity_z)

    plane_shape = jax.ShapeDtypeStruct((3, rows, width), jnp.bfloat16)
    row_shape = jax.ShapeDtypeStruct((8, width), jnp.bfloat16)
    own_one, own_two, row_one, row_two, owners, columns = pl.pallas_call(
        pack_kernel,
        out_shape=(plane_shape, plane_shape, row_shape, row_shape)
        + (
            jax.ShapeDtypeStruct((1, kxr), jnp.int32),
            jax.ShapeDtypeStruct((3 * levels, 128), jnp.float32),
        ),
        in_specs=[HBM] * 7,
        out_specs=(VMEM,) * 6,
        scratch_shapes=[
            pltpu.SMEM((3, levels), jnp.float32),
            pltpu.SemaphoreType.DMA((3, 2)),
            pltpu.SemaphoreType.DMA((4,)),
        ],
        compiler_params=limit,
    )(*[in_hbm(array) for array in (*fields, owners.reshape(1, kxr), below, above, metric)])
    plane_one = exchange(own_one, "gz", planes, 0)
    plane_two = exchange(own_two, "gz", planes, 1)
    row_one = exchange(row_one, "gy", groups, 0)
    row_two = exchange(row_two, "gy", groups, 1)

    table, factors = [jnp.asarray(array) for array in x_tables(width, kxr, rows * groups)]
    pick, green, table, factors = pl.pallas_call(
        functools.partial(mode_kernel, groups, CAP, kyr, levels, depth),
        out_shape=(
            jax.ShapeDtypeStruct((2 * kxr, groups * CAP * 2), jnp.bfloat16),
            jax.ShapeDtypeStruct((depth, planes, kyr, 128), jnp.float32),
            jax.ShapeDtypeStruct(table.shape, table.dtype),
            jax.ShapeDtypeStruct(factors.shape, factors.dtype),
        ),
        in_specs=[VMEM, VMEM, HBM, HBM],
        out_specs=(VMEM,) * 4,
        scratch_shapes=[pltpu.SemaphoreType.DMA((5,))],
        compiler_params=limit,
        cost_estimate=COST,
    )(owners, columns, in_hbm(table), in_hbm(factors))

    strain, spectra = pl.pallas_call(
        functools.partial(early_kernel, groups, planes),
        out_shape=(
            jax.ShapeDtypeStruct((depth, 6, rows, width), jnp.float32),
            jax.ShapeDtypeStruct((3 * PAD_ROWS + 6 * 8, 2 * kxr), jnp.float32),
        ),
        in_specs=[VMEM] * 6,
        out_specs=(VMEM,) * 2,
        scratch_shapes=[pltpu.VMEM((2 * (5 * rows + 6 * 8), width), jnp.bfloat16)],
        compiler_params=limit,
        cost_estimate=COST,
    )(own_one, own_two, row_one, row_two, table, factors)

    reach = rows + 4
    count = depth * 7 * rows
    outgoing = pl.pallas_call(
        functools.partial(late_kernel, planes, groups, CAP),
        out_shape=jax.ShapeDtypeStruct((planes * groups * reach, 128), jnp.int16),
        in_specs=[VMEM] * 9,
        out_specs=VMEM,
        scratch_shapes=[
            pltpu.VMEM((2 * count, width), jnp.bfloat16),
            pltpu.VMEM((groups * reach, 128), jnp.float32),
        ],
        compiler_params=limit,
    )(own_one, own_two, plane_one, plane_two, strain, spectra, table, factors, pick)
    outgoing = outgoing.reshape(planes * groups, reach // 2, 2, 128)
    received = lax.all_to_all(outgoing, ("gz", "gy"), split_axis=0, concat_axis=0, tiled=True)
    received = received.reshape(planes * groups * reach, 128)

    basis = jnp.asarray(y_tables(rows, groups, kyr))
    solved = pl.pallas_call(
        functools.partial(solve_kernel, kyr, depth, CAP, reach),
        out_shape=jax.ShapeDtypeStruct((CAP * 2, depth, kyr), jnp.float32),
        in_specs=[VMEM] * 3,
        out_specs=VMEM,
        scratch_shapes=[pltpu.VMEM(received.shape, jnp.float32)],
        compiler_params=limit,
    )(received, basis, green)
    return solved.reshape(1, CAP, 2, depth, kyr)


def solution(mesh):
    placed = (P("gz", "gy", None), P("gz", "gy", None), P("gz", "gy", None), P(), P(), P(), P())
    return jax.shard_map(
        functools.partial(per_device, mesh.shape["gy"], mesh.shape["gz"]),
        mesh=mesh,
        in_specs=placed,
        out_specs=P("gy", None, None, "gz", None),
        check_vma=False,
    )
```

```python
import functools
import math

import jax
import jax.numpy as jnp
import numpy as np
from jax import lax
from jax.experimental import pallas as pl
from jax.experimental.pallas import tpu as pltpu
from jax.sharding import PartitionSpec as P

CAP = 16
SMAG_COEF = 0.12
STRAIN_FLOOR = 0.01
BASE_SHIFT = 0.004
MODE_SHIFT = 0.02

CHUNK = 256
PAD_ROWS = 24
CODES = 32000.0
STEPS = 32.0
VMEM = pl.BlockSpec(memory_space=pltpu.VMEM)
HBM = pl.BlockSpec(memory_space=pltpu.HBM)
SMEM = pl.BlockSpec(memory_space=pltpu.SMEM)


def split(value):
    high = value.astype(jnp.bfloat16)
    low = (value - high.astype(jnp.float32)).astype(jnp.bfloat16)
    return high, low


def split_table(table, parts):
    pieces = []
    for _ in range(parts):
        pieces.append(table.astype(jnp.bfloat16))
        table = table - pieces[-1].astype(np.float64)
    return pieces


def matmul(left, right):
    return jnp.dot(left, right, preferred_element_type=jnp.float32)


def x_tables(width, kxr, grid_rows):
    norm = 1.0 / math.sqrt(width * grid_rows)
    phase = (np.arange(width)[:, None] * np.arange(kxr)[None, :] % width) * (2.0 * np.pi / width)
    table = np.stack([np.cos(phase) * norm, -np.sin(phase) * norm], axis=2)
    pieces = split_table(table.reshape(width, 2 * kxr), 2)
    angle = np.arange(kxr) * (2.0 * np.pi / width)
    turn = np.stack([-np.sin(angle), np.sin(angle)], axis=1).reshape(2 * kxr) * 0.5
    second = np.repeat(-4.0 * np.sin(angle * 0.5) ** 2, 2)
    return np.concatenate(pieces, axis=1), np.stack([turn, second]).astype(np.float32)


def y_tables(rows, groups, kyr):
    grid_rows = rows * groups
    nowhere = -grid_rows
    offset = np.concatenate([np.arange(rows), [-1, rows, nowhere, nowhere]])
    cells = (np.arange(groups)[:, None] * rows + offset[None, :]).reshape(-1)
    ky = np.arange(kyr) - kyr // 2
    phase = (ky[:, None] * cells[None, :] % grid_rows) * (2.0 * np.pi / grid_rows)
    valid = (cells >= 0) & (cells < grid_rows)
    table = np.concatenate([np.cos(phase), np.sin(phase)], axis=0) * valid[None, :]
    return np.concatenate(split_table(table, 2), axis=0)


def mode_kernel(
    groups, capacity, kyr, levels, depth,
    owners, columns, table_hbm, factors_hbm,
    pick, green, table, factors, arrived,
):
    copies = [pltpu.make_async_copy(factors_hbm, factors, arrived.at[0])]
    share = table.shape[0] // (arrived.shape[0] - 1)
    for i in range(1, arrived.shape[0]):
        at = pl.ds((i - 1) * share, share)
        copies.append(pltpu.make_async_copy(table_hbm.at[at], table.at[at], arrived.at[i]))
    for copy in copies:
        copy.start()
    kxr = owners.shape[1]
    below, above, metric = [
        [columns[i * levels + k : i * levels + k + 1, :] for k in range(levels)] for i in range(3)
    ]
    places, gy = lax.axis_index("gz"), lax.axis_index("gy")
    shape = (2 * kxr, kxr)
    mode = lax.broadcasted_iota(jnp.int32, shape, 0) // 2
    other = lax.broadcasted_iota(jnp.int32, shape, 1)
    named = owners[...].astype(jnp.float32)
    owner = jnp.sum(jnp.where(mode == other, named, 0.0), axis=1, keepdims=True)
    rank = jnp.sum(
        jnp.where((named == owner) & (other < mode), 1.0, 0.0), axis=1, keepdims=True
    )
    slot = (owner * capacity + rank).astype(jnp.int32)
    part = lax.broadcasted_iota(jnp.int32, (2 * kxr, 1), 0) % 2
    column = lax.broadcasted_iota(jnp.int32, (2 * kxr, groups * capacity * 2), 1)
    pick[...] = jnp.where(slot * 2 + part == column, 1.0, 0.0).astype(jnp.bfloat16)

    lane = lax.broadcasted_iota(jnp.int32, (2 * kxr, 128), 1)
    here = gy * capacity + lane % (2 * capacity) // 2
    owned = (slot == here) & (part == 0)
    mode_id = (lax.broadcasted_iota(jnp.int32, (2 * kxr, 128), 0) // 2).astype(jnp.float32)
    kx = jnp.sum(jnp.where(owned, mode_id, 0.0), axis=0, keepdims=True)
    filled = jnp.sum(jnp.where(owned, 1.0, 0.0), axis=0, keepdims=True)

    size = 64
    at = lax.broadcasted_iota(jnp.int32, (size, 128), 1) // (2 * capacity)

    def turn(step, carry):
        start = pl.multiple_of(step * size, size)
        ky = lax.broadcasted_iota(jnp.int32, (size, 128), 0) + (start - kyr // 2)
        ky = ky.astype(jnp.float32)
        radius = kx * kx + ky * ky
        inside = jnp.where(radius <= float(kxr * kxr), filled, 0.0)
        shift = BASE_SHIFT + MODE_SHIFT * (radius / float(kxr * kxr))
        inverse = []
        for k in range(levels):
            pivot = -(below[k] + above[k] + metric[k] * shift)
            if k > 0:
                pivot = pivot - below[k] * above[k - 1] * inverse[-1]
            inverse.append(1.0 / pivot)
        for k in range(depth):
            target = places * depth + k
            forward = []
            for pos in range(levels):
                unit = jnp.where(target == pos, 1.0, 0.0)
                value = inside * unit
                if pos > 0:
                    value = value - above[pos - 1] * inverse[pos - 1] * forward[-1]
                forward.append(value)
            weights = [None] * levels
            for pos in range(levels - 1, -1, -1):
                value = forward[pos]
                if pos < levels - 1:
                    value = value - below[pos + 1] * weights[pos + 1]
                weights[pos] = value * inverse[pos]
            for block in range(levels // depth):
                total = jnp.zeros((size, 128), jnp.float32)
                for j in range(depth + 2):
                    pos = block * depth - 1 + j
                    if 0 <= pos < levels:
                        total = jnp.where(at == j, weights[pos], total)
                green[k, block, pl.ds(start, size), :] = total
        return carry

    lax.fori_loop(0, kyr // size, turn, 0)
    for copy in copies:
        copy.wait()


def pack_kernel(
    vx, vy, vz, owners_hbm, below_hbm, above_hbm, metric_hbm,
    own_one, own_two, row_one, row_two, owners, columns, scalars, arrived, small,
):
    rows = vx.shape[1]
    odd, odd_row = lax.axis_index("gz") % 2, lax.axis_index("gy") % 2
    copies = []
    for i, field in enumerate((vx, vy, vz)):
        for k, plane in enumerate((own_one, own_two)):
            level = odd if k else 1 - odd
            copies.append(pltpu.make_async_copy(field.at[level], plane.at[i], arrived.at[i, k]))
    others = [pltpu.make_async_copy(owners_hbm, owners, small.at[3])]
    for i, array in enumerate((below_hbm, above_hbm, metric_hbm)):
        others.append(pltpu.make_async_copy(array, scalars.at[i], small.at[i]))
    for copy in copies + others:
        copy.start()
    sub = lax.broadcasted_iota(jnp.int32, (8, vx.shape[2]), 0)
    bottom = jnp.zeros((8, vx.shape[2]), jnp.float32)
    top = bottom
    for copy in others:
        copy.wait()
    levels = scalars.shape[1]
    for i in range(3):
        for k in range(levels):
            at = i * levels + k
            columns[at : at + 1, :] = jnp.full((1, 128), scalars[i, k], jnp.float32)
    for i in range(3):
        for k, plane in enumerate((own_one, own_two)):
            copies[2 * i + k].wait()
            field = plane[i].astype(jnp.float32)
            bottom = jnp.where(sub == 2 * i + k, field[0:1], bottom)
            top = jnp.where(sub == 2 * i + k, field[rows - 1 : rows], top)
    row_one[...] = jnp.where(odd_row == 0, top, bottom).astype(jnp.bfloat16)
    row_two[...] = jnp.where(odd_row == 0, bottom, top).astype(jnp.bfloat16)


def up(field):
    return pltpu.roll(field, PAD_ROWS - 1, 0)


def down(field):
    return pltpu.roll(field, 1, 0)


def padded(field):
    empty = jnp.zeros((PAD_ROWS - field.shape[0], field.shape[1]), field.dtype)
    return jnp.concatenate([field, empty], axis=0)


def magnitude(squared):
    return SMAG_COEF * (squared * lax.rsqrt(squared))


def put_lines(lines, cells, fields):
    count = lines.shape[0] // 2
    start = 0
    for field in fields:
        high, low = split(field)
        size = field.shape[0]
        lines[start : start + size, cells] = high
        lines[count + start : count + start + size, cells] = low
        start += size


def transformed(lines, table):
    count, modes = lines.shape[0] // 2, table.shape[1] // 2
    product = matmul(lines[...], table[...])
    product = product[:count] + product[count:]
    return product[:, :modes] + product[:, modes:]


def slope_of(factors, field):
    modes = field.shape[1]
    even = lax.broadcasted_iota(jnp.int32, (1, modes), 1) % 2 == 0
    moved = jnp.where(even, pltpu.roll(field, modes - 1, 1), pltpu.roll(field, 1, 1))
    return factors[0:1] * moved


def early_kernel(
    groups, planes,
    own_one, own_two, table, factors,
    strain, spectra, lines,
):
    rows, width = own_one.shape[1:]
    gz, gy = lax.axis_index("gz"), lax.axis_index("gy")
    first = jnp.where(gz == 0, 1.0, 0.0)
    last = jnp.where(gz == planes - 1, 1.0, 0.0)
    odd = gz % 2
    sub = lax.broadcasted_iota(jnp.int32, (8, CHUNK), 0)
    ghost_rows = jnp.where((sub == 0) & (gy == groups - 1) | (sub == 7) & (gy == 0), 1.0, 0.0)

    for step in range(width // CHUNK):
        here = step * CHUNK
        before, after = (here - 128) % width, (here + CHUNK) % width
        cells = pl.ds(here, CHUNK)
        flat, rims = [], []
        for k, source in enumerate((own_one, own_two)):
            sign = jnp.where(odd == k, 1.0, -1.0)
            own = [source[i, :, cells].astype(jnp.float32) for i in range(3)]
            x, y, rim = [], [], []
            for i in range(3):
                window = jnp.concatenate(
                    [
                        source[i, :, pl.ds(before, 128)].astype(jnp.float32),
                        own[i],
                        source[i, :, pl.ds(after, 128)].astype(jnp.float32),
                    ],
                    axis=1,
                )
                difference = pltpu.roll(window, CHUNK + 255, 1) - pltpu.roll(window, 1, 1)
                x.append(difference[:, 128 : 128 + CHUNK])
                field = padded(own[i])
                difference = up(field) - down(field)
                y.append(difference[:rows])
                rim.append(difference[rows:])
            e01 = y[0] + x[1]
            strain[k, 0, :, cells] = x[0]
            strain[k, 1, :, cells] = y[1]
            strain[k, 2, :, cells] = e01
            strain[k, 3, :, cells] = sign * x[2]
            strain[k, 4, :, cells] = sign * y[2]
            squared = 0.5 * (rim[1] * rim[1]) + 0.25 * (rim[0] * rim[0] + rim[2] * rim[2])
            viscous = ghost_rows * magnitude(squared + STRAIN_FLOOR)
            rims += [viscous * rim[0], viscous * rim[1], viscous * (sign * rim[2])]
            flat.append(x[0] + y[1])

        ghost = [(first - last) * own_two[i, :, cells].astype(jnp.float32) for i in range(3)]
        squared = 0.5 * (ghost[2] * ghost[2])
        squared = squared + 0.25 * (ghost[0] * ghost[0] + ghost[1] * ghost[1])
        viscous = magnitude(squared + STRAIN_FLOOR)
        put_lines(lines, cells, flat + [viscous * ghost[i] for i in range(3)] + rims)

    total = transformed(lines, table)
    pieces = [padded(total[rows * i : rows * (i + 1)]) for i in range(5)]
    t02, t12, s22 = pieces[2:]
    cross = 0.25 * (up(t12) - down(t12)) + slope_of(factors, t02)
    pieces = pieces[:2] + [s22 + (last - first) * cross]
    for i, piece in enumerate(pieces + [total[5 * rows :]]):
        spectra[PAD_ROWS * i : PAD_ROWS * i + piece.shape[0], :] = piece


def stress_lines(k, other, plane, row_one, row_two, strain, table, lines):
    rows, width = other.shape[1:]
    odd_row = lax.axis_index("gy") % 2
    sign = jnp.where(lax.axis_index("gz") % 2 == k, 1.0, -1.0)
    row = lax.broadcasted_iota(jnp.int32, (rows, CHUNK), 0)
    for step in range(width // CHUNK):
        cells = pl.ds(step * CHUNK, CHUNK)
        ones = row_one[:, cells].astype(jnp.float32)
        twos = row_two[:, cells].astype(jnp.float32)
        lows = jnp.where(odd_row == 0, twos, ones)
        highs = jnp.where(odd_row == 0, ones, twos)
        z, beyond = [], []
        for i in range(3):
            at = 2 * i + k
            z.append(plane[i, :, cells].astype(jnp.float32) - other[i, :, cells].astype(jnp.float32))
            beyond.append(
                jnp.where(
                    row == rows - 1,
                    highs[at : at + 1],
                    jnp.where(row == 0, -lows[at : at + 1], 0.0),
                )
            )
        x0 = strain[k, 0, :, cells]
        y1 = strain[k, 1, :, cells] + beyond[1]
        e01 = strain[k, 2, :, cells] + beyond[0]
        e02 = z[0] + strain[k, 3, :, cells]
        e12 = z[1] + strain[k, 4, :, cells] + sign * beyond[2]
        squared = 0.5 * (x0 * x0 + y1 * y1 + z[2] * z[2]) + STRAIN_FLOOR
        squared = squared + 0.25 * (e01 * e01 + e02 * e02 + e12 * e12)
        viscous = magnitude(squared)
        fields = [viscous * field for field in (e01, y1, e12, z[2], e02, x0)]
        put_lines(lines, cells, fields + [z[2] + sign * beyond[1]])
    return transformed(lines, table)


def late_kernel(other, plane, row_one, row_two, strain, table, out, lines):
    out[...] = stress_lines(0, other, plane, row_one, row_two, strain, table, lines)


def last_kernel(
    planes, groups, capacity,
    other, plane, row_one, row_two, strain, table, earlier, spectra, factors, pick,
    out, lines, codes,
):
    rows = other.shape[1]
    gz = lax.axis_index("gz")
    first = jnp.where(gz == 0, 1.0, 0.0)
    last = jnp.where(gz == planes - 1, 1.0, 0.0)
    odd = gz % 2
    totals = (earlier, stress_lines(1, other, plane, row_one, row_two, strain, table, lines))
    parts = []
    for k in range(2):
        sign = jnp.where(odd == k, 1.0, -1.0)
        pieces = [totals[k][rows * i : rows * (i + 1)] for i in range(7)]
        for i in range(3):
            start = 3 * PAD_ROWS + 8 * (3 * k + i)
            pieces[i] = jnp.concatenate([pieces[i], spectra[start : start + 8, :]], axis=0)
        t01, p11, t12 = pieces[:3]
        s22, t02, s00, rise = [padded(piece) for piece in pieces[3:]]
        p11 = up(p11) + down(p11) - 2.0 * p11
        t01 = up(t01) - down(t01)
        t12 = 0.25 * (up(t12) - down(t12))
        flat = spectra[k * PAD_ROWS : (k + 1) * PAD_ROWS, :]
        s22, rise = sign * s22, sign * rise
        middle = p11 - 2.0 * s22 + 0.5 * (flat + rise)
        middle = middle + slope_of(factors, t01) + factors[1:2] * s00
        cross = sign * (t12 + slope_of(factors, t02))
        parts.append([s22 + cross, middle, s22 - cross])

    ghost = spectra[2 * PAD_ROWS : 3 * PAD_ROWS, :]
    lower = [jnp.where(odd == 1, p, q) for p, q in zip(*parts)]
    upper = [jnp.where(odd == 1, q, p) for p, q in zip(*parts)]
    spectrum = [
        lower[0],
        lower[1] + upper[0] + first * ghost,
        lower[2] + upper[1] + last * ghost,
        upper[2],
    ]
    count = len(spectrum)

    stacked = jnp.concatenate(spectrum, axis=0)
    selected = matmul(jnp.concatenate(split(stacked), axis=0), pick[...])
    size = count * PAD_ROWS
    selected = selected[:size] + selected[size:]

    lane = lax.broadcasted_iota(jnp.int32, (PAD_ROWS, 128), 1)
    empty_block = jnp.zeros((PAD_ROWS, 128), jnp.float32)
    sub_lanes = lax.broadcasted_iota(jnp.int32, (8, 128), 0)
    share = 2 * capacity
    for half in range(groups * share // 128):
        pieces = [
            selected[PAD_ROWS * j : PAD_ROWS * (j + 1), 128 * half : 128 * (half + 1)]
            for j in range(count)
        ]
        for place in range(128 // share):
            block = empty_block
            for j in range(count):
                distance = (share * (j - place)) % 128
                moved = pltpu.roll(pieces[j], distance, 1) if distance else pieces[j]
                block = jnp.where(lane // share == j, moved, block)
            largest = jnp.max(jnp.abs(block), axis=0, keepdims=True)
            power = jnp.floor(jnp.log2(jnp.maximum(largest, 1e-35)) * STEPS) + 1.0
            block = jnp.floor(block * (CODES * jnp.exp2(power * (-1.0 / STEPS))) + 0.5)
            rim = pltpu.roll(block[rows:], 1, 0)
            rim = jnp.where(sub_lanes < 2, rim, jnp.where(sub_lanes == 2, power, 0.0))
            base = (half * (128 // share) + place) * (rows + 4)
            codes[base : base + rows, :] = block[:rows]
            codes[base + rows : base + rows + 4, :] = rim[:4]
    packed = codes[...].astype(jnp.int32).astype(jnp.int16)
    for side in range(planes):
        out[side * packed.shape[0] : (side + 1) * packed.shape[0], :] = packed


def solve_kernel(kyr, depth, capacity, reach, received, basis, green, out, codes):
    planes = green.shape[1]
    sources = received.shape[0] // reach
    codes[...] = received[...].astype(jnp.int32).astype(jnp.float32)
    power = codes[pl.ds(reach - 2, sources, stride=reach), :]
    scale = jnp.exp2(power * (1.0 / STEPS)) * (1.0 / CODES)
    row = lax.broadcasted_iota(jnp.int32, (2 * reach, 128), 0)
    values = []
    for pair in range(0, sources, 2):
        factor = jnp.where(row < reach, scale[pair : pair + 1], scale[pair + 1 : pair + 2])
        values.append(codes[pair * reach : (pair + 2) * reach, :] * factor)
    each = sources // planes // 2
    blocks = [jnp.concatenate(values[i * each : (i + 1) * each], axis=0) for i in range(planes)]
    high, low = split(jnp.concatenate(blocks, axis=1))
    product = matmul(basis[...], high)
    product = product[: 2 * kyr] + product[2 * kyr :] + matmul(basis[: 2 * kyr, :], low)
    cosine = [jnp.zeros((kyr, 128), jnp.float32) for _ in range(depth)]
    sine = [jnp.zeros((kyr, 128), jnp.float32) for _ in range(depth)]
    for block in range(planes):
        lanes = slice(block * 128, (block + 1) * 128)
        for k in range(depth):
            cosine[k] = cosine[k] + green[k, block] * product[:kyr, lanes]
            sine[k] = sine[k] + green[k, block] * product[kyr:, lanes]
    lane = lax.broadcasted_iota(jnp.int32, (kyr, 128), 1)
    share = 2 * capacity

    def gathered(field):
        distance = 64
        while distance >= share:
            field = field + pltpu.roll(field, distance, 1)
            distance //= 2
        return field

    result = jnp.zeros((kyr, 128), jnp.float32)
    for k in range(depth):
        real = gathered(cosine[k])
        turned = gathered(sine[k])
        turned = jnp.where(lane % 2 == 0, pltpu.roll(turned, 127, 1), -pltpu.roll(turned, 1, 1))
        result = jnp.where(lane // share == k, real + turned, result)
    flipped = result.T
    for k in range(depth):
        out[:, k, :] = flipped[k * share : (k + 1) * share]


def exchange(array, axis, size, shifted):
    pairs = [(i, i + 1) for i in range(shifted, size - 1, 2)]
    return lax.ppermute(array, axis, pairs + [(j, i) for i, j in pairs])


def in_hbm(array):
    return pltpu.with_memory_space_constraint(array, pltpu.HBM)


def per_device(groups, planes, velocity_x, velocity_y, velocity_z, owners, below, above, metric):
    depth, rows, width = velocity_x.shape
    kxr = owners.shape[0]
    kyr = 2 * kxr
    levels = below.shape[0]
    limit = pltpu.CompilerParams(vmem_limit_bytes=32 * 1024 * 1024)
    fields = (velocity_x, velocity_y, velocity_z)

    plane_shape = jax.ShapeDtypeStruct((3, rows, width), jnp.bfloat16)
    row_shape = jax.ShapeDtypeStruct((8, width), jnp.bfloat16)
    own_one, own_two, row_one, row_two, owners, columns = pl.pallas_call(
        pack_kernel,
        out_shape=(plane_shape, plane_shape, row_shape, row_shape)
        + (
            jax.ShapeDtypeStruct((1, kxr), jnp.int32),
            jax.ShapeDtypeStruct((3 * levels, 128), jnp.float32),
        ),
        in_specs=[HBM] * 7,
        out_specs=(VMEM,) * 6,
        scratch_shapes=[
            pltpu.SMEM((3, levels), jnp.float32),
            pltpu.SemaphoreType.DMA((3, 2)),
            pltpu.SemaphoreType.DMA((4,)),
        ],
        compiler_params=limit,
    )(*[in_hbm(array) for array in (*fields, owners.reshape(1, kxr), below, above, metric)])
    plane_one = exchange(own_one, "gz", planes, 0)
    plane_two = exchange(own_two, "gz", planes, 1)
    row_one = exchange(row_one, "gy", groups, 0)
    row_two = exchange(row_two, "gy", groups, 1)

    table, factors = [jnp.asarray(array) for array in x_tables(width, kxr, rows * groups)]
    pick, green, table, factors = pl.pallas_call(
        functools.partial(mode_kernel, groups, CAP, kyr, levels, depth),
        out_shape=(
            jax.ShapeDtypeStruct((2 * kxr, groups * CAP * 2), jnp.bfloat16),
            jax.ShapeDtypeStruct((depth, planes, kyr, 128), jnp.float32),
            jax.ShapeDtypeStruct(table.shape, table.dtype),
            jax.ShapeDtypeStruct(factors.shape, factors.dtype),
        ),
        in_specs=[VMEM, VMEM, HBM, HBM],
        out_specs=(VMEM,) * 4,
        scratch_shapes=[pltpu.SemaphoreType.DMA((5,))],
        compiler_params=limit,
    )(owners, columns, in_hbm(table), in_hbm(factors))

    strain, spectra = pl.pallas_call(
        functools.partial(early_kernel, groups, planes),
        out_shape=(
            jax.ShapeDtypeStruct((depth, 5, rows, width), jnp.float32),
            jax.ShapeDtypeStruct((3 * PAD_ROWS + 6 * 8, 2 * kxr), jnp.float32),
        ),
        in_specs=[VMEM] * 4,
        out_specs=(VMEM,) * 2,
        scratch_shapes=[pltpu.VMEM((2 * (5 * rows + 6 * 8), width), jnp.bfloat16)],
        compiler_params=limit,
    )(own_one, own_two, table, factors)

    reach = rows + 4
    held = pltpu.VMEM((2 * 7 * rows, width), jnp.bfloat16)
    earlier = pl.pallas_call(
        late_kernel,
        out_shape=jax.ShapeDtypeStruct((7 * rows, 2 * kxr), jnp.float32),
        in_specs=[VMEM] * 6,
        out_specs=VMEM,
        scratch_shapes=[held],
        compiler_params=limit,
    )(own_two, plane_one, row_one, row_two, strain, table)
    outgoing = pl.pallas_call(
        functools.partial(last_kernel, planes, groups, CAP),
        out_shape=jax.ShapeDtypeStruct((planes * groups * reach, 128), jnp.int16),
        in_specs=[VMEM] * 10,
        out_specs=VMEM,
        scratch_shapes=[held, pltpu.VMEM((groups * reach, 128), jnp.float32)],
        compiler_params=limit,
    )(own_one, plane_two, row_one, row_two, strain, table, earlier, spectra, factors, pick)
    outgoing = outgoing.reshape(planes * groups, reach // 2, 2, 128)
    received = lax.all_to_all(outgoing, ("gz", "gy"), split_axis=0, concat_axis=0, tiled=True)
    received = received.reshape(planes * groups * reach, 128)

    basis = jnp.asarray(y_tables(rows, groups, kyr))
    solved = pl.pallas_call(
        functools.partial(solve_kernel, kyr, depth, CAP, reach),
        out_shape=jax.ShapeDtypeStruct((CAP * 2, depth, kyr), jnp.float32),
        in_specs=[VMEM] * 3,
        out_specs=VMEM,
        scratch_shapes=[pltpu.VMEM(received.shape, jnp.float32)],
        compiler_params=limit,
    )(received, basis, green)
    return solved.reshape(1, CAP, 2, depth, kyr)


def solution(mesh):
    placed = (P("gz", "gy", None), P("gz", "gy", None), P("gz", "gy", None), P(), P(), P(), P())
    return jax.shard_map(
        functools.partial(per_device, mesh.shape["gy"], mesh.shape["gz"]),
        mesh=mesh,
        in_specs=placed,
        out_specs=P("gy", None, None, "gz", None),
        check_vma=False,
    )
```

```python
import functools
import math

import jax
import jax.numpy as jnp
import numpy as np
from jax import lax
from jax.experimental import pallas as pl
from jax.experimental.pallas import tpu as pltpu
from jax.sharding import PartitionSpec as P

CAP = 16
SMAG_COEF = 0.12
STRAIN_FLOOR = 0.01
BASE_SHIFT = 0.004
MODE_SHIFT = 0.02

CHUNK = 256
PAD_ROWS = 24
CODES = 32000.0
STEPS = 32.0
VMEM = pl.BlockSpec(memory_space=pltpu.VMEM)
HBM = pl.BlockSpec(memory_space=pltpu.HBM)
SMEM = pl.BlockSpec(memory_space=pltpu.SMEM)


def split(value):
    high = value.astype(jnp.bfloat16)
    low = (value - high.astype(jnp.float32)).astype(jnp.bfloat16)
    return high, low


def split_table(table, parts):
    pieces = []
    for _ in range(parts):
        pieces.append(table.astype(jnp.bfloat16))
        table = table - pieces[-1].astype(np.float64)
    return pieces


def matmul(left, right):
    return jnp.dot(left, right, preferred_element_type=jnp.float32)


def x_tables(width, kxr, grid_rows):
    norm = 1.0 / math.sqrt(width * grid_rows)
    phase = (np.arange(width)[:, None] * np.arange(kxr)[None, :] % width) * (2.0 * np.pi / width)
    table = np.stack([np.cos(phase) * norm, -np.sin(phase) * norm], axis=2)
    pieces = split_table(table.reshape(width, 2 * kxr), 2)
    angle = np.arange(kxr) * (2.0 * np.pi / width)
    turn = np.stack([-np.sin(angle), np.sin(angle)], axis=1).reshape(2 * kxr) * 0.5
    second = np.repeat(-4.0 * np.sin(angle * 0.5) ** 2, 2)
    return np.concatenate(pieces, axis=1), np.stack([turn, second]).astype(np.float32)


def y_tables(rows, groups, kyr):
    grid_rows = rows * groups
    nowhere = -grid_rows
    offset = np.concatenate([[nowhere, -1, rows, nowhere], np.arange(rows)])
    cells = (np.arange(groups)[:, None] * rows + offset[None, :]).reshape(-1)
    ky = np.arange(kyr) - kyr // 2
    phase = (ky[:, None] * cells[None, :] % grid_rows) * (2.0 * np.pi / grid_rows)
    valid = (cells >= 0) & (cells < grid_rows)
    table = np.concatenate([np.cos(phase), np.sin(phase)], axis=0) * valid[None, :]
    return np.concatenate(split_table(table, 2), axis=0)


def mode_kernel(
    groups, capacity, kyr, levels, depth,
    owners, columns, table_hbm, factors_hbm,
    pick, green, table, factors, arrived,
):
    copies = [pltpu.make_async_copy(factors_hbm, factors, arrived.at[0])]
    share = table.shape[0] // (arrived.shape[0] - 1)
    for i in range(1, arrived.shape[0]):
        at = pl.ds((i - 1) * share, share)
        copies.append(pltpu.make_async_copy(table_hbm.at[at], table.at[at], arrived.at[i]))
    for copy in copies:
        copy.start()
    kxr = owners.shape[1]
    below, above, metric = [
        [columns[i * levels + k : i * levels + k + 1, :] for k in range(levels)] for i in range(3)
    ]
    places, gy = lax.axis_index("gz"), lax.axis_index("gy")
    shape = (2 * kxr, kxr)
    mode = lax.broadcasted_iota(jnp.int32, shape, 0) // 2
    other = lax.broadcasted_iota(jnp.int32, shape, 1)
    named = owners[...].astype(jnp.float32)
    owner = jnp.sum(jnp.where(mode == other, named, 0.0), axis=1, keepdims=True)
    rank = jnp.sum(
        jnp.where((named == owner) & (other < mode), 1.0, 0.0), axis=1, keepdims=True
    )
    slot = (owner * capacity + rank).astype(jnp.int32)
    part = lax.broadcasted_iota(jnp.int32, (2 * kxr, 1), 0) % 2
    column = lax.broadcasted_iota(jnp.int32, (2 * kxr, groups * capacity * 2), 1)
    pick[...] = jnp.where(slot * 2 + part == column, 1.0, 0.0).astype(jnp.bfloat16)

    lane = lax.broadcasted_iota(jnp.int32, (2 * kxr, 128), 1)
    here = gy * capacity + lane % (2 * capacity) // 2
    owned = (slot == here) & (part == 0)
    mode_id = (lax.broadcasted_iota(jnp.int32, (2 * kxr, 128), 0) // 2).astype(jnp.float32)
    kx = jnp.sum(jnp.where(owned, mode_id, 0.0), axis=0, keepdims=True)
    filled = jnp.sum(jnp.where(owned, 1.0, 0.0), axis=0, keepdims=True)

    size = 64
    at = lax.broadcasted_iota(jnp.int32, (size, 128), 1) // (2 * capacity)

    def turn(step, carry):
        start = pl.multiple_of(step * size, size)
        ky = lax.broadcasted_iota(jnp.int32, (size, 128), 0) + (start - kyr // 2)
        ky = ky.astype(jnp.float32)
        radius = kx * kx + ky * ky
        inside = jnp.where(radius <= float(kxr * kxr), filled, 0.0)
        shift = BASE_SHIFT + MODE_SHIFT * (radius / float(kxr * kxr))
        inverse = []
        for k in range(levels):
            pivot = -(below[k] + above[k] + metric[k] * shift)
            if k > 0:
                pivot = pivot - below[k] * above[k - 1] * inverse[-1]
            inverse.append(1.0 / pivot)
        for k in range(depth):
            target = places * depth + k
            forward = []
            for pos in range(levels):
                unit = jnp.where(target == pos, 1.0, 0.0)
                value = inside * unit
                if pos > 0:
                    value = value - above[pos - 1] * inverse[pos - 1] * forward[-1]
                forward.append(value)
            weights = [None] * levels
            for pos in range(levels - 1, -1, -1):
                value = forward[pos]
                if pos < levels - 1:
                    value = value - below[pos + 1] * weights[pos + 1]
                weights[pos] = value * inverse[pos]
            for block in range(levels // depth):
                total = jnp.zeros((size, 128), jnp.float32)
                for j in range(depth + 2):
                    pos = block * depth - 1 + j
                    if 0 <= pos < levels:
                        total = jnp.where(at == j, weights[pos], total)
                green[k, block, pl.ds(start, size), :] = total
        return carry

    lax.fori_loop(0, kyr // size, turn, 0)
    for copy in copies:
        copy.wait()


def pack_kernel(
    vx, vy, vz, owners_hbm, below_hbm, above_hbm, metric_hbm,
    own_one, own_two, row_one, row_two, owners, columns, scalars, arrived, small,
):
    rows = vx.shape[1]
    odd, odd_row = lax.axis_index("gz") % 2, lax.axis_index("gy") % 2
    copies = []
    for i, field in enumerate((vx, vy, vz)):
        for k, plane in enumerate((own_one, own_two)):
            level = odd if k else 1 - odd
            copies.append(pltpu.make_async_copy(field.at[level], plane.at[i], arrived.at[i, k]))
    others = [pltpu.make_async_copy(owners_hbm, owners, small.at[3])]
    for i, array in enumerate((below_hbm, above_hbm, metric_hbm)):
        others.append(pltpu.make_async_copy(array, scalars.at[i], small.at[i]))
    for copy in copies + others:
        copy.start()
    sub = lax.broadcasted_iota(jnp.int32, (8, vx.shape[2]), 0)
    bottom = jnp.zeros((8, vx.shape[2]), jnp.float32)
    top = bottom
    for copy in others:
        copy.wait()
    levels = scalars.shape[1]
    for i in range(3):
        for k in range(levels):
            at = i * levels + k
            columns[at : at + 1, :] = jnp.full((1, 128), scalars[i, k], jnp.float32)
    for i in range(3):
        for k, plane in enumerate((own_one, own_two)):
            copies[2 * i + k].wait()
            field = plane[i].astype(jnp.float32)
            bottom = jnp.where(sub == 2 * i + k, field[0:1], bottom)
            top = jnp.where(sub == 2 * i + k, field[rows - 1 : rows], top)
    row_one[...] = jnp.where(odd_row == 0, top, bottom).astype(jnp.bfloat16)
    row_two[...] = jnp.where(odd_row == 0, bottom, top).astype(jnp.bfloat16)


def up(field):
    return pltpu.roll(field, PAD_ROWS - 1, 0)


def down(field):
    return pltpu.roll(field, 1, 0)


def padded(field):
    empty = jnp.zeros((PAD_ROWS - field.shape[0], field.shape[1]), field.dtype)
    return jnp.concatenate([field, empty], axis=0)


def magnitude(squared):
    return SMAG_COEF * (squared * lax.rsqrt(squared))


def put_lines(lines, cells, fields):
    count = lines.shape[0] // 2
    start = 0
    for field in fields:
        high, low = split(field)
        size = field.shape[0]
        lines[start : start + size, cells] = high
        lines[count + start : count + start + size, cells] = low
        start += size


def transformed(lines, table):
    count, modes = lines.shape[0] // 2, table.shape[1] // 2
    product = matmul(lines[...], table[...])
    product = product[:count] + product[count:]
    return product[:, :modes] + product[:, modes:]


def slope_of(factors, field):
    modes = field.shape[1]
    even = lax.broadcasted_iota(jnp.int32, (1, modes), 1) % 2 == 0
    moved = jnp.where(even, pltpu.roll(field, modes - 1, 1), pltpu.roll(field, 1, 1))
    return factors[0:1] * moved


def early_kernel(
    groups, planes,
    own_one, own_two, table, factors,
    strain, spectra, lines,
):
    rows, width = own_one.shape[1:]
    gz, gy = lax.axis_index("gz"), lax.axis_index("gy")
    first = jnp.where(gz == 0, 1.0, 0.0)
    last = jnp.where(gz == planes - 1, 1.0, 0.0)
    odd = gz % 2
    sub = lax.broadcasted_iota(jnp.int32, (8, CHUNK), 0)
    ghost_rows = jnp.where((sub == 0) & (gy == groups - 1) | (sub == 7) & (gy == 0), 1.0, 0.0)

    for step in range(width // CHUNK):
        here = step * CHUNK
        before, after = (here - 128) % width, (here + CHUNK) % width
        cells = pl.ds(here, CHUNK)
        flat, rims = [], []
        for k, source in enumerate((own_one, own_two)):
            sign = jnp.where(odd == k, 1.0, -1.0)
            own = [source[i, :, cells].astype(jnp.float32) for i in range(3)]
            x, y, rim = [], [], []
            for i in range(3):
                window = jnp.concatenate(
                    [
                        source[i, :, pl.ds(before, 128)].astype(jnp.float32),
                        own[i],
                        source[i, :, pl.ds(after, 128)].astype(jnp.float32),
                    ],
                    axis=1,
                )
                difference = pltpu.roll(window, CHUNK + 255, 1) - pltpu.roll(window, 1, 1)
                x.append(difference[:, 128 : 128 + CHUNK])
                field = padded(own[i])
                difference = up(field) - down(field)
                y.append(difference[:rows])
                rim.append(difference[rows:])
            e01 = y[0] + x[1]
            strain[k, 0, :, cells] = x[0]
            strain[k, 1, :, cells] = y[1]
            strain[k, 2, :, cells] = e01
            strain[k, 3, :, cells] = sign * x[2]
            strain[k, 4, :, cells] = sign * y[2]
            squared = 0.5 * (rim[1] * rim[1]) + 0.25 * (rim[0] * rim[0] + rim[2] * rim[2])
            viscous = ghost_rows * magnitude(squared + STRAIN_FLOOR)
            rims += [viscous * rim[0], viscous * rim[1], viscous * (sign * rim[2])]
            flat.append(x[0] + y[1])

        ghost = [(first - last) * own_two[i, :, cells].astype(jnp.float32) for i in range(3)]
        squared = 0.5 * (ghost[2] * ghost[2])
        squared = squared + 0.25 * (ghost[0] * ghost[0] + ghost[1] * ghost[1])
        viscous = magnitude(squared + STRAIN_FLOOR)
        edge = [viscous * ghost[i] for i in range(3)]
        put_lines(lines, cells, flat + edge + [jnp.concatenate(rims, axis=0)])

    total = transformed(lines, table)
    pieces = [padded(total[rows * i : rows * (i + 1)]) for i in range(5)]
    t02, t12, s22 = pieces[2:]
    cross = 0.25 * (up(t12) - down(t12)) + slope_of(factors, t02)
    pieces = pieces[:2] + [s22 + (last - first) * cross]
    for i, piece in enumerate(pieces + [total[5 * rows :]]):
        spectra[PAD_ROWS * i : PAD_ROWS * i + piece.shape[0], :] = piece


def stress_lines(k, other, plane, row_one, row_two, strain, table, lines):
    rows, width = other.shape[1:]
    odd_row = lax.axis_index("gy") % 2
    sign = jnp.where(lax.axis_index("gz") % 2 == k, 1.0, -1.0)
    row = lax.broadcasted_iota(jnp.int32, (rows, CHUNK), 0)
    for step in range(width // CHUNK):
        cells = pl.ds(step * CHUNK, CHUNK)
        ones = row_one[:, cells].astype(jnp.float32)
        twos = row_two[:, cells].astype(jnp.float32)
        lows = jnp.where(odd_row == 0, twos, ones)
        highs = jnp.where(odd_row == 0, ones, twos)
        z, beyond = [], []
        for i in range(3):
            at = 2 * i + k
            z.append(plane[i, :, cells].astype(jnp.float32) - other[i, :, cells].astype(jnp.float32))
            beyond.append(
                jnp.where(
                    row == rows - 1,
                    highs[at : at + 1],
                    jnp.where(row == 0, -lows[at : at + 1], 0.0),
                )
            )
        x0 = strain[k, 0, :, cells]
        y1 = strain[k, 1, :, cells] + beyond[1]
        e01 = strain[k, 2, :, cells] + beyond[0]
        e02 = z[0] + strain[k, 3, :, cells]
        e12 = z[1] + strain[k, 4, :, cells] + sign * beyond[2]
        squared = 0.5 * (x0 * x0 + y1 * y1 + z[2] * z[2]) + STRAIN_FLOOR
        squared = squared + 0.25 * (e01 * e01 + e02 * e02 + e12 * e12)
        viscous = magnitude(squared)
        fields = [viscous * field for field in (e01, y1, e12, z[2], e02, x0)]
        put_lines(lines, cells, fields + [z[2] + sign * beyond[1]])
    return transformed(lines, table)


def late_kernel(other, plane, row_one, row_two, strain, table, out, lines):
    out[...] = stress_lines(0, other, plane, row_one, row_two, strain, table, lines)


def last_kernel(
    planes, groups, capacity,
    other, plane, row_one, row_two, strain, table, earlier, spectra, factors, pick,
    out, lines, codes,
):
    rows = other.shape[1]
    gz = lax.axis_index("gz")
    first = jnp.where(gz == 0, 1.0, 0.0)
    last = jnp.where(gz == planes - 1, 1.0, 0.0)
    odd = gz % 2
    totals = (earlier, stress_lines(1, other, plane, row_one, row_two, strain, table, lines))
    parts = []
    for k in range(2):
        sign = jnp.where(odd == k, 1.0, -1.0)
        pieces = [totals[k][rows * i : rows * (i + 1)] for i in range(7)]
        for i in range(3):
            start = 3 * PAD_ROWS + 8 * (3 * k + i)
            pieces[i] = jnp.concatenate([pieces[i], spectra[start : start + 8, :]], axis=0)
        t01, p11, t12 = pieces[:3]
        s22, t02, s00, rise = [padded(piece) for piece in pieces[3:]]
        p11 = up(p11) + down(p11) - 2.0 * p11
        t01 = up(t01) - down(t01)
        t12 = 0.25 * (up(t12) - down(t12))
        flat = spectra[k * PAD_ROWS : (k + 1) * PAD_ROWS, :]
        s22, rise = sign * s22, sign * rise
        middle = p11 - 2.0 * s22 + 0.5 * (flat + rise)
        middle = middle + slope_of(factors, t01) + factors[1:2] * s00
        cross = sign * (t12 + slope_of(factors, t02))
        parts.append([s22 + cross, middle, s22 - cross])

    ghost = spectra[2 * PAD_ROWS : 3 * PAD_ROWS, :]
    lower = [jnp.where(odd == 1, p, q) for p, q in zip(*parts)]
    upper = [jnp.where(odd == 1, q, p) for p, q in zip(*parts)]
    spectrum = [
        lower[0],
        lower[1] + upper[0] + first * ghost,
        lower[2] + upper[1] + last * ghost,
        upper[2],
    ]
    count = len(spectrum)

    stacked = jnp.concatenate(spectrum, axis=0)
    selected = matmul(jnp.concatenate(split(stacked), axis=0), pick[...])
    size = count * PAD_ROWS
    selected = selected[:size] + selected[size:]

    lane = lax.broadcasted_iota(jnp.int32, (PAD_ROWS, 128), 1)
    empty_block = jnp.zeros((PAD_ROWS, 128), jnp.float32)
    sub_lanes = lax.broadcasted_iota(jnp.int32, (8, 128), 0)
    share = 2 * capacity
    for half in range(groups * share // 128):
        pieces = [
            selected[PAD_ROWS * j : PAD_ROWS * (j + 1), 128 * half : 128 * (half + 1)]
            for j in range(count)
        ]
        for place in range(128 // share):
            block = empty_block
            for j in range(count):
                distance = (share * (j - place)) % 128
                moved = pltpu.roll(pieces[j], distance, 1) if distance else pieces[j]
                block = jnp.where(lane // share == j, moved, block)
            largest = jnp.max(jnp.abs(block), axis=0, keepdims=True)
            power = jnp.floor(jnp.log2(jnp.maximum(largest, 1e-35)) * STEPS) + 1.0
            block = jnp.floor(block * (CODES * jnp.exp2(power * (-1.0 / STEPS))) + 0.5)
            rim = pltpu.roll(block[rows:], 2, 0)
            rim = jnp.where(sub_lanes == 0, power, jnp.where(sub_lanes < 3, rim, 0.0))
            base = (half * (128 // share) + place) * (rows + 4)
            codes[base : base + 4, :] = rim[:4]
            codes[base + 4 : base + 4 + rows, :] = block[:rows]
    packed = codes[...].astype(jnp.int32).astype(jnp.int16)
    for side in range(planes):
        out[side * packed.shape[0] : (side + 1) * packed.shape[0], :] = packed


def solve_kernel(kyr, depth, capacity, reach, received, basis, green, out, codes):
    planes = green.shape[1]
    sources = received.shape[0] // reach
    codes[...] = received[...].astype(jnp.int32).astype(jnp.float32)
    power = codes[pl.ds(0, sources, stride=reach), :]
    scale = jnp.exp2(power * (1.0 / STEPS)) * (1.0 / CODES)
    row = lax.broadcasted_iota(jnp.int32, (2 * reach, 128), 0)
    values = []
    for pair in range(0, sources, 2):
        factor = jnp.where(row < reach, scale[pair : pair + 1], scale[pair + 1 : pair + 2])
        values.append(codes[pair * reach : (pair + 2) * reach, :] * factor)
    each = sources // planes // 2
    blocks = [jnp.concatenate(values[i * each : (i + 1) * each], axis=0) for i in range(planes)]
    high, low = split(jnp.concatenate(blocks, axis=1))
    product = matmul(basis[...], high)
    product = product[: 2 * kyr] + product[2 * kyr :] + matmul(basis[: 2 * kyr, :], low)
    cosine = [jnp.zeros((kyr, 128), jnp.float32) for _ in range(depth)]
    sine = [jnp.zeros((kyr, 128), jnp.float32) for _ in range(depth)]
    for block in range(planes):
        lanes = slice(block * 128, (block + 1) * 128)
        for k in range(depth):
            cosine[k] = cosine[k] + green[k, block] * product[:kyr, lanes]
            sine[k] = sine[k] + green[k, block] * product[kyr:, lanes]
    lane = lax.broadcasted_iota(jnp.int32, (kyr, 128), 1)
    share = 2 * capacity

    def gathered(fields):
        fields = [field + pltpu.roll(field, 64, 1) for field in fields]
        field = jnp.where(lane < 64, fields[0], fields[1])
        return field + pltpu.roll(field, share, 1)

    turned = gathered(sine)
    turned = jnp.where(lane % 2 == 0, pltpu.roll(turned, 127, 1), -pltpu.roll(turned, 1, 1))
    result = gathered(cosine) + turned
    flipped = result.T
    for k in range(depth):
        out[:, k, :] = flipped[64 * k + share : 64 * k + 2 * share]


def exchange(array, axis, size, shifted):
    pairs = [(i, i + 1) for i in range(shifted, size - 1, 2)]
    return lax.ppermute(array, axis, pairs + [(j, i) for i, j in pairs])


def in_hbm(array):
    return pltpu.with_memory_space_constraint(array, pltpu.HBM)


def per_device(groups, planes, velocity_x, velocity_y, velocity_z, owners, below, above, metric):
    depth, rows, width = velocity_x.shape
    kxr = owners.shape[0]
    kyr = 2 * kxr
    levels = below.shape[0]
    limit = pltpu.CompilerParams(vmem_limit_bytes=32 * 1024 * 1024)
    fields = (velocity_x, velocity_y, velocity_z)

    plane_shape = jax.ShapeDtypeStruct((3, rows, width), jnp.bfloat16)
    row_shape = jax.ShapeDtypeStruct((8, width), jnp.bfloat16)
    own_one, own_two, row_one, row_two, owners, columns = pl.pallas_call(
        pack_kernel,
        out_shape=(plane_shape, plane_shape, row_shape, row_shape)
        + (
            jax.ShapeDtypeStruct((1, kxr), jnp.int32),
            jax.ShapeDtypeStruct((3 * levels, 128), jnp.float32),
        ),
        in_specs=[HBM] * 7,
        out_specs=(VMEM,) * 6,
        scratch_shapes=[
            pltpu.SMEM((3, levels), jnp.float32),
            pltpu.SemaphoreType.DMA((3, 2)),
            pltpu.SemaphoreType.DMA((4,)),
        ],
        compiler_params=limit,
    )(*[in_hbm(array) for array in (*fields, owners.reshape(1, kxr), below, above, metric)])
    plane_one = exchange(own_one, "gz", planes, 0)
    plane_two = exchange(own_two, "gz", planes, 1)
    row_one = exchange(row_one, "gy", groups, 0)
    row_two = exchange(row_two, "gy", groups, 1)

    table, factors = [jnp.asarray(array) for array in x_tables(width, kxr, rows * groups)]
    pick, green, table, factors = pl.pallas_call(
        functools.partial(mode_kernel, groups, CAP, kyr, levels, depth),
        out_shape=(
            jax.ShapeDtypeStruct((2 * kxr, groups * CAP * 2), jnp.bfloat16),
            jax.ShapeDtypeStruct((depth, planes, kyr, 128), jnp.float32),
            jax.ShapeDtypeStruct(table.shape, table.dtype),
            jax.ShapeDtypeStruct(factors.shape, factors.dtype),
        ),
        in_specs=[VMEM, VMEM, HBM, HBM],
        out_specs=(VMEM,) * 4,
        scratch_shapes=[pltpu.SemaphoreType.DMA((5,))],
        compiler_params=limit,
    )(owners, columns, in_hbm(table), in_hbm(factors))

    strain, spectra = pl.pallas_call(
        functools.partial(early_kernel, groups, planes),
        out_shape=(
            jax.ShapeDtypeStruct((depth, 5, rows, width), jnp.float32),
            jax.ShapeDtypeStruct((3 * PAD_ROWS + 6 * 8, 2 * kxr), jnp.float32),
        ),
        in_specs=[VMEM] * 4,
        out_specs=(VMEM,) * 2,
        scratch_shapes=[pltpu.VMEM((2 * (5 * rows + 6 * 8), width), jnp.bfloat16)],
        compiler_params=limit,
    )(own_one, own_two, table, factors)

    reach = rows + 4
    held = pltpu.VMEM((2 * 7 * rows, width), jnp.bfloat16)
    earlier = pl.pallas_call(
        late_kernel,
        out_shape=jax.ShapeDtypeStruct((7 * rows, 2 * kxr), jnp.float32),
        in_specs=[VMEM] * 6,
        out_specs=VMEM,
        scratch_shapes=[held],
        compiler_params=limit,
    )(own_two, plane_one, row_one, row_two, strain, table)
    outgoing = pl.pallas_call(
        functools.partial(last_kernel, planes, groups, CAP),
        out_shape=jax.ShapeDtypeStruct((planes * groups * reach, 128), jnp.int16),
        in_specs=[VMEM] * 10,
        out_specs=VMEM,
        scratch_shapes=[held, pltpu.VMEM((groups * reach, 128), jnp.float32)],
        compiler_params=limit,
    )(own_one, plane_two, row_one, row_two, strain, table, earlier, spectra, factors, pick)
    outgoing = outgoing.reshape(planes * groups, reach // 2, 2, 128)
    received = lax.all_to_all(outgoing, ("gz", "gy"), split_axis=0, concat_axis=0, tiled=True)
    received = received.reshape(planes * groups * reach, 128)

    basis = jnp.asarray(y_tables(rows, groups, kyr))
    solved = pl.pallas_call(
        functools.partial(solve_kernel, kyr, depth, CAP, reach),
        out_shape=jax.ShapeDtypeStruct((CAP * 2, depth, kyr), jnp.float32),
        in_specs=[VMEM] * 3,
        out_specs=VMEM,
        scratch_shapes=[pltpu.VMEM(received.shape, jnp.float32)],
        compiler_params=limit,
    )(received, basis, green)
    return solved.reshape(1, CAP, 2, depth, kyr)


def solution(mesh):
    placed = (P("gz", "gy", None), P("gz", "gy", None), P("gz", "gy", None), P(), P(), P(), P())
    return jax.shard_map(
        functools.partial(per_device, mesh.shape["gy"], mesh.shape["gz"]),
        mesh=mesh,
        in_specs=placed,
        out_specs=P("gy", None, None, "gz", None),
        check_vma=False,
    )
```

```python
import functools
import math

import jax
import jax.numpy as jnp
import numpy as np
from jax import lax
from jax.experimental import pallas as pl
from jax.experimental.pallas import tpu as pltpu
from jax.sharding import PartitionSpec as P

CAP = 16
SMAG_COEF = 0.12
STRAIN_FLOOR = 0.01
BASE_SHIFT = 0.004
MODE_SHIFT = 0.02

CHUNK = 256
PAD_ROWS = 24
CODES = 32000.0
STEPS = 32.0
PIECES = 3
VMEM = pl.BlockSpec(memory_space=pltpu.VMEM)
HBM = pl.BlockSpec(memory_space=pltpu.HBM)
SMEM = pl.BlockSpec(memory_space=pltpu.SMEM)


def split(value):
    high = value.astype(jnp.bfloat16)
    low = (value - high.astype(jnp.float32)).astype(jnp.bfloat16)
    return high, low


def split_table(table, parts):
    pieces = []
    for _ in range(parts):
        pieces.append(table.astype(jnp.bfloat16))
        table = table - pieces[-1].astype(np.float64)
    return pieces


def matmul(left, right):
    return jnp.dot(left, right, preferred_element_type=jnp.float32)


def mode_order(place, kxr):
    return 2 * place - (2 * place // kxr) * (kxr - 1)


def x_tables(width, kxr, grid_rows):
    norm = 1.0 / math.sqrt(width * grid_rows)
    modes = mode_order(np.arange(kxr), kxr)
    phase = (np.arange(width // 2)[:, None] * modes[None, :] % width) * (2.0 * np.pi / width)
    table = np.stack([np.cos(phase) * norm, -np.sin(phase) * norm], axis=2)
    table = table.reshape(width // 2, 2, kxr).transpose(1, 0, 2).reshape(width, kxr)
    angle = modes * (2.0 * np.pi / width)
    turn = np.stack([-np.sin(angle), np.sin(angle)], axis=1).reshape(2 * kxr) * 0.5
    second = np.repeat(-4.0 * np.sin(angle * 0.5) ** 2, 2)
    pieces = split_table(table, PIECES) + [np.zeros(table.shape, jnp.bfloat16)]
    return np.concatenate(pieces, axis=1), np.stack([turn, second]).astype(np.float32)


def y_tables(rows, groups, kyr):
    grid_rows = rows * groups
    nowhere = -grid_rows
    offset = np.concatenate([[nowhere, -1, rows, nowhere], np.arange(rows)])
    cells = (np.arange(groups)[:, None] * rows + offset[None, :]).reshape(-1)
    ky = np.arange(kyr) - kyr // 2
    phase = (ky[:, None] * cells[None, :] % grid_rows) * (2.0 * np.pi / grid_rows)
    valid = (cells >= 0) & (cells < grid_rows)
    table = np.concatenate([np.cos(phase), np.sin(phase)], axis=0) * valid[None, :]
    return np.concatenate(split_table(table, 2), axis=0)


def mode_kernel(
    groups, capacity, kyr, levels, depth,
    owners, columns, table_hbm, factors_hbm,
    pick, green, table, factors, arrived,
):
    copies = [pltpu.make_async_copy(factors_hbm, factors, arrived.at[0])]
    share = table.shape[0] // (arrived.shape[0] - 1)
    for i in range(1, arrived.shape[0]):
        at = pl.ds((i - 1) * share, share)
        copies.append(pltpu.make_async_copy(table_hbm.at[at], table.at[at], arrived.at[i]))
    for copy in copies:
        copy.start()
    kxr = owners.shape[1]
    below, above, metric = [
        [columns[i * levels + k : i * levels + k + 1, :] for k in range(levels)] for i in range(3)
    ]
    places, gy = lax.axis_index("gz"), lax.axis_index("gy")
    shape = (2 * kxr, kxr)
    mode = mode_order(lax.broadcasted_iota(jnp.int32, shape, 0) // 2, kxr)
    other = lax.broadcasted_iota(jnp.int32, shape, 1)
    named = owners[...].astype(jnp.float32)
    owner = jnp.sum(jnp.where(mode == other, named, 0.0), axis=1, keepdims=True)
    rank = jnp.sum(
        jnp.where((named == owner) & (other < mode), 1.0, 0.0), axis=1, keepdims=True
    )
    slot = (owner * capacity + rank).astype(jnp.int32)
    part = lax.broadcasted_iota(jnp.int32, (2 * kxr, 1), 0) % 2
    column = lax.broadcasted_iota(jnp.int32, (2 * kxr, groups * capacity * 2), 1)
    pick[...] = jnp.where(slot * 2 + part == column, 1.0, 0.0).astype(jnp.bfloat16)

    lane = lax.broadcasted_iota(jnp.int32, (2 * kxr, 128), 1)
    here = gy * capacity + lane % (2 * capacity) // 2
    owned = (slot == here) & (part == 0)
    mode_id = mode_order(lax.broadcasted_iota(jnp.int32, (2 * kxr, 128), 0) // 2, kxr)
    mode_id = mode_id.astype(jnp.float32)
    kx = jnp.sum(jnp.where(owned, mode_id, 0.0), axis=0, keepdims=True)
    filled = jnp.sum(jnp.where(owned, 1.0, 0.0), axis=0, keepdims=True)

    size = 64
    at = lax.broadcasted_iota(jnp.int32, (size, 128), 1) // (2 * capacity)

    def turn(step, carry):
        start = pl.multiple_of(step * size, size)
        ky = lax.broadcasted_iota(jnp.int32, (size, 128), 0) + (start - kyr // 2)
        ky = ky.astype(jnp.float32)
        radius = kx * kx + ky * ky
        inside = jnp.where(radius <= float(kxr * kxr), filled, 0.0)
        shift = BASE_SHIFT + MODE_SHIFT * (radius / float(kxr * kxr))
        inverse = []
        for k in range(levels):
            pivot = -(below[k] + above[k] + metric[k] * shift)
            if k > 0:
                pivot = pivot - below[k] * above[k - 1] * inverse[-1]
            inverse.append(1.0 / pivot)
        for k in range(depth):
            target = places * depth + k
            forward = []
            for pos in range(levels):
                unit = jnp.where(target == pos, 1.0, 0.0)
                value = inside * unit
                if pos > 0:
                    value = value - above[pos - 1] * inverse[pos - 1] * forward[-1]
                forward.append(value)
            weights = [None] * levels
            for pos in range(levels - 1, -1, -1):
                value = forward[pos]
                if pos < levels - 1:
                    value = value - below[pos + 1] * weights[pos + 1]
                weights[pos] = value * inverse[pos]
            for block in range(levels // depth):
                total = jnp.zeros((size, 128), jnp.float32)
                for j in range(depth + 2):
                    pos = block * depth - 1 + j
                    if 0 <= pos < levels:
                        total = jnp.where(at == j, weights[pos], total)
                green[k, block, pl.ds(start, size), :] = total
        return carry

    lax.fori_loop(0, kyr // size, turn, 0)
    for copy in copies:
        copy.wait()


def pack_kernel(
    vx, vy, vz, owners_hbm, below_hbm, above_hbm, metric_hbm,
    own_one, own_two, row_one, row_two, owners, columns, scalars, arrived, small,
):
    rows = vx.shape[1]
    odd, odd_row = lax.axis_index("gz") % 2, lax.axis_index("gy") % 2
    copies = []
    for i, field in enumerate((vx, vy, vz)):
        for k, plane in enumerate((own_one, own_two)):
            level = odd if k else 1 - odd
            copies.append(pltpu.make_async_copy(field.at[level], plane.at[i], arrived.at[i, k]))
    others = [pltpu.make_async_copy(owners_hbm, owners, small.at[3])]
    for i, array in enumerate((below_hbm, above_hbm, metric_hbm)):
        others.append(pltpu.make_async_copy(array, scalars.at[i], small.at[i]))
    for copy in copies + others:
        copy.start()
    sub = lax.broadcasted_iota(jnp.int32, (8, vx.shape[2]), 0)
    bottom = jnp.zeros((8, vx.shape[2]), jnp.float32)
    top = bottom
    for copy in others:
        copy.wait()
    levels = scalars.shape[1]
    for i in range(3):
        for k in range(levels):
            at = i * levels + k
            columns[at : at + 1, :] = jnp.full((1, 128), scalars[i, k], jnp.float32)
    for i in range(3):
        for k, plane in enumerate((own_one, own_two)):
            copies[2 * i + k].wait()
            field = plane[i].astype(jnp.float32)
            bottom = jnp.where(sub == 2 * i + k, field[0:1], bottom)
            top = jnp.where(sub == 2 * i + k, field[rows - 1 : rows], top)
    row_one[...] = jnp.where(odd_row == 0, top, bottom).astype(jnp.bfloat16)
    row_two[...] = jnp.where(odd_row == 0, bottom, top).astype(jnp.bfloat16)


def up(field):
    return pltpu.roll(field, PAD_ROWS - 1, 0)


def down(field):
    return pltpu.roll(field, 1, 0)


def padded(field):
    empty = jnp.zeros((PAD_ROWS - field.shape[0], field.shape[1]), field.dtype)
    return jnp.concatenate([field, empty], axis=0)


def magnitude(squared):
    return SMAG_COEF * (squared * lax.rsqrt(squared))


def put_lines(lines, step, near, far):
    cells = pl.ds(step * CHUNK, CHUNK)
    count = lines.shape[1] // PIECES
    start = 0
    for one, other in zip(near, far):
        size = one.shape[0]
        for parity, field in enumerate((one + other, one - other)):
            for piece in range(PIECES):
                at = piece * count + start
                part = field.astype(jnp.bfloat16)
                lines[parity, at : at + size, cells] = part
                field = field - part.astype(jnp.float32)
        start += size


def transformed(lines, table):
    count, half = lines.shape[1] // PIECES, lines.shape[2]
    modes = table.shape[1] // (PIECES + 1)
    totals = []
    for parity in range(2):
        product = matmul(lines[parity], table[parity * half : (parity + 1) * half, :])
        total = product[:count, : 2 * modes] + product[:count, 2 * modes :]
        for piece in range(1, PIECES):
            total = total + product[piece * count : (piece + 1) * count, : 2 * modes]
        totals.append(total + pltpu.roll(total, modes, 1))
    lane = lax.broadcasted_iota(jnp.int32, (1, 2 * modes), 1)
    return jnp.where(lane < modes, *totals)


def slope_of(factors, field):
    modes = field.shape[1]
    even = lax.broadcasted_iota(jnp.int32, (1, modes), 1) % 2 == 0
    moved = jnp.where(even, pltpu.roll(field, modes - 1, 1), pltpu.roll(field, 1, 1))
    return factors[0:1] * moved


def early_kernel(
    groups, planes,
    own_one, own_two, table, factors,
    strain, spectra, lines,
):
    rows, width = own_one.shape[1:]
    gz, gy = lax.axis_index("gz"), lax.axis_index("gy")
    first = jnp.where(gz == 0, 1.0, 0.0)
    last = jnp.where(gz == planes - 1, 1.0, 0.0)
    odd = gz % 2
    sub = lax.broadcasted_iota(jnp.int32, (8, CHUNK), 0)
    ghost_rows = jnp.where((sub == 0) & (gy == groups - 1) | (sub == 7) & (gy == 0), 1.0, 0.0)

    def fields_at(step):
        here = step * CHUNK
        before, after = (here - 128) % width, (here + CHUNK) % width
        cells = pl.ds(here, CHUNK)
        flat, rims = [], []
        for k, source in enumerate((own_one, own_two)):
            sign = jnp.where(odd == k, 1.0, -1.0)
            own = [source[i, :, cells].astype(jnp.float32) for i in range(3)]
            x, y, rim = [], [], []
            for i in range(3):
                window = jnp.concatenate(
                    [
                        source[i, :, pl.ds(before, 128)].astype(jnp.float32),
                        own[i],
                        source[i, :, pl.ds(after, 128)].astype(jnp.float32),
                    ],
                    axis=1,
                )
                difference = pltpu.roll(window, CHUNK + 255, 1) - pltpu.roll(window, 1, 1)
                x.append(difference[:, 128 : 128 + CHUNK])
                field = padded(own[i])
                difference = up(field) - down(field)
                y.append(difference[:rows])
                rim.append(difference[rows:])
            e01 = y[0] + x[1]
            strain[k, 0, :, cells] = x[0]
            strain[k, 1, :, cells] = y[1]
            strain[k, 2, :, cells] = e01
            strain[k, 3, :, cells] = sign * x[2]
            strain[k, 4, :, cells] = sign * y[2]
            squared = 0.5 * (rim[1] * rim[1]) + 0.25 * (rim[0] * rim[0] + rim[2] * rim[2])
            viscous = ghost_rows * magnitude(squared + STRAIN_FLOOR)
            rims += [viscous * rim[0], viscous * rim[1], viscous * (sign * rim[2])]
            flat.append(x[0] + y[1])

        ghost = [(first - last) * own_two[i, :, cells].astype(jnp.float32) for i in range(3)]
        squared = 0.5 * (ghost[2] * ghost[2])
        squared = squared + 0.25 * (ghost[0] * ghost[0] + ghost[1] * ghost[1])
        viscous = magnitude(squared + STRAIN_FLOOR)
        edge = [viscous * ghost[i] for i in range(3)]
        return flat + edge + [jnp.concatenate(rims, axis=0)]

    steps = width // CHUNK // 2
    for step in range(steps):
        put_lines(lines, step, fields_at(step), fields_at(step + steps))

    total = transformed(lines, table)
    pieces = [padded(total[rows * i : rows * (i + 1)]) for i in range(5)]
    t02, t12, s22 = pieces[2:]
    cross = 0.25 * (up(t12) - down(t12)) + slope_of(factors, t02)
    pieces = pieces[:2] + [s22 + (last - first) * cross]
    for i, piece in enumerate(pieces + [total[5 * rows :]]):
        spectra[PAD_ROWS * i : PAD_ROWS * i + piece.shape[0], :] = piece


def corrected(k, cells, row_one, row_two, strain):
    rows = strain.shape[2]
    odd_row = lax.axis_index("gy") % 2
    sign = jnp.where(lax.axis_index("gz") % 2 == k, 1.0, -1.0)
    row = lax.broadcasted_iota(jnp.int32, (rows, CHUNK), 0)
    ones = row_one[:, cells].astype(jnp.float32)
    twos = row_two[:, cells].astype(jnp.float32)
    lows = jnp.where(odd_row == 0, twos, ones)
    highs = jnp.where(odd_row == 0, ones, twos)

    def beyond(i):
        at = 2 * i + k
        inner = jnp.where(row == 0, -lows[at : at + 1], 0.0)
        return jnp.where(row == rows - 1, highs[at : at + 1], inner)

    x0, sx2 = strain[k, 0, :, cells], strain[k, 3, :, cells]
    edge = beyond(1)
    y1 = strain[k, 1, :, cells] + edge
    e01 = strain[k, 2, :, cells] + beyond(0)
    sy2 = strain[k, 4, :, cells] + sign * beyond(2)
    flat = 0.5 * (x0 * x0 + y1 * y1) + 0.25 * (e01 * e01) + STRAIN_FLOOR
    return x0, y1, e01, sx2, sy2, flat, sign * edge


def stress_lines(slopes_at, other, plane, table, lines):
    def fields_at(step):
        cells = pl.ds(step * CHUNK, CHUNK)
        x0, y1, e01, sx2, sy2, flat, edge = slopes_at(cells)
        z = [
            plane[i, :, cells].astype(jnp.float32) - other[i, :, cells].astype(jnp.float32)
            for i in range(3)
        ]
        e02, e12 = z[0] + sx2, z[1] + sy2
        squared = flat + 0.5 * (z[2] * z[2]) + 0.25 * (e02 * e02 + e12 * e12)
        viscous = magnitude(squared)
        fields = [viscous * field for field in (e01, y1, e12, z[2], e02, x0)]
        return fields + [z[2] + edge]

    steps = plane.shape[2] // CHUNK // 2
    for step in range(steps):
        put_lines(lines, step, fields_at(step), fields_at(step + steps))
    return transformed(lines, table)


def late_kernel(other, plane, row_one, row_two, strain, table, out, ready, lines):
    slopes_at = lambda cells: corrected(0, cells, row_one, row_two, strain)
    out[...] = stress_lines(slopes_at, other, plane, table, lines)
    for step in range(plane.shape[2] // CHUNK):
        cells = pl.ds(step * CHUNK, CHUNK)
        for i, field in enumerate(corrected(1, cells, row_one, row_two, strain)):
            ready[i, :, cells] = field


def last_kernel(
    planes, groups, capacity,
    other, plane, ready, table, earlier, spectra, factors, pick,
    out, lines, codes,
):
    rows = other.shape[1]
    gz = lax.axis_index("gz")
    first = jnp.where(gz == 0, 1.0, 0.0)
    last = jnp.where(gz == planes - 1, 1.0, 0.0)
    odd = gz % 2
    slopes_at = lambda cells: [ready[i, :, cells] for i in range(7)]
    totals = (earlier, stress_lines(slopes_at, other, plane, table, lines))
    parts = []
    for k in range(2):
        sign = jnp.where(odd == k, 1.0, -1.0)
        pieces = [totals[k][rows * i : rows * (i + 1)] for i in range(7)]
        for i in range(3):
            start = 3 * PAD_ROWS + 8 * (3 * k + i)
            pieces[i] = jnp.concatenate([pieces[i], spectra[start : start + 8, :]], axis=0)
        t01, p11, t12 = pieces[:3]
        s22, t02, s00, rise = [padded(piece) for piece in pieces[3:]]
        p11 = up(p11) + down(p11) - 2.0 * p11
        t01 = up(t01) - down(t01)
        t12 = 0.25 * (up(t12) - down(t12))
        flat = spectra[k * PAD_ROWS : (k + 1) * PAD_ROWS, :]
        s22, rise = sign * s22, sign * rise
        middle = p11 - 2.0 * s22 + 0.5 * (flat + rise)
        middle = middle + slope_of(factors, t01) + factors[1:2] * s00
        cross = sign * (t12 + slope_of(factors, t02))
        parts.append([s22 + cross, middle, s22 - cross])

    ghost = spectra[2 * PAD_ROWS : 3 * PAD_ROWS, :]
    lower = [jnp.where(odd == 1, p, q) for p, q in zip(*parts)]
    upper = [jnp.where(odd == 1, q, p) for p, q in zip(*parts)]
    spectrum = [
        lower[0],
        lower[1] + upper[0] + first * ghost,
        lower[2] + upper[1] + last * ghost,
        upper[2],
    ]
    count = len(spectrum)

    stacked = jnp.concatenate(spectrum, axis=0)
    selected = matmul(jnp.concatenate(split(stacked), axis=0), pick[...])
    size = count * PAD_ROWS
    selected = selected[:size] + selected[size:]

    lane = lax.broadcasted_iota(jnp.int32, (PAD_ROWS, 128), 1)
    empty_block = jnp.zeros((PAD_ROWS, 128), jnp.float32)
    sub_lanes = lax.broadcasted_iota(jnp.int32, (8, 128), 0)
    share = 2 * capacity
    for half in range(groups * share // 128):
        pieces = [
            selected[PAD_ROWS * j : PAD_ROWS * (j + 1), 128 * half : 128 * (half + 1)]
            for j in range(count)
        ]
        for place in range(128 // share):
            block = empty_block
            for j in range(count):
                distance = (share * (j - place)) % 128
                moved = pltpu.roll(pieces[j], distance, 1) if distance else pieces[j]
                block = jnp.where(lane // share == j, moved, block)
            largest = jnp.max(jnp.abs(block), axis=0, keepdims=True)
            power = jnp.floor(jnp.log2(jnp.maximum(largest, 1e-30)) * STEPS) + 1.0
            block = jnp.floor(block * (CODES * jnp.exp2(power * (-1.0 / STEPS))) + 0.5)
            rim = pltpu.roll(block[rows:], 2, 0)
            rim = jnp.where(sub_lanes == 0, power, jnp.where(sub_lanes < 3, rim, 0.0))
            base = (half * (128 // share) + place) * (rows + 4)
            codes[base : base + 4, :] = rim[:4]
            codes[base + 4 : base + 4 + rows, :] = block[:rows]
    packed = codes[...].astype(jnp.int32).astype(jnp.int16)
    for side in range(planes):
        out[side * packed.shape[0] : (side + 1) * packed.shape[0], :] = packed


def solve_kernel(kyr, depth, capacity, reach, received, basis, green, out, codes):
    planes = green.shape[1]
    sources = received.shape[0] // reach
    codes[...] = received[...].astype(jnp.int32).astype(jnp.float32)
    power = codes[pl.ds(0, sources, stride=reach), :]
    scale = jnp.exp2(power * (1.0 / STEPS)) * (1.0 / CODES)
    row = lax.broadcasted_iota(jnp.int32, (2 * reach, 128), 0)
    values = []
    for pair in range(0, sources, 2):
        factor = jnp.where(row < reach, scale[pair : pair + 1], scale[pair + 1 : pair + 2])
        values.append(codes[pair * reach : (pair + 2) * reach, :] * factor)
    each = sources // planes // 2
    blocks = [jnp.concatenate(values[i * each : (i + 1) * each], axis=0) for i in range(planes)]
    high, low = split(jnp.concatenate(blocks, axis=1))
    product = matmul(basis[...], high)
    product = product[: 2 * kyr] + product[2 * kyr :] + matmul(basis[: 2 * kyr, :], low)
    cosine = [jnp.zeros((kyr, 128), jnp.float32) for _ in range(depth)]
    sine = [jnp.zeros((kyr, 128), jnp.float32) for _ in range(depth)]
    for block in range(planes):
        lanes = slice(block * 128, (block + 1) * 128)
        for k in range(depth):
            cosine[k] = cosine[k] + green[k, block] * product[:kyr, lanes]
            sine[k] = sine[k] + green[k, block] * product[kyr:, lanes]
    lane = lax.broadcasted_iota(jnp.int32, (kyr, 128), 1)
    share = 2 * capacity

    def gathered(fields):
        fields = [field + pltpu.roll(field, 64, 1) for field in fields]
        field = jnp.where(lane < 64, fields[0], fields[1])
        return field + pltpu.roll(field, share, 1)

    turned = gathered(sine)
    turned = jnp.where(lane % 2 == 0, pltpu.roll(turned, 127, 1), -pltpu.roll(turned, 1, 1))
    result = gathered(cosine) + turned
    flipped = result.T
    for k in range(depth):
        out[:, k, :] = flipped[64 * k + share : 64 * k + 2 * share]


def exchange(array, axis, size, shifted):
    pairs = [(i, i + 1) for i in range(shifted, size - 1, 2)]
    return lax.ppermute(array, axis, pairs + [(j, i) for i, j in pairs])


def in_hbm(array):
    return pltpu.with_memory_space_constraint(array, pltpu.HBM)


def per_device(groups, planes, velocity_x, velocity_y, velocity_z, owners, below, above, metric):
    depth, rows, width = velocity_x.shape
    kxr = owners.shape[0]
    kyr = 2 * kxr
    levels = below.shape[0]
    limit = pltpu.CompilerParams(vmem_limit_bytes=32 * 1024 * 1024)
    fields = (velocity_x, velocity_y, velocity_z)

    plane_shape = jax.ShapeDtypeStruct((3, rows, width), jnp.bfloat16)
    row_shape = jax.ShapeDtypeStruct((8, width), jnp.bfloat16)
    own_one, own_two, row_one, row_two, owners, columns = pl.pallas_call(
        pack_kernel,
        out_shape=(plane_shape, plane_shape, row_shape, row_shape)
        + (
            jax.ShapeDtypeStruct((1, kxr), jnp.int32),
            jax.ShapeDtypeStruct((3 * levels, 128), jnp.float32),
        ),
        in_specs=[HBM] * 7,
        out_specs=(VMEM,) * 6,
        scratch_shapes=[
            pltpu.SMEM((3, levels), jnp.float32),
            pltpu.SemaphoreType.DMA((3, 2)),
            pltpu.SemaphoreType.DMA((4,)),
        ],
        compiler_params=limit,
    )(*[in_hbm(array) for array in (*fields, owners.reshape(1, kxr), below, above, metric)])
    plane_one = exchange(own_one, "gz", planes, 0)
    plane_two = exchange(own_two, "gz", planes, 1)
    row_one = exchange(row_one, "gy", groups, 0)
    row_two = exchange(row_two, "gy", groups, 1)

    table, factors = [jnp.asarray(array) for array in x_tables(width, kxr, rows * groups)]
    pick, green, table, factors = pl.pallas_call(
        functools.partial(mode_kernel, groups, CAP, kyr, levels, depth),
        out_shape=(
            jax.ShapeDtypeStruct((2 * kxr, groups * CAP * 2), jnp.bfloat16),
            jax.ShapeDtypeStruct((depth, planes, kyr, 128), jnp.float32),
            jax.ShapeDtypeStruct(table.shape, table.dtype),
            jax.ShapeDtypeStruct(factors.shape, factors.dtype),
        ),
        in_specs=[VMEM, VMEM, HBM, HBM],
        out_specs=(VMEM,) * 4,
        scratch_shapes=[pltpu.SemaphoreType.DMA((5,))],
        compiler_params=limit,
    )(owners, columns, in_hbm(table), in_hbm(factors))

    strain, spectra = pl.pallas_call(
        functools.partial(early_kernel, groups, planes),
        out_shape=(
            jax.ShapeDtypeStruct((depth, 5, rows, width), jnp.float32),
            jax.ShapeDtypeStruct((3 * PAD_ROWS + 6 * 8, 2 * kxr), jnp.float32),
        ),
        in_specs=[VMEM] * 4,
        out_specs=(VMEM,) * 2,
        scratch_shapes=[pltpu.VMEM((2, PIECES * (5 * rows + 6 * 8), width // 2), jnp.bfloat16)],
        compiler_params=limit,
    )(own_one, own_two, table, factors)

    reach = rows + 4
    held = pltpu.VMEM((2, PIECES * 7 * rows, width // 2), jnp.bfloat16)
    earlier, ready = pl.pallas_call(
        late_kernel,
        out_shape=(
            jax.ShapeDtypeStruct((7 * rows, 2 * kxr), jnp.float32),
            jax.ShapeDtypeStruct((7, rows, width), jnp.float32),
        ),
        in_specs=[VMEM] * 6,
        out_specs=(VMEM,) * 2,
        scratch_shapes=[held],
        compiler_params=limit,
    )(own_two, plane_one, row_one, row_two, strain, table)
    outgoing = pl.pallas_call(
        functools.partial(last_kernel, planes, groups, CAP),
        out_shape=jax.ShapeDtypeStruct((planes * groups * reach, 128), jnp.int16),
        in_specs=[VMEM] * 8,
        out_specs=VMEM,
        scratch_shapes=[held, pltpu.VMEM((groups * reach, 128), jnp.float32)],
        compiler_params=limit,
    )(own_one, plane_two, ready, table, earlier, spectra, factors, pick)
    outgoing = outgoing.reshape(planes * groups, reach // 2, 2, 128)
    received = lax.all_to_all(outgoing, ("gz", "gy"), split_axis=0, concat_axis=0, tiled=True)
    received = received.reshape(planes * groups * reach, 128)

    basis = jnp.asarray(y_tables(rows, groups, kyr))
    solved = pl.pallas_call(
        functools.partial(solve_kernel, kyr, depth, CAP, reach),
        out_shape=jax.ShapeDtypeStruct((CAP * 2, depth, kyr), jnp.float32),
        in_specs=[VMEM] * 3,
        out_specs=VMEM,
        scratch_shapes=[pltpu.VMEM(received.shape, jnp.float32)],
        compiler_params=limit,
    )(received, basis, green)
    return solved.reshape(1, CAP, 2, depth, kyr)


def solution(mesh):
    placed = (P("gz", "gy", None), P("gz", "gy", None), P("gz", "gy", None), P(), P(), P(), P())
    return jax.shard_map(
        functools.partial(per_device, mesh.shape["gy"], mesh.shape["gz"]),
        mesh=mesh,
        in_specs=placed,
        out_specs=P("gy", None, None, "gz", None),
        check_vma=False,
    )
```

```python
import functools
import math

import jax
import jax.numpy as jnp
import numpy as np
from jax import lax
from jax.experimental import pallas as pl
from jax.experimental.pallas import tpu as pltpu
from jax.sharding import PartitionSpec as P

CAP = 16
SMAG_COEF = 0.12
STRAIN_FLOOR = 0.01
BASE_SHIFT = 0.004
MODE_SHIFT = 0.02

CHUNK = 256
PAD_ROWS = 24
CODES = 32000.0
STEPS = 32.0
PIECES = 3
VMEM = pl.BlockSpec(memory_space=pltpu.VMEM)
HBM = pl.BlockSpec(memory_space=pltpu.HBM)
SMEM = pl.BlockSpec(memory_space=pltpu.SMEM)


def split(value):
    high = value.astype(jnp.bfloat16)
    low = (value - high.astype(jnp.float32)).astype(jnp.bfloat16)
    return high, low


def split_table(table, parts):
    pieces = []
    for _ in range(parts):
        pieces.append(table.astype(jnp.bfloat16))
        table = table - pieces[-1].astype(np.float64)
    return pieces


def matmul(left, right):
    return jnp.dot(left, right, preferred_element_type=jnp.float32)


def mode_order(place, kxr):
    return 2 * place - (2 * place // kxr) * (kxr - 1)


def x_tables(width, kxr, grid_rows):
    norm = 1.0 / math.sqrt(width * grid_rows)
    modes = mode_order(np.arange(kxr), kxr)
    phase = (np.arange(width // 2)[:, None] * modes[None, :] % width) * (2.0 * np.pi / width)
    table = np.stack([np.cos(phase) * norm, -np.sin(phase) * norm], axis=2)
    table = table.reshape(width // 2, 2, kxr).transpose(1, 0, 2).reshape(width, kxr)
    angle = modes * (2.0 * np.pi / width)
    turn = np.stack([-np.sin(angle), np.sin(angle)], axis=1).reshape(2 * kxr) * 0.5
    second = np.repeat(-4.0 * np.sin(angle * 0.5) ** 2, 2)
    pieces = split_table(table, PIECES) + [np.zeros(table.shape, jnp.bfloat16)]
    return np.concatenate(pieces, axis=1), np.stack([turn, second]).astype(np.float32)


def y_tables(rows, groups, kyr):
    grid_rows = rows * groups
    nowhere = -grid_rows
    offset = np.concatenate([[nowhere, -1, rows, nowhere], np.arange(rows)])
    cells = (np.arange(groups)[:, None] * rows + offset[None, :]).reshape(-1)
    ky = np.arange(kyr) - kyr // 2
    phase = (ky[:, None] * cells[None, :] % grid_rows) * (2.0 * np.pi / grid_rows)
    valid = (cells >= 0) & (cells < grid_rows)
    table = np.concatenate([np.cos(phase), np.sin(phase)], axis=0) * valid[None, :]
    return np.concatenate(split_table(table, 2), axis=0)


def mode_kernel(
    groups, capacity, kyr, levels, depth,
    owners, columns, table_hbm, factors_hbm,
    pick, green, table, factors, arrived,
):
    copies = [pltpu.make_async_copy(factors_hbm, factors, arrived.at[0])]
    share = table.shape[0] // (arrived.shape[0] - 1)
    for i in range(1, arrived.shape[0]):
        at = pl.ds((i - 1) * share, share)
        copies.append(pltpu.make_async_copy(table_hbm.at[at], table.at[at], arrived.at[i]))
    for copy in copies:
        copy.start()
    kxr = owners.shape[1]
    below, above, metric = [
        [columns[i * levels + k : i * levels + k + 1, :] for k in range(levels)] for i in range(3)
    ]
    places, gy = lax.axis_index("gz"), lax.axis_index("gy")
    shape = (2 * kxr, kxr)
    mode = mode_order(lax.broadcasted_iota(jnp.int32, shape, 0) // 2, kxr)
    other = lax.broadcasted_iota(jnp.int32, shape, 1)
    named = owners[...].astype(jnp.float32)
    owner = jnp.sum(jnp.where(mode == other, named, 0.0), axis=1, keepdims=True)
    rank = jnp.sum(
        jnp.where((named == owner) & (other < mode), 1.0, 0.0), axis=1, keepdims=True
    )
    slot = (owner * capacity + rank).astype(jnp.int32)
    part = lax.broadcasted_iota(jnp.int32, (2 * kxr, 1), 0) % 2
    column = lax.broadcasted_iota(jnp.int32, (2 * kxr, groups * capacity * 2), 1)
    chosen = jnp.where(slot * 2 + part == column, 1.0, 0.0)
    if pick.dtype == jnp.bfloat16:
        pick[...] = chosen.astype(jnp.bfloat16)
    else:
        place = lax.broadcasted_iota(jnp.int32, chosen.shape, 0).astype(jnp.float32)
        source = jnp.sum(chosen * place, axis=0, keepdims=True).astype(jnp.int32)
        filled = jnp.sum(chosen, axis=0, keepdims=True).astype(jnp.int32)
        pick[...] = jnp.concatenate([source, filled] + [source * 0] * 6, axis=0)

    lane = lax.broadcasted_iota(jnp.int32, (2 * kxr, 128), 1)
    here = gy * capacity + lane % (2 * capacity) // 2
    owned = (slot == here) & (part == 0)
    mode_id = mode_order(lax.broadcasted_iota(jnp.int32, (2 * kxr, 128), 0) // 2, kxr)
    mode_id = mode_id.astype(jnp.float32)
    kx = jnp.sum(jnp.where(owned, mode_id, 0.0), axis=0, keepdims=True)
    filled = jnp.sum(jnp.where(owned, 1.0, 0.0), axis=0, keepdims=True)

    size = 64
    at = lax.broadcasted_iota(jnp.int32, (size, 128), 1) // (2 * capacity)

    def turn(step, carry):
        start = pl.multiple_of(step * size, size)
        ky = lax.broadcasted_iota(jnp.int32, (size, 128), 0) + (start - kyr // 2)
        ky = ky.astype(jnp.float32)
        radius = kx * kx + ky * ky
        inside = jnp.where(radius <= float(kxr * kxr), filled, 0.0)
        shift = BASE_SHIFT + MODE_SHIFT * (radius / float(kxr * kxr))
        inverse = []
        for k in range(levels):
            pivot = -(below[k] + above[k] + metric[k] * shift)
            if k > 0:
                pivot = pivot - below[k] * above[k - 1] * inverse[-1]
            inverse.append(1.0 / pivot)
        for k in range(depth):
            target = places * depth + k
            forward = []
            for pos in range(levels):
                unit = jnp.where(target == pos, 1.0, 0.0)
                value = inside * unit
                if pos > 0:
                    value = value - above[pos - 1] * inverse[pos - 1] * forward[-1]
                forward.append(value)
            weights = [None] * levels
            for pos in range(levels - 1, -1, -1):
                value = forward[pos]
                if pos < levels - 1:
                    value = value - below[pos + 1] * weights[pos + 1]
                weights[pos] = value * inverse[pos]
            for block in range(levels // depth):
                total = jnp.zeros((size, 128), jnp.float32)
                for j in range(depth + 2):
                    pos = block * depth - 1 + j
                    if 0 <= pos < levels:
                        total = jnp.where(at == j, weights[pos], total)
                green[k, block, pl.ds(start, size), :] = total
        return carry

    lax.fori_loop(0, kyr // size, turn, 0)
    for copy in copies:
        copy.wait()


def pack_kernel(
    vx, vy, vz, owners_hbm, below_hbm, above_hbm, metric_hbm,
    own_one, own_two, row_one, row_two, owners, columns, scalars, arrived, small,
):
    rows = vx.shape[1]
    odd, odd_row = lax.axis_index("gz") % 2, lax.axis_index("gy") % 2
    copies = []
    for i, field in enumerate((vx, vy, vz)):
        for k, plane in enumerate((own_one, own_two)):
            level = odd if k else 1 - odd
            copies.append(pltpu.make_async_copy(field.at[level], plane.at[i], arrived.at[i, k]))
    others = [pltpu.make_async_copy(owners_hbm, owners, small.at[3])]
    for i, array in enumerate((below_hbm, above_hbm, metric_hbm)):
        others.append(pltpu.make_async_copy(array, scalars.at[i], small.at[i]))
    for copy in copies + others:
        copy.start()
    sub = lax.broadcasted_iota(jnp.int32, (8, vx.shape[2]), 0)
    bottom = jnp.zeros((8, vx.shape[2]), jnp.float32)
    top = bottom
    for copy in others:
        copy.wait()
    levels = scalars.shape[1]
    for i in range(3):
        for k in range(levels):
            at = i * levels + k
            columns[at : at + 1, :] = jnp.full((1, 128), scalars[i, k], jnp.float32)
    for i in range(3):
        for k, plane in enumerate((own_one, own_two)):
            copies[2 * i + k].wait()
            field = plane[i].astype(jnp.float32)
            bottom = jnp.where(sub == 2 * i + k, field[0:1], bottom)
            top = jnp.where(sub == 2 * i + k, field[rows - 1 : rows], top)
    row_one[...] = jnp.where(odd_row == 0, top, bottom).astype(jnp.bfloat16)
    row_two[...] = jnp.where(odd_row == 0, bottom, top).astype(jnp.bfloat16)


def up(field):
    return pltpu.roll(field, PAD_ROWS - 1, 0)


def down(field):
    return pltpu.roll(field, 1, 0)


def padded(field):
    empty = jnp.zeros((PAD_ROWS - field.shape[0], field.shape[1]), field.dtype)
    return jnp.concatenate([field, empty], axis=0)


def magnitude(squared):
    return SMAG_COEF * (squared * lax.rsqrt(squared))


def put_lines(lines, step, near, far):
    cells = pl.ds(step * CHUNK, CHUNK)
    count = lines.shape[1] // PIECES
    start = 0
    for one, other in zip(near, far):
        size = one.shape[0]
        for parity, field in enumerate((one + other, one - other)):
            for piece in range(PIECES):
                at = piece * count + start
                part = field.astype(jnp.bfloat16)
                lines[parity, at : at + size, cells] = part
                field = field - part.astype(jnp.float32)
        start += size


def transformed(lines, table):
    count, half = lines.shape[1] // PIECES, lines.shape[2]
    modes = table.shape[1] // (PIECES + 1)
    totals = []
    for parity in range(2):
        product = matmul(lines[parity], table[parity * half : (parity + 1) * half, :])
        total = product[:count, : 2 * modes] + product[:count, 2 * modes :]
        for piece in range(1, PIECES):
            total = total + product[piece * count : (piece + 1) * count, : 2 * modes]
        totals.append(total + pltpu.roll(total, modes, 1))
    lane = lax.broadcasted_iota(jnp.int32, (1, 2 * modes), 1)
    return jnp.where(lane < modes, *totals)


def slope_of(factors, field):
    modes = field.shape[1]
    even = lax.broadcasted_iota(jnp.int32, (1, modes), 1) % 2 == 0
    moved = jnp.where(even, pltpu.roll(field, modes - 1, 1), pltpu.roll(field, 1, 1))
    return factors[0:1] * moved


def early_kernel(
    groups, planes,
    own_one, own_two, table, factors,
    strain, spectra, lines,
):
    rows, width = own_one.shape[1:]
    gz, gy = lax.axis_index("gz"), lax.axis_index("gy")
    first = jnp.where(gz == 0, 1.0, 0.0)
    last = jnp.where(gz == planes - 1, 1.0, 0.0)
    odd = gz % 2
    sub = lax.broadcasted_iota(jnp.int32, (8, CHUNK), 0)
    ghost_rows = jnp.where((sub == 0) & (gy == groups - 1) | (sub == 7) & (gy == 0), 1.0, 0.0)

    def fields_at(step):
        here = step * CHUNK
        before, after = (here - 128) % width, (here + CHUNK) % width
        cells = pl.ds(here, CHUNK)
        flat, rims = [], []
        for k, source in enumerate((own_one, own_two)):
            sign = jnp.where(odd == k, 1.0, -1.0)
            own = [source[i, :, cells].astype(jnp.float32) for i in range(3)]
            x, y, rim = [], [], []
            for i in range(3):
                window = jnp.concatenate(
                    [
                        source[i, :, pl.ds(before, 128)].astype(jnp.float32),
                        own[i],
                        source[i, :, pl.ds(after, 128)].astype(jnp.float32),
                    ],
                    axis=1,
                )
                difference = pltpu.roll(window, CHUNK + 255, 1) - pltpu.roll(window, 1, 1)
                x.append(difference[:, 128 : 128 + CHUNK])
                field = padded(own[i])
                difference = up(field) - down(field)
                y.append(difference[:rows])
                rim.append(difference[rows:])
            e01 = y[0] + x[1]
            strain[k, 0, :, cells] = x[0]
            strain[k, 1, :, cells] = y[1]
            strain[k, 2, :, cells] = e01
            strain[k, 3, :, cells] = sign * x[2]
            strain[k, 4, :, cells] = sign * y[2]
            squared = 0.5 * (rim[1] * rim[1]) + 0.25 * (rim[0] * rim[0] + rim[2] * rim[2])
            viscous = ghost_rows * magnitude(squared + STRAIN_FLOOR)
            rims += [viscous * rim[0], viscous * rim[1], viscous * (sign * rim[2])]
            flat.append(x[0] + y[1])

        ghost = [(first - last) * own_two[i, :, cells].astype(jnp.float32) for i in range(3)]
        squared = 0.5 * (ghost[2] * ghost[2])
        squared = squared + 0.25 * (ghost[0] * ghost[0] + ghost[1] * ghost[1])
        viscous = magnitude(squared + STRAIN_FLOOR)
        edge = [viscous * ghost[i] for i in range(3)]
        return flat + edge + [jnp.concatenate(rims, axis=0)]

    steps = width // CHUNK // 2
    for step in range(steps):
        put_lines(lines, step, fields_at(step), fields_at(step + steps))

    total = transformed(lines, table)
    pieces = [padded(total[rows * i : rows * (i + 1)]) for i in range(5)]
    t02, t12, s22 = pieces[2:]
    cross = 0.25 * (up(t12) - down(t12)) + slope_of(factors, t02)
    pieces = pieces[:2] + [s22 + (last - first) * cross]
    for i, piece in enumerate(pieces + [total[5 * rows :]]):
        spectra[PAD_ROWS * i : PAD_ROWS * i + piece.shape[0], :] = piece


def corrected(k, cells, row_one, row_two, strain):
    rows = strain.shape[2]
    odd_row = lax.axis_index("gy") % 2
    sign = jnp.where(lax.axis_index("gz") % 2 == k, 1.0, -1.0)
    row = lax.broadcasted_iota(jnp.int32, (rows, CHUNK), 0)
    ones = row_one[:, cells].astype(jnp.float32)
    twos = row_two[:, cells].astype(jnp.float32)
    lows = jnp.where(odd_row == 0, twos, ones)
    highs = jnp.where(odd_row == 0, ones, twos)

    def beyond(i):
        at = 2 * i + k
        inner = jnp.where(row == 0, -lows[at : at + 1], 0.0)
        return jnp.where(row == rows - 1, highs[at : at + 1], inner)

    x0, sx2 = strain[k, 0, :, cells], strain[k, 3, :, cells]
    edge = beyond(1)
    y1 = strain[k, 1, :, cells] + edge
    e01 = strain[k, 2, :, cells] + beyond(0)
    sy2 = strain[k, 4, :, cells] + sign * beyond(2)
    flat = 0.5 * (x0 * x0 + y1 * y1) + 0.25 * (e01 * e01) + STRAIN_FLOOR
    return x0, y1, e01, sx2, sy2, flat, sign * edge


def stress_lines(slopes_at, other, plane, table, lines):
    def fields_at(step):
        cells = pl.ds(step * CHUNK, CHUNK)
        x0, y1, e01, sx2, sy2, flat, edge = slopes_at(cells)
        z = [
            plane[i, :, cells].astype(jnp.float32) - other[i, :, cells].astype(jnp.float32)
            for i in range(3)
        ]
        e02, e12 = z[0] + sx2, z[1] + sy2
        squared = flat + 0.5 * (z[2] * z[2]) + 0.25 * (e02 * e02 + e12 * e12)
        viscous = magnitude(squared)
        fields = [viscous * field for field in (e01, y1, e12, z[2], e02, x0)]
        return fields + [z[2] + edge]

    steps = plane.shape[2] // CHUNK // 2
    for step in range(steps):
        put_lines(lines, step, fields_at(step), fields_at(step + steps))
    return transformed(lines, table)


def late_kernel(other, plane, row_one, row_two, strain, table, out, ready, lines):
    slopes_at = lambda cells: corrected(0, cells, row_one, row_two, strain)
    out[...] = stress_lines(slopes_at, other, plane, table, lines)
    for step in range(plane.shape[2] // CHUNK):
        cells = pl.ds(step * CHUNK, CHUNK)
        for i, field in enumerate(corrected(1, cells, row_one, row_two, strain)):
            ready[i, :, cells] = field


def last_kernel(
    planes, groups, capacity,
    other, plane, ready, table, earlier, spectra, factors, pick,
    out, lines, codes,
):
    rows = other.shape[1]
    gz = lax.axis_index("gz")
    first = jnp.where(gz == 0, 1.0, 0.0)
    last = jnp.where(gz == planes - 1, 1.0, 0.0)
    odd = gz % 2
    slopes_at = lambda cells: [ready[i, :, cells] for i in range(7)]
    totals = (earlier, stress_lines(slopes_at, other, plane, table, lines))
    parts = []
    for k in range(2):
        sign = jnp.where(odd == k, 1.0, -1.0)
        pieces = [totals[k][rows * i : rows * (i + 1)] for i in range(7)]
        for i in range(3):
            start = 3 * PAD_ROWS + 8 * (3 * k + i)
            pieces[i] = jnp.concatenate([pieces[i], spectra[start : start + 8, :]], axis=0)
        t01, p11, t12 = pieces[:3]
        s22, t02, s00, rise = [padded(piece) for piece in pieces[3:]]
        p11 = up(p11) + down(p11) - 2.0 * p11
        t01 = up(t01) - down(t01)
        t12 = 0.25 * (up(t12) - down(t12))
        flat = spectra[k * PAD_ROWS : (k + 1) * PAD_ROWS, :]
        s22, rise = sign * s22, sign * rise
        middle = p11 - 2.0 * s22 + 0.5 * (flat + rise)
        middle = middle + slope_of(factors, t01) + factors[1:2] * s00
        cross = sign * (t12 + slope_of(factors, t02))
        parts.append([s22 + cross, middle, s22 - cross])

    ghost = spectra[2 * PAD_ROWS : 3 * PAD_ROWS, :]
    lower = [jnp.where(odd == 1, p, q) for p, q in zip(*parts)]
    upper = [jnp.where(odd == 1, q, p) for p, q in zip(*parts)]
    spectrum = [
        lower[0],
        lower[1] + upper[0] + first * ghost,
        lower[2] + upper[1] + last * ghost,
        upper[2],
    ]
    count = len(spectrum)

    stacked = jnp.concatenate(spectrum, axis=0)
    if pick.dtype == jnp.bfloat16:
        selected = matmul(jnp.concatenate(split(stacked), axis=0), pick[...])
        size = count * PAD_ROWS
        selected = selected[:size] + selected[size:]
    else:
        halves = []
        for start in range(0, pick.shape[1], 128):
            source = jnp.broadcast_to(pick[0:1, start : start + 128], stacked.shape)
            taken = jnp.take_along_axis(stacked, source, axis=1)
            halves.append(jnp.where(pick[1:2, start : start + 128] > 0, taken, 0.0))
        selected = jnp.concatenate(halves, axis=1)

    lane = lax.broadcasted_iota(jnp.int32, (PAD_ROWS, 128), 1)
    empty_block = jnp.zeros((PAD_ROWS, 128), jnp.float32)
    sub_lanes = lax.broadcasted_iota(jnp.int32, (8, 128), 0)
    share = 2 * capacity
    for half in range(groups * share // 128):
        pieces = [
            selected[PAD_ROWS * j : PAD_ROWS * (j + 1), 128 * half : 128 * (half + 1)]
            for j in range(count)
        ]
        for place in range(128 // share):
            block = empty_block
            for j in range(count):
                distance = (share * (j - place)) % 128
                moved = pltpu.roll(pieces[j], distance, 1) if distance else pieces[j]
                block = jnp.where(lane // share == j, moved, block)
            largest = jnp.max(jnp.abs(block), axis=0, keepdims=True)
            power = jnp.floor(jnp.log2(jnp.maximum(largest, 1e-30)) * STEPS) + 1.0
            block = jnp.floor(block * (CODES * jnp.exp2(power * (-1.0 / STEPS))) + 0.5)
            rim = pltpu.roll(block[rows:], 2, 0)
            rim = jnp.where(sub_lanes == 0, power, jnp.where(sub_lanes < 3, rim, 0.0))
            base = (half * (128 // share) + place) * (rows + 4)
            codes[base : base + 4, :] = rim[:4]
            codes[base + 4 : base + 4 + rows, :] = block[:rows]
    packed = codes[...].astype(jnp.int32).astype(jnp.int16)
    for side in range(planes):
        out[side * packed.shape[0] : (side + 1) * packed.shape[0], :] = packed


def solve_kernel(kyr, depth, capacity, reach, received, basis, green, out, codes):
    planes = green.shape[1]
    sources = received.shape[0] // reach
    codes[...] = received[...].astype(jnp.int32).astype(jnp.float32)
    power = codes[pl.ds(0, sources, stride=reach), :]
    scale = jnp.exp2(power * (1.0 / STEPS)) * (1.0 / CODES)
    row = lax.broadcasted_iota(jnp.int32, (2 * reach, 128), 0)
    values = []
    for pair in range(0, sources, 2):
        factor = jnp.where(row < reach, scale[pair : pair + 1], scale[pair + 1 : pair + 2])
        values.append(codes[pair * reach : (pair + 2) * reach, :] * factor)
    each = sources // planes // 2
    blocks = [jnp.concatenate(values[i * each : (i + 1) * each], axis=0) for i in range(planes)]
    high, low = split(jnp.concatenate(blocks, axis=1))
    product = matmul(basis[...], high)
    product = product[: 2 * kyr] + product[2 * kyr :] + matmul(basis[: 2 * kyr, :], low)
    cosine = [jnp.zeros((kyr, 128), jnp.float32) for _ in range(depth)]
    sine = [jnp.zeros((kyr, 128), jnp.float32) for _ in range(depth)]
    for block in range(planes):
        lanes = slice(block * 128, (block + 1) * 128)
        for k in range(depth):
            cosine[k] = cosine[k] + green[k, block] * product[:kyr, lanes]
            sine[k] = sine[k] + green[k, block] * product[kyr:, lanes]
    lane = lax.broadcasted_iota(jnp.int32, (kyr, 128), 1)
    share = 2 * capacity

    def gathered(fields):
        fields = [field + pltpu.roll(field, 64, 1) for field in fields]
        field = jnp.where(lane < 64, fields[0], fields[1])
        return field + pltpu.roll(field, share, 1)

    turned = gathered(sine)
    turned = jnp.where(lane % 2 == 0, pltpu.roll(turned, 127, 1), -pltpu.roll(turned, 1, 1))
    result = gathered(cosine) + turned
    flipped = result.T
    for k in range(depth):
        out[:, k, :] = flipped[64 * k + share : 64 * k + 2 * share]


def exchange(array, axis, size, shifted):
    pairs = [(i, i + 1) for i in range(shifted, size - 1, 2)]
    return lax.ppermute(array, axis, pairs + [(j, i) for i, j in pairs])


def in_hbm(array):
    return pltpu.with_memory_space_constraint(array, pltpu.HBM)


def per_device(groups, planes, velocity_x, velocity_y, velocity_z, owners, below, above, metric):
    depth, rows, width = velocity_x.shape
    kxr = owners.shape[0]
    kyr = 2 * kxr
    levels = below.shape[0]
    limit = pltpu.CompilerParams(vmem_limit_bytes=32 * 1024 * 1024)
    fields = (velocity_x, velocity_y, velocity_z)

    plane_shape = jax.ShapeDtypeStruct((3, rows, width), jnp.bfloat16)
    row_shape = jax.ShapeDtypeStruct((8, width), jnp.bfloat16)
    own_one, own_two, row_one, row_two, owners, columns = pl.pallas_call(
        pack_kernel,
        out_shape=(plane_shape, plane_shape, row_shape, row_shape)
        + (
            jax.ShapeDtypeStruct((1, kxr), jnp.int32),
            jax.ShapeDtypeStruct((3 * levels, 128), jnp.float32),
        ),
        in_specs=[HBM] * 7,
        out_specs=(VMEM,) * 6,
        scratch_shapes=[
            pltpu.SMEM((3, levels), jnp.float32),
            pltpu.SemaphoreType.DMA((3, 2)),
            pltpu.SemaphoreType.DMA((4,)),
        ],
        compiler_params=limit,
    )(*[in_hbm(array) for array in (*fields, owners.reshape(1, kxr), below, above, metric)])
    plane_one = exchange(own_one, "gz", planes, 0)
    plane_two = exchange(own_two, "gz", planes, 1)
    row_one = exchange(row_one, "gy", groups, 0)
    row_two = exchange(row_two, "gy", groups, 1)

    table, factors = [jnp.asarray(array) for array in x_tables(width, kxr, rows * groups)]
    if 2 * kxr == 128:
        pick_shape = jax.ShapeDtypeStruct((8, groups * CAP * 2), jnp.int32)
    else:
        pick_shape = jax.ShapeDtypeStruct((2 * kxr, groups * CAP * 2), jnp.bfloat16)
    pick, green, table, factors = pl.pallas_call(
        functools.partial(mode_kernel, groups, CAP, kyr, levels, depth),
        out_shape=(
            pick_shape,
            jax.ShapeDtypeStruct((depth, planes, kyr, 128), jnp.float32),
            jax.ShapeDtypeStruct(table.shape, table.dtype),
            jax.ShapeDtypeStruct(factors.shape, factors.dtype),
        ),
        in_specs=[VMEM, VMEM, HBM, HBM],
        out_specs=(VMEM,) * 4,
        scratch_shapes=[pltpu.SemaphoreType.DMA((5,))],
        compiler_params=limit,
    )(owners, columns, in_hbm(table), in_hbm(factors))

    strain, spectra = pl.pallas_call(
        functools.partial(early_kernel, groups, planes),
        out_shape=(
            jax.ShapeDtypeStruct((depth, 5, rows, width), jnp.float32),
            jax.ShapeDtypeStruct((3 * PAD_ROWS + 6 * 8, 2 * kxr), jnp.float32),
        ),
        in_specs=[VMEM] * 4,
        out_specs=(VMEM,) * 2,
        scratch_shapes=[pltpu.VMEM((2, PIECES * (5 * rows + 6 * 8), width // 2), jnp.bfloat16)],
        compiler_params=limit,
    )(own_one, own_two, table, factors)

    reach = rows + 4
    held = pltpu.VMEM((2, PIECES * 7 * rows, width // 2), jnp.bfloat16)
    earlier, ready = pl.pallas_call(
        late_kernel,
        out_shape=(
            jax.ShapeDtypeStruct((7 * rows, 2 * kxr), jnp.float32),
            jax.ShapeDtypeStruct((7, rows, width), jnp.float32),
        ),
        in_specs=[VMEM] * 6,
        out_specs=(VMEM,) * 2,
        scratch_shapes=[held],
        compiler_params=limit,
    )(own_two, plane_one, row_one, row_two, strain, table)
    outgoing = pl.pallas_call(
        functools.partial(last_kernel, planes, groups, CAP),
        out_shape=jax.ShapeDtypeStruct((planes * groups * reach, 128), jnp.int16),
        in_specs=[VMEM] * 8,
        out_specs=VMEM,
        scratch_shapes=[held, pltpu.VMEM((groups * reach, 128), jnp.float32)],
        compiler_params=limit,
    )(own_one, plane_two, ready, table, earlier, spectra, factors, pick)
    outgoing = outgoing.reshape(planes * groups, reach // 2, 2, 128)
    received = lax.all_to_all(outgoing, ("gz", "gy"), split_axis=0, concat_axis=0, tiled=True)
    received = received.reshape(planes * groups * reach, 128)

    basis = jnp.asarray(y_tables(rows, groups, kyr))
    solved = pl.pallas_call(
        functools.partial(solve_kernel, kyr, depth, CAP, reach),
        out_shape=jax.ShapeDtypeStruct((CAP * 2, depth, kyr), jnp.float32),
        in_specs=[VMEM] * 3,
        out_specs=VMEM,
        scratch_shapes=[pltpu.VMEM(received.shape, jnp.float32)],
        compiler_params=limit,
    )(received, basis, green)
    return solved.reshape(1, CAP, 2, depth, kyr)


def solution(mesh):
    placed = (P("gz", "gy", None), P("gz", "gy", None), P("gz", "gy", None), P(), P(), P(), P())
    return jax.shard_map(
        functools.partial(per_device, mesh.shape["gy"], mesh.shape["gz"]),
        mesh=mesh,
        in_specs=placed,
        out_specs=P("gy", None, None, "gz", None),
        check_vma=False,
    )
```

```python
import functools
import math

import jax
import jax.numpy as jnp
import numpy as np
from jax import lax
from jax.experimental import pallas as pl
from jax.experimental.pallas import tpu as pltpu
from jax.sharding import PartitionSpec as P

CAP = 16
SMAG_COEF = 0.12
STRAIN_FLOOR = 0.01
BASE_SHIFT = 0.004
MODE_SHIFT = 0.02

CHUNK = 256
PAD_ROWS = 24
CODES = 32000.0
STEPS = 32.0
PIECES = 3
VMEM = pl.BlockSpec(memory_space=pltpu.VMEM)
HBM = pl.BlockSpec(memory_space=pltpu.HBM)
SMEM = pl.BlockSpec(memory_space=pltpu.SMEM)


def split(value):
    high = value.astype(jnp.bfloat16)
    low = (value - high.astype(jnp.float32)).astype(jnp.bfloat16)
    return high, low


def split_table(table, parts):
    pieces = []
    for _ in range(parts):
        pieces.append(table.astype(jnp.bfloat16))
        table = table - pieces[-1].astype(np.float64)
    return pieces


def matmul(left, right):
    return jnp.dot(left, right, preferred_element_type=jnp.float32)


def mode_order(place, kxr):
    return 2 * place - (2 * place // kxr) * (kxr - 1)


def x_tables(width, kxr, grid_rows):
    norm = 1.0 / math.sqrt(width * grid_rows)
    modes = mode_order(np.arange(kxr), kxr)
    phase = (np.arange(width // 2)[:, None] * modes[None, :] % width) * (2.0 * np.pi / width)
    table = np.stack([np.cos(phase) * norm, -np.sin(phase) * norm], axis=2)
    table = table.reshape(width // 2, 2, kxr).transpose(1, 0, 2).reshape(width, kxr)
    angle = modes * (2.0 * np.pi / width)
    turn = np.stack([-np.sin(angle), np.sin(angle)], axis=1).reshape(2 * kxr) * 0.5
    second = np.repeat(-4.0 * np.sin(angle * 0.5) ** 2, 2)
    pieces = split_table(table, PIECES) + [np.zeros(table.shape, jnp.bfloat16)]
    return np.concatenate(pieces, axis=1), np.stack([turn, second]).astype(np.float32)


def y_tables(rows, groups, kyr):
    grid_rows = rows * groups
    nowhere = -grid_rows
    offset = np.concatenate([[nowhere, -1, rows, nowhere], np.arange(rows)])
    cells = (np.arange(groups)[:, None] * rows + offset[None, :]).reshape(-1)
    ky = np.arange(kyr) - kyr // 2
    phase = (ky[:, None] * cells[None, :] % grid_rows) * (2.0 * np.pi / grid_rows)
    valid = (cells >= 0) & (cells < grid_rows)
    table = np.concatenate([np.cos(phase), np.sin(phase)], axis=0) * valid[None, :]
    return np.concatenate(split_table(table, 2), axis=0)


def mode_kernel(
    groups, capacity, kyr, levels, depth,
    owners_hbm, below_hbm, above_hbm, metric_hbm, table_hbm, factors_hbm,
    pick, green, table, factors, owners, scalars, arrived, small,
):
    copies = [pltpu.make_async_copy(factors_hbm, factors, arrived.at[0])]
    share = table.shape[0] // (arrived.shape[0] - 1)
    for i in range(1, arrived.shape[0]):
        at = pl.ds((i - 1) * share, share)
        copies.append(pltpu.make_async_copy(table_hbm.at[at], table.at[at], arrived.at[i]))
    others = [pltpu.make_async_copy(owners_hbm, owners, small.at[3])]
    for i, array in enumerate((below_hbm, above_hbm, metric_hbm)):
        others.append(pltpu.make_async_copy(array, scalars.at[i], small.at[i]))
    for copy in others + copies:
        copy.start()
    for copy in others:
        copy.wait()
    kxr = owners.shape[1]
    below, above, metric = [[scalars[i, k] for k in range(levels)] for i in range(3)]
    places, gy = lax.axis_index("gz"), lax.axis_index("gy")
    shape = (2 * kxr, kxr)
    mode = mode_order(lax.broadcasted_iota(jnp.int32, shape, 0) // 2, kxr)
    other = lax.broadcasted_iota(jnp.int32, shape, 1)
    named = owners[...].astype(jnp.float32)
    owner = jnp.sum(jnp.where(mode == other, named, 0.0), axis=1, keepdims=True)
    rank = jnp.sum(
        jnp.where((named == owner) & (other < mode), 1.0, 0.0), axis=1, keepdims=True
    )
    slot = (owner * capacity + rank).astype(jnp.int32)
    part = lax.broadcasted_iota(jnp.int32, (2 * kxr, 1), 0) % 2
    column = lax.broadcasted_iota(jnp.int32, (2 * kxr, groups * capacity * 2), 1)
    chosen = jnp.where(slot * 2 + part == column, 1.0, 0.0)
    if pick.dtype == jnp.bfloat16:
        pick[...] = chosen.astype(jnp.bfloat16)
    else:
        place = lax.broadcasted_iota(jnp.int32, chosen.shape, 0).astype(jnp.float32)
        source = jnp.sum(chosen * place, axis=0, keepdims=True).astype(jnp.int32)
        filled = jnp.sum(chosen, axis=0, keepdims=True).astype(jnp.int32)
        pick[...] = jnp.concatenate([source, filled] + [source * 0] * 6, axis=0)

    lane = lax.broadcasted_iota(jnp.int32, (2 * kxr, 128), 1)
    here = gy * capacity + lane % (2 * capacity) // 2
    owned = (slot == here) & (part == 0)
    mode_id = mode_order(lax.broadcasted_iota(jnp.int32, (2 * kxr, 128), 0) // 2, kxr)
    mode_id = mode_id.astype(jnp.float32)
    kx = jnp.sum(jnp.where(owned, mode_id, 0.0), axis=0, keepdims=True)
    filled = jnp.sum(jnp.where(owned, 1.0, 0.0), axis=0, keepdims=True)

    size = 64
    at = lax.broadcasted_iota(jnp.int32, (size, 128), 1) // (2 * capacity)

    def turn(step, carry):
        start = pl.multiple_of(step * size, size)
        ky = lax.broadcasted_iota(jnp.int32, (size, 128), 0) + (start - kyr // 2)
        ky = ky.astype(jnp.float32)
        radius = kx * kx + ky * ky
        inside = jnp.where(radius <= float(kxr * kxr), filled, 0.0)
        shift = BASE_SHIFT + MODE_SHIFT * (radius / float(kxr * kxr))
        inverse = []
        for k in range(levels):
            pivot = -(below[k] + above[k] + metric[k] * shift)
            if k > 0:
                pivot = pivot - below[k] * above[k - 1] * inverse[-1]
            inverse.append(1.0 / pivot)
        for k in range(depth):
            target = places * depth + k
            forward = []
            for pos in range(levels):
                unit = jnp.where(target == pos, 1.0, 0.0)
                value = inside * unit
                if pos > 0:
                    value = value - above[pos - 1] * inverse[pos - 1] * forward[-1]
                forward.append(value)
            weights = [None] * levels
            for pos in range(levels - 1, -1, -1):
                value = forward[pos]
                if pos < levels - 1:
                    value = value - below[pos + 1] * weights[pos + 1]
                weights[pos] = value * inverse[pos]
            for block in range(levels // depth):
                total = jnp.zeros((size, 128), jnp.float32)
                for j in range(depth + 2):
                    pos = block * depth - 1 + j
                    if 0 <= pos < levels:
                        total = jnp.where(at == j, weights[pos], total)
                green[k, block, pl.ds(start, size), :] = total
        return carry

    lax.fori_loop(0, kyr // size, turn, 0)
    for copy in copies:
        copy.wait()


def pack_kernel(vx, vy, vz, own_one, own_two, arrived):
    odd = lax.axis_index("gz") % 2
    copies = []
    for k, plane in enumerate((own_one, own_two)):
        for i, field in enumerate((vx, vy, vz)):
            level = odd if k else 1 - odd
            copies.append(pltpu.make_async_copy(field.at[level], plane.at[i], arrived.at[i, k]))
    for copy in copies:
        copy.start()
    for copy in copies:
        copy.wait()


def row_kernel(own_one, own_two, row_one, row_two):
    rows, width = own_one.shape[1:]
    odd_row = lax.axis_index("gy") % 2
    sub = lax.broadcasted_iota(jnp.int32, (8, width), 0)
    bottom = jnp.zeros((8, width), jnp.float32)
    top = bottom
    for i in range(3):
        for k, plane in enumerate((own_one, own_two)):
            field = plane[i].astype(jnp.float32)
            bottom = jnp.where(sub == 2 * i + k, field[0:1], bottom)
            top = jnp.where(sub == 2 * i + k, field[rows - 1 : rows], top)
    row_one[...] = jnp.where(odd_row == 0, top, bottom).astype(jnp.bfloat16)
    row_two[...] = jnp.where(odd_row == 0, bottom, top).astype(jnp.bfloat16)


def up(field):
    return pltpu.roll(field, PAD_ROWS - 1, 0)


def down(field):
    return pltpu.roll(field, 1, 0)


def padded(field):
    empty = jnp.zeros((PAD_ROWS - field.shape[0], field.shape[1]), field.dtype)
    return jnp.concatenate([field, empty], axis=0)


def magnitude(squared):
    return SMAG_COEF * (squared * lax.rsqrt(squared))


def put_lines(lines, step, near, far):
    cells = pl.ds(step * CHUNK, CHUNK)
    count = lines.shape[1] // PIECES
    start = 0
    for one, other in zip(near, far):
        size = one.shape[0]
        for parity, field in enumerate((one + other, one - other)):
            for piece in range(PIECES):
                at = piece * count + start
                part = field.astype(jnp.bfloat16)
                lines[parity, at : at + size, cells] = part
                field = field - part.astype(jnp.float32)
        start += size


def transformed(lines, table):
    count, half = lines.shape[1] // PIECES, lines.shape[2]
    modes = table.shape[1] // (PIECES + 1)
    totals = []
    for parity in range(2):
        product = matmul(lines[parity], table[parity * half : (parity + 1) * half, :])
        total = product[:count, : 2 * modes] + product[:count, 2 * modes :]
        for piece in range(1, PIECES):
            total = total + product[piece * count : (piece + 1) * count, : 2 * modes]
        totals.append(total + pltpu.roll(total, modes, 1))
    lane = lax.broadcasted_iota(jnp.int32, (1, 2 * modes), 1)
    return jnp.where(lane < modes, *totals)


def slope_of(factors, field):
    modes = field.shape[1]
    even = lax.broadcasted_iota(jnp.int32, (1, modes), 1) % 2 == 0
    moved = jnp.where(even, pltpu.roll(field, modes - 1, 1), pltpu.roll(field, 1, 1))
    return factors[0:1] * moved


def early_kernel(
    groups, planes,
    own_one, own_two, table, factors,
    strain, spectra, lines,
):
    rows, width = own_one.shape[1:]
    gz, gy = lax.axis_index("gz"), lax.axis_index("gy")
    first = jnp.where(gz == 0, 1.0, 0.0)
    last = jnp.where(gz == planes - 1, 1.0, 0.0)
    odd = gz % 2
    sub = lax.broadcasted_iota(jnp.int32, (8, CHUNK), 0)
    ghost_rows = jnp.where((sub == 0) & (gy == groups - 1) | (sub == 7) & (gy == 0), 1.0, 0.0)

    def fields_at(step):
        here = step * CHUNK
        before, after = (here - 128) % width, (here + CHUNK) % width
        cells = pl.ds(here, CHUNK)
        flat, rims = [], []
        for k, source in enumerate((own_one, own_two)):
            sign = jnp.where(odd == k, 1.0, -1.0)
            own = [source[i, :, cells].astype(jnp.float32) for i in range(3)]
            x, y, rim = [], [], []
            for i in range(3):
                window = jnp.concatenate(
                    [
                        source[i, :, pl.ds(before, 128)].astype(jnp.float32),
                        own[i],
                        source[i, :, pl.ds(after, 128)].astype(jnp.float32),
                    ],
                    axis=1,
                )
                difference = pltpu.roll(window, CHUNK + 255, 1) - pltpu.roll(window, 1, 1)
                x.append(difference[:, 128 : 128 + CHUNK])
                field = padded(own[i])
                difference = up(field) - down(field)
                y.append(difference[:rows])
                rim.append(difference[rows:])
            e01 = y[0] + x[1]
            strain[k, 0, :, cells] = x[0]
            strain[k, 1, :, cells] = y[1]
            strain[k, 2, :, cells] = e01
            strain[k, 3, :, cells] = sign * x[2]
            strain[k, 4, :, cells] = sign * y[2]
            squared = 0.5 * (rim[1] * rim[1]) + 0.25 * (rim[0] * rim[0] + rim[2] * rim[2])
            viscous = ghost_rows * magnitude(squared + STRAIN_FLOOR)
            rims += [viscous * rim[0], viscous * rim[1], viscous * (sign * rim[2])]
            flat.append(x[0] + y[1])

        ghost = [(first - last) * own_two[i, :, cells].astype(jnp.float32) for i in range(3)]
        squared = 0.5 * (ghost[2] * ghost[2])
        squared = squared + 0.25 * (ghost[0] * ghost[0] + ghost[1] * ghost[1])
        viscous = magnitude(squared + STRAIN_FLOOR)
        edge = [viscous * ghost[i] for i in range(3)]
        return flat + edge + [jnp.concatenate(rims, axis=0)]

    steps = width // CHUNK // 2
    for step in range(steps):
        put_lines(lines, step, fields_at(step), fields_at(step + steps))

    total = transformed(lines, table)
    pieces = [padded(total[rows * i : rows * (i + 1)]) for i in range(5)]
    t02, t12, s22 = pieces[2:]
    cross = 0.25 * (up(t12) - down(t12)) + slope_of(factors, t02)
    pieces = pieces[:2] + [s22 + (last - first) * cross]
    for i, piece in enumerate(pieces + [total[5 * rows :]]):
        spectra[PAD_ROWS * i : PAD_ROWS * i + piece.shape[0], :] = piece


def corrected(k, cells, row_one, row_two, strain):
    rows = strain.shape[2]
    odd_row = lax.axis_index("gy") % 2
    sign = jnp.where(lax.axis_index("gz") % 2 == k, 1.0, -1.0)
    row = lax.broadcasted_iota(jnp.int32, (rows, CHUNK), 0)
    ones = row_one[:, cells].astype(jnp.float32)
    twos = row_two[:, cells].astype(jnp.float32)
    lows = jnp.where(odd_row == 0, twos, ones)
    highs = jnp.where(odd_row == 0, ones, twos)

    def beyond(i):
        at = 2 * i + k
        inner = jnp.where(row == 0, -lows[at : at + 1], 0.0)
        return jnp.where(row == rows - 1, highs[at : at + 1], inner)

    x0, sx2 = strain[k, 0, :, cells], strain[k, 3, :, cells]
    edge = beyond(1)
    y1 = strain[k, 1, :, cells] + edge
    e01 = strain[k, 2, :, cells] + beyond(0)
    sy2 = strain[k, 4, :, cells] + sign * beyond(2)
    flat = 0.5 * (x0 * x0 + y1 * y1) + 0.25 * (e01 * e01) + STRAIN_FLOOR
    return x0, y1, e01, sx2, sy2, flat, sign * edge


def stress_lines(slopes_at, other, plane, table, lines):
    def fields_at(step):
        cells = pl.ds(step * CHUNK, CHUNK)
        x0, y1, e01, sx2, sy2, flat, edge = slopes_at(cells)
        z = [
            plane[i, :, cells].astype(jnp.float32) - other[i, :, cells].astype(jnp.float32)
            for i in range(3)
        ]
        e02, e12 = z[0] + sx2, z[1] + sy2
        squared = flat + 0.5 * (z[2] * z[2]) + 0.25 * (e02 * e02 + e12 * e12)
        viscous = magnitude(squared)
        fields = [viscous * field for field in (e01, y1, e12, z[2], e02, x0)]
        return fields + [z[2] + edge]

    steps = plane.shape[2] // CHUNK // 2
    for step in range(steps):
        put_lines(lines, step, fields_at(step), fields_at(step + steps))
    return transformed(lines, table)


def late_kernel(other, plane, row_one, row_two, strain, table, out, ready, lines):
    slopes_at = lambda cells: corrected(0, cells, row_one, row_two, strain)
    out[...] = stress_lines(slopes_at, other, plane, table, lines)
    for step in range(plane.shape[2] // CHUNK):
        cells = pl.ds(step * CHUNK, CHUNK)
        for i, field in enumerate(corrected(1, cells, row_one, row_two, strain)):
            ready[i, :, cells] = field


def last_kernel(
    planes, groups, capacity,
    other, plane, ready, table, earlier, spectra, factors, pick,
    out, lines, codes,
):
    rows = other.shape[1]
    gz = lax.axis_index("gz")
    first = jnp.where(gz == 0, 1.0, 0.0)
    last = jnp.where(gz == planes - 1, 1.0, 0.0)
    odd = gz % 2
    slopes_at = lambda cells: [ready[i, :, cells] for i in range(7)]
    totals = (earlier, stress_lines(slopes_at, other, plane, table, lines))
    parts = []
    for k in range(2):
        sign = jnp.where(odd == k, 1.0, -1.0)
        pieces = [totals[k][rows * i : rows * (i + 1)] for i in range(7)]
        for i in range(3):
            start = 3 * PAD_ROWS + 8 * (3 * k + i)
            pieces[i] = jnp.concatenate([pieces[i], spectra[start : start + 8, :]], axis=0)
        t01, p11, t12 = pieces[:3]
        s22, t02, s00, rise = [padded(piece) for piece in pieces[3:]]
        p11 = up(p11) + down(p11) - 2.0 * p11
        t01 = up(t01) - down(t01)
        t12 = 0.25 * (up(t12) - down(t12))
        flat = spectra[k * PAD_ROWS : (k + 1) * PAD_ROWS, :]
        s22, rise = sign * s22, sign * rise
        middle = p11 - 2.0 * s22 + 0.5 * (flat + rise)
        middle = middle + slope_of(factors, t01) + factors[1:2] * s00
        cross = sign * (t12 + slope_of(factors, t02))
        parts.append([s22 + cross, middle, s22 - cross])

    ghost = spectra[2 * PAD_ROWS : 3 * PAD_ROWS, :]
    lower = [jnp.where(odd == 1, p, q) for p, q in zip(*parts)]
    upper = [jnp.where(odd == 1, q, p) for p, q in zip(*parts)]
    spectrum = [
        lower[0],
        lower[1] + upper[0] + first * ghost,
        lower[2] + upper[1] + last * ghost,
        upper[2],
    ]
    count = len(spectrum)

    stacked = jnp.concatenate(spectrum, axis=0)
    if pick.dtype == jnp.bfloat16:
        selected = matmul(jnp.concatenate(split(stacked), axis=0), pick[...])
        size = count * PAD_ROWS
        selected = selected[:size] + selected[size:]
    else:
        halves = []
        for start in range(0, pick.shape[1], 128):
            source = jnp.broadcast_to(pick[0:1, start : start + 128], stacked.shape)
            taken = jnp.take_along_axis(stacked, source, axis=1)
            halves.append(jnp.where(pick[1:2, start : start + 128] > 0, taken, 0.0))
        selected = jnp.concatenate(halves, axis=1)

    lane = lax.broadcasted_iota(jnp.int32, (PAD_ROWS, 128), 1)
    empty_block = jnp.zeros((PAD_ROWS, 128), jnp.float32)
    sub_lanes = lax.broadcasted_iota(jnp.int32, (8, 128), 0)
    share = 2 * capacity
    for half in range(groups * share // 128):
        pieces = [
            selected[PAD_ROWS * j : PAD_ROWS * (j + 1), 128 * half : 128 * (half + 1)]
            for j in range(count)
        ]
        for place in range(128 // share):
            block = empty_block
            for j in range(count):
                distance = (share * (j - place)) % 128
                moved = pltpu.roll(pieces[j], distance, 1) if distance else pieces[j]
                block = jnp.where(lane // share == j, moved, block)
            largest = jnp.max(jnp.abs(block), axis=0, keepdims=True)
            power = jnp.floor(jnp.log2(jnp.maximum(largest, 1e-30)) * STEPS) + 1.0
            block = jnp.floor(block * (CODES * jnp.exp2(power * (-1.0 / STEPS))) + 0.5)
            rim = pltpu.roll(block[rows:], 2, 0)
            rim = jnp.where(sub_lanes == 0, power, jnp.where(sub_lanes < 3, rim, 0.0))
            base = (half * (128 // share) + place) * (rows + 4)
            codes[base : base + 4, :] = rim[:4]
            codes[base + 4 : base + 4 + rows, :] = block[:rows]
    packed = codes[...].astype(jnp.int32).astype(jnp.int16)
    for side in range(planes):
        out[side * packed.shape[0] : (side + 1) * packed.shape[0], :] = packed


def solve_kernel(kyr, depth, capacity, reach, received, basis, green, out, codes):
    planes = green.shape[1]
    sources = received.shape[0] // reach
    codes[...] = received[...].astype(jnp.int32).astype(jnp.float32)
    power = codes[pl.ds(0, sources, stride=reach), :]
    scale = jnp.exp2(power * (1.0 / STEPS)) * (1.0 / CODES)
    row = lax.broadcasted_iota(jnp.int32, (2 * reach, 128), 0)
    values = []
    for pair in range(0, sources, 2):
        factor = jnp.where(row < reach, scale[pair : pair + 1], scale[pair + 1 : pair + 2])
        values.append(codes[pair * reach : (pair + 2) * reach, :] * factor)
    each = sources // planes // 2
    blocks = [jnp.concatenate(values[i * each : (i + 1) * each], axis=0) for i in range(planes)]
    high, low = split(jnp.concatenate(blocks, axis=1))
    product = matmul(basis[...], high)
    product = product[: 2 * kyr] + product[2 * kyr :] + matmul(basis[: 2 * kyr, :], low)
    cosine = [jnp.zeros((kyr, 128), jnp.float32) for _ in range(depth)]
    sine = [jnp.zeros((kyr, 128), jnp.float32) for _ in range(depth)]
    for block in range(planes):
        lanes = slice(block * 128, (block + 1) * 128)
        for k in range(depth):
            cosine[k] = cosine[k] + green[k, block] * product[:kyr, lanes]
            sine[k] = sine[k] + green[k, block] * product[kyr:, lanes]
    lane = lax.broadcasted_iota(jnp.int32, (kyr, 128), 1)
    share = 2 * capacity

    def gathered(fields):
        fields = [field + pltpu.roll(field, 64, 1) for field in fields]
        field = jnp.where(lane < 64, fields[0], fields[1])
        return field + pltpu.roll(field, share, 1)

    turned = gathered(sine)
    turned = jnp.where(lane % 2 == 0, pltpu.roll(turned, 127, 1), -pltpu.roll(turned, 1, 1))
    result = gathered(cosine) + turned
    flipped = result.T
    for k in range(depth):
        out[:, k, :] = flipped[64 * k + share : 64 * k + 2 * share]


def exchange(array, axis, size, shifted):
    pairs = [(i, i + 1) for i in range(shifted, size - 1, 2)]
    return lax.ppermute(array, axis, pairs + [(j, i) for i, j in pairs])


def in_hbm(array):
    return pltpu.with_memory_space_constraint(array, pltpu.HBM)


def per_device(groups, planes, velocity_x, velocity_y, velocity_z, owners, below, above, metric):
    depth, rows, width = velocity_x.shape
    kxr = owners.shape[0]
    kyr = 2 * kxr
    levels = below.shape[0]
    limit = pltpu.CompilerParams(vmem_limit_bytes=32 * 1024 * 1024)
    fields = (velocity_x, velocity_y, velocity_z)

    plane_shape = jax.ShapeDtypeStruct((3, rows, width), jnp.bfloat16)
    row_shape = jax.ShapeDtypeStruct((8, width), jnp.bfloat16)
    own_one, own_two = pl.pallas_call(
        pack_kernel,
        out_shape=(plane_shape, plane_shape),
        in_specs=[HBM] * 3,
        out_specs=(VMEM,) * 2,
        scratch_shapes=[pltpu.SemaphoreType.DMA((3, 2))],
        compiler_params=limit,
    )(*[in_hbm(field) for field in fields])
    plane_one = exchange(own_one, "gz", planes, 0)
    plane_two = exchange(own_two, "gz", planes, 1)
    row_one, row_two = pl.pallas_call(
        row_kernel,
        out_shape=(row_shape, row_shape),
        in_specs=[VMEM] * 2,
        out_specs=(VMEM,) * 2,
        compiler_params=limit,
    )(own_one, own_two)
    row_one = exchange(row_one, "gy", groups, 0)
    row_two = exchange(row_two, "gy", groups, 1)

    table, factors = [jnp.asarray(array) for array in x_tables(width, kxr, rows * groups)]
    if 2 * kxr == 128:
        pick_shape = jax.ShapeDtypeStruct((8, groups * CAP * 2), jnp.int32)
    else:
        pick_shape = jax.ShapeDtypeStruct((2 * kxr, groups * CAP * 2), jnp.bfloat16)
    pick, green, table, factors = pl.pallas_call(
        functools.partial(mode_kernel, groups, CAP, kyr, levels, depth),
        out_shape=(
            pick_shape,
            jax.ShapeDtypeStruct((depth, planes, kyr, 128), jnp.float32),
            jax.ShapeDtypeStruct(table.shape, table.dtype),
            jax.ShapeDtypeStruct(factors.shape, factors.dtype),
        ),
        in_specs=[HBM] * 6,
        out_specs=(VMEM,) * 4,
        scratch_shapes=[
            pltpu.VMEM((1, kxr), jnp.int32),
            pltpu.SMEM((3, levels), jnp.float32),
            pltpu.SemaphoreType.DMA((5,)),
            pltpu.SemaphoreType.DMA((4,)),
        ],
        compiler_params=limit,
    )(*map(in_hbm, (owners.reshape(1, kxr), below, above, metric, table, factors)))

    strain, spectra = pl.pallas_call(
        functools.partial(early_kernel, groups, planes),
        out_shape=(
            jax.ShapeDtypeStruct((depth, 5, rows, width), jnp.float32),
            jax.ShapeDtypeStruct((3 * PAD_ROWS + 6 * 8, 2 * kxr), jnp.float32),
        ),
        in_specs=[VMEM] * 4,
        out_specs=(VMEM,) * 2,
        scratch_shapes=[pltpu.VMEM((2, PIECES * (5 * rows + 6 * 8), width // 2), jnp.bfloat16)],
        compiler_params=limit,
    )(own_one, own_two, table, factors)

    reach = rows + 4
    held = pltpu.VMEM((2, PIECES * 7 * rows, width // 2), jnp.bfloat16)
    earlier, ready = pl.pallas_call(
        late_kernel,
        out_shape=(
            jax.ShapeDtypeStruct((7 * rows, 2 * kxr), jnp.float32),
            jax.ShapeDtypeStruct((7, rows, width), jnp.float32),
        ),
        in_specs=[VMEM] * 6,
        out_specs=(VMEM,) * 2,
        scratch_shapes=[held],
        compiler_params=limit,
    )(own_two, plane_one, row_one, row_two, strain, table)
    outgoing = pl.pallas_call(
        functools.partial(last_kernel, planes, groups, CAP),
        out_shape=jax.ShapeDtypeStruct((planes * groups * reach, 128), jnp.int16),
        in_specs=[VMEM] * 8,
        out_specs=VMEM,
        scratch_shapes=[held, pltpu.VMEM((groups * reach, 128), jnp.float32)],
        compiler_params=limit,
    )(own_one, plane_two, ready, table, earlier, spectra, factors, pick)
    outgoing = outgoing.reshape(planes * groups, reach // 2, 2, 128)
    received = lax.all_to_all(outgoing, ("gz", "gy"), split_axis=0, concat_axis=0, tiled=True)
    received = received.reshape(planes * groups * reach, 128)

    basis = jnp.asarray(y_tables(rows, groups, kyr))
    solved = pl.pallas_call(
        functools.partial(solve_kernel, kyr, depth, CAP, reach),
        out_shape=jax.ShapeDtypeStruct((CAP * 2, depth, kyr), jnp.float32),
        in_specs=[VMEM] * 3,
        out_specs=VMEM,
        scratch_shapes=[pltpu.VMEM(received.shape, jnp.float32)],
        compiler_params=limit,
    )(received, basis, green)
    return solved.reshape(1, CAP, 2, depth, kyr)


def solution(mesh):
    placed = (P("gz", "gy", None), P("gz", "gy", None), P("gz", "gy", None), P(), P(), P(), P())
    return jax.shard_map(
        functools.partial(per_device, mesh.shape["gy"], mesh.shape["gz"]),
        mesh=mesh,
        in_specs=placed,
        out_specs=P("gy", None, None, "gz", None),
        check_vma=False,
    )
```

```python
import functools
import math

import jax
import jax.numpy as jnp
import numpy as np
from jax import lax
from jax.experimental import pallas as pl
from jax.experimental.pallas import tpu as pltpu
from jax.sharding import PartitionSpec as P

CAP = 16
SMAG_COEF = 0.12
STRAIN_FLOOR = 0.01
BASE_SHIFT = 0.004
MODE_SHIFT = 0.02

CHUNK = 256
MARGIN = 8
CODES = 32000.0
STEPS = 32.0
PIECES = 3
VMEM = pl.BlockSpec(memory_space=pltpu.VMEM)
HBM = pl.BlockSpec(memory_space=pltpu.HBM)
SMEM = pl.BlockSpec(memory_space=pltpu.SMEM)


def split(value):
    high = value.astype(jnp.bfloat16)
    low = (value - high.astype(jnp.float32)).astype(jnp.bfloat16)
    return high, low


def split_table(table, parts):
    pieces = []
    for _ in range(parts):
        pieces.append(table.astype(jnp.bfloat16))
        table = table - pieces[-1].astype(np.float64)
    return pieces


def matmul(left, right):
    return jnp.dot(left, right, preferred_element_type=jnp.float32)


def mode_order(place, kxr):
    return 2 * place - (2 * place // kxr) * (kxr - 1)


def x_tables(width, kxr, grid_rows):
    norm = 1.0 / math.sqrt(width * grid_rows)
    modes = mode_order(np.arange(kxr), kxr)
    phase = (np.arange(width // 2)[:, None] * modes[None, :] % width) * (2.0 * np.pi / width)
    table = np.stack([np.cos(phase) * norm, -np.sin(phase) * norm], axis=2)
    table = table.reshape(width // 2, 2, kxr).transpose(1, 0, 2).reshape(width, kxr)
    angle = modes * (2.0 * np.pi / width)
    turn = np.stack([-np.sin(angle), np.sin(angle)], axis=1).reshape(2 * kxr) * 0.5
    second = np.repeat(-4.0 * np.sin(angle * 0.5) ** 2, 2)
    pieces = split_table(table, PIECES) + [np.zeros(table.shape, jnp.bfloat16)]
    return np.concatenate(pieces, axis=1), np.stack([turn, second]).astype(np.float32)


def y_tables(rows, groups, kyr):
    grid_rows = rows * groups
    nowhere = -grid_rows
    offset = np.concatenate([[nowhere, -1, rows, nowhere], np.arange(rows)])
    cells = (np.arange(groups)[:, None] * rows + offset[None, :]).reshape(-1)
    ky = np.arange(kyr) - kyr // 2
    phase = (ky[:, None] * cells[None, :] % grid_rows) * (2.0 * np.pi / grid_rows)
    valid = (cells >= 0) & (cells < grid_rows)
    table = np.concatenate([np.cos(phase), np.sin(phase)], axis=0) * valid[None, :]
    return np.concatenate(split_table(table, 2), axis=0)


def mode_kernel(
    groups, capacity, kyr, levels, depth,
    owners_hbm, below_hbm, above_hbm, metric_hbm, table_hbm, factors_hbm,
    pick, green, table, factors, owners, scalars, arrived, small,
):
    copies = [pltpu.make_async_copy(factors_hbm, factors, arrived.at[0])]
    share = table.shape[0] // (arrived.shape[0] - 1)
    for i in range(1, arrived.shape[0]):
        at = pl.ds((i - 1) * share, share)
        copies.append(pltpu.make_async_copy(table_hbm.at[at], table.at[at], arrived.at[i]))
    others = [pltpu.make_async_copy(owners_hbm, owners, small.at[3])]
    for i, array in enumerate((below_hbm, above_hbm, metric_hbm)):
        others.append(pltpu.make_async_copy(array, scalars.at[i], small.at[i]))
    for copy in others + copies:
        copy.start()
    for copy in others:
        copy.wait()
    kxr = owners.shape[1]
    below, above, metric = [[scalars[i, k] for k in range(levels)] for i in range(3)]
    places, gy = lax.axis_index("gz"), lax.axis_index("gy")
    shape = (2 * kxr, kxr)
    mode = mode_order(lax.broadcasted_iota(jnp.int32, shape, 0) // 2, kxr)
    other = lax.broadcasted_iota(jnp.int32, shape, 1)
    named = owners[...].astype(jnp.float32)
    owner = jnp.sum(jnp.where(mode == other, named, 0.0), axis=1, keepdims=True)
    rank = jnp.sum(
        jnp.where((named == owner) & (other < mode), 1.0, 0.0), axis=1, keepdims=True
    )
    slot = (owner * capacity + rank).astype(jnp.int32)
    part = lax.broadcasted_iota(jnp.int32, (2 * kxr, 1), 0) % 2
    column = lax.broadcasted_iota(jnp.int32, (2 * kxr, groups * capacity * 2), 1)
    chosen = jnp.where(slot * 2 + part == column, 1.0, 0.0)
    if pick.dtype == jnp.bfloat16:
        pick[...] = chosen.astype(jnp.bfloat16)
    else:
        place = lax.broadcasted_iota(jnp.int32, chosen.shape, 0).astype(jnp.float32)
        source = jnp.sum(chosen * place, axis=0, keepdims=True).astype(jnp.int32)
        filled = jnp.sum(chosen, axis=0, keepdims=True).astype(jnp.int32)
        pick[...] = jnp.concatenate([source, filled] + [source * 0] * 6, axis=0)

    lane = lax.broadcasted_iota(jnp.int32, (2 * kxr, 128), 1)
    here = gy * capacity + lane % (2 * capacity) // 2
    owned = (slot == here) & (part == 0)
    mode_id = mode_order(lax.broadcasted_iota(jnp.int32, (2 * kxr, 128), 0) // 2, kxr)
    mode_id = mode_id.astype(jnp.float32)
    kx = jnp.sum(jnp.where(owned, mode_id, 0.0), axis=0, keepdims=True)
    filled = jnp.sum(jnp.where(owned, 1.0, 0.0), axis=0, keepdims=True)

    size = 64
    at = lax.broadcasted_iota(jnp.int32, (size, 128), 1) // (2 * capacity)

    def turn(step, carry):
        start = pl.multiple_of(step * size, size)
        ky = lax.broadcasted_iota(jnp.int32, (size, 128), 0) + (start - kyr // 2)
        ky = ky.astype(jnp.float32)
        radius = kx * kx + ky * ky
        inside = jnp.where(radius <= float(kxr * kxr), filled, 0.0)
        shift = BASE_SHIFT + MODE_SHIFT * (radius / float(kxr * kxr))
        inverse = []
        for k in range(levels):
            pivot = -(below[k] + above[k] + metric[k] * shift)
            if k > 0:
                pivot = pivot - below[k] * above[k - 1] * inverse[-1]
            inverse.append(1.0 / pivot)
        for k in range(depth):
            target = places * depth + k
            forward = []
            for pos in range(levels):
                unit = jnp.where(target == pos, 1.0, 0.0)
                value = inside * unit
                if pos > 0:
                    value = value - above[pos - 1] * inverse[pos - 1] * forward[-1]
                forward.append(value)
            weights = [None] * levels
            for pos in range(levels - 1, -1, -1):
                value = forward[pos]
                if pos < levels - 1:
                    value = value - below[pos + 1] * weights[pos + 1]
                weights[pos] = value * inverse[pos]
            for block in range(levels // depth):
                total = jnp.zeros((size, 128), jnp.float32)
                for j in range(depth + 2):
                    pos = block * depth - 1 + j
                    if 0 <= pos < levels:
                        total = jnp.where(at == j, weights[pos], total)
                green[k, block, pl.ds(start, size), :] = total
        return carry

    lax.fori_loop(0, kyr // size, turn, 0)
    for copy in copies:
        copy.wait()


def pack_kernel(vx, vy, vz, own_one, own_two, arrived):
    odd = lax.axis_index("gz") % 2
    copies = []
    for k, plane in enumerate((own_one, own_two)):
        for i, field in enumerate((vx, vy, vz)):
            level = odd if k else 1 - odd
            copies.append(pltpu.make_async_copy(field.at[level], plane.at[i], arrived.at[i, k]))
    for copy in copies:
        copy.start()
    for copy in copies:
        copy.wait()


def row_kernel(own_one, own_two, row_one, row_two):
    rows, width = own_one.shape[1:]
    odd_row = lax.axis_index("gy") % 2
    sub = lax.broadcasted_iota(jnp.int32, (8, width), 0)
    bottom = jnp.zeros((8, width), jnp.float32)
    top = bottom
    for i in range(3):
        for k, plane in enumerate((own_one, own_two)):
            field = plane[i].astype(jnp.float32)
            bottom = jnp.where(sub == 2 * i + k, field[0:1], bottom)
            top = jnp.where(sub == 2 * i + k, field[rows - 1 : rows], top)
    row_one[...] = jnp.where(odd_row == 0, top, bottom).astype(jnp.bfloat16)
    row_two[...] = jnp.where(odd_row == 0, bottom, top).astype(jnp.bfloat16)


def up(field):
    return pltpu.roll(field, field.shape[0] - 1, 0)


def down(field):
    return pltpu.roll(field, 1, 0)


def padded(field):
    empty = jnp.zeros((MARGIN, field.shape[1]), field.dtype)
    return jnp.concatenate([field, empty], axis=0)


def magnitude(squared):
    return SMAG_COEF * (squared * lax.rsqrt(squared))


def put_lines(lines, step, near, far):
    cells = pl.ds(step * CHUNK, CHUNK)
    count = lines.shape[1] // PIECES
    start = 0
    for one, other in zip(near, far):
        size = one.shape[0]
        for parity, field in enumerate((one + other, one - other)):
            for piece in range(PIECES):
                at = piece * count + start
                part = field.astype(jnp.bfloat16)
                lines[parity, at : at + size, cells] = part
                field = field - part.astype(jnp.float32)
        start += size


def transformed(lines, table):
    count, half = lines.shape[1] // PIECES, lines.shape[2]
    modes = table.shape[1] // (PIECES + 1)
    totals = []
    for parity in range(2):
        product = matmul(lines[parity], table[parity * half : (parity + 1) * half, :])
        total = product[:count, : 2 * modes] + product[:count, 2 * modes :]
        for piece in range(1, PIECES):
            total = total + product[piece * count : (piece + 1) * count, : 2 * modes]
        totals.append(total + pltpu.roll(total, modes, 1))
    lane = lax.broadcasted_iota(jnp.int32, (1, 2 * modes), 1)
    return jnp.where(lane < modes, *totals)


def slope_of(factors, field):
    modes = field.shape[1]
    even = lax.broadcasted_iota(jnp.int32, (1, modes), 1) % 2 == 0
    moved = jnp.where(even, pltpu.roll(field, modes - 1, 1), pltpu.roll(field, 1, 1))
    return factors[0:1] * moved


def early_kernel(
    groups, planes,
    own_one, own_two, table, factors,
    strain, spectra, lines,
):
    rows, width = own_one.shape[1:]
    gz, gy = lax.axis_index("gz"), lax.axis_index("gy")
    first = jnp.where(gz == 0, 1.0, 0.0)
    last = jnp.where(gz == planes - 1, 1.0, 0.0)
    odd = gz % 2
    sub = lax.broadcasted_iota(jnp.int32, (8, CHUNK), 0)
    ghost_rows = jnp.where((sub == 0) & (gy == groups - 1) | (sub == 7) & (gy == 0), 1.0, 0.0)

    def fields_at(step):
        here = step * CHUNK
        before, after = (here - 128) % width, (here + CHUNK) % width
        cells = pl.ds(here, CHUNK)
        flat, rims = [], []
        for k, source in enumerate((own_one, own_two)):
            sign = jnp.where(odd == k, 1.0, -1.0)
            own = [source[i, :, cells].astype(jnp.float32) for i in range(3)]
            x, y, rim = [], [], []
            for i in range(3):
                window = jnp.concatenate(
                    [
                        source[i, :, pl.ds(before, 128)].astype(jnp.float32),
                        own[i],
                        source[i, :, pl.ds(after, 128)].astype(jnp.float32),
                    ],
                    axis=1,
                )
                difference = pltpu.roll(window, CHUNK + 255, 1) - pltpu.roll(window, 1, 1)
                x.append(difference[:, 128 : 128 + CHUNK])
                field = padded(own[i])
                difference = up(field) - down(field)
                y.append(difference[:rows])
                rim.append(difference[rows:])
            e01 = y[0] + x[1]
            strain[k, 0, :, cells] = x[0]
            strain[k, 1, :, cells] = y[1]
            strain[k, 2, :, cells] = e01
            strain[k, 3, :, cells] = sign * x[2]
            strain[k, 4, :, cells] = sign * y[2]
            squared = 0.5 * (rim[1] * rim[1]) + 0.25 * (rim[0] * rim[0] + rim[2] * rim[2])
            viscous = ghost_rows * magnitude(squared + STRAIN_FLOOR)
            rims += [viscous * rim[0], viscous * rim[1], viscous * (sign * rim[2])]
            flat.append(x[0] + y[1])

        ghost = [(first - last) * own_two[i, :, cells].astype(jnp.float32) for i in range(3)]
        squared = 0.5 * (ghost[2] * ghost[2])
        squared = squared + 0.25 * (ghost[0] * ghost[0] + ghost[1] * ghost[1])
        viscous = magnitude(squared + STRAIN_FLOOR)
        edge = [viscous * ghost[i] for i in range(3)]
        return flat + edge + [jnp.concatenate(rims, axis=0)]

    steps = width // CHUNK // 2
    for step in range(steps):
        put_lines(lines, step, fields_at(step), fields_at(step + steps))

    total = transformed(lines, table)
    pieces = [padded(total[rows * i : rows * (i + 1)]) for i in range(5)]
    t02, t12, s22 = pieces[2:]
    cross = 0.25 * (up(t12) - down(t12)) + slope_of(factors, t02)
    pieces = pieces[:2] + [s22 + (last - first) * cross]
    for i, piece in enumerate(pieces + [total[5 * rows :]]):
        start = (rows + MARGIN) * i
        spectra[start : start + piece.shape[0], :] = piece


def corrected(k, cells, row_one, row_two, strain):
    rows = strain.shape[2]
    odd_row = lax.axis_index("gy") % 2
    sign = jnp.where(lax.axis_index("gz") % 2 == k, 1.0, -1.0)
    row = lax.broadcasted_iota(jnp.int32, (rows, CHUNK), 0)
    ones = row_one[:, cells].astype(jnp.float32)
    twos = row_two[:, cells].astype(jnp.float32)
    lows = jnp.where(odd_row == 0, twos, ones)
    highs = jnp.where(odd_row == 0, ones, twos)

    def beyond(i):
        at = 2 * i + k
        inner = jnp.where(row == 0, -lows[at : at + 1], 0.0)
        return jnp.where(row == rows - 1, highs[at : at + 1], inner)

    x0, sx2 = strain[k, 0, :, cells], strain[k, 3, :, cells]
    edge = beyond(1)
    y1 = strain[k, 1, :, cells] + edge
    e01 = strain[k, 2, :, cells] + beyond(0)
    sy2 = strain[k, 4, :, cells] + sign * beyond(2)
    flat = 0.5 * (x0 * x0 + y1 * y1) + 0.25 * (e01 * e01) + STRAIN_FLOOR
    return x0, y1, e01, sx2, sy2, flat, sign * edge


def stress_lines(slopes_at, other, plane, table, lines):
    def fields_at(step):
        cells = pl.ds(step * CHUNK, CHUNK)
        x0, y1, e01, sx2, sy2, flat, edge = slopes_at(cells)
        z = [
            plane[i, :, cells].astype(jnp.float32) - other[i, :, cells].astype(jnp.float32)
            for i in range(3)
        ]
        e02, e12 = z[0] + sx2, z[1] + sy2
        squared = flat + 0.5 * (z[2] * z[2]) + 0.25 * (e02 * e02 + e12 * e12)
        viscous = magnitude(squared)
        fields = [viscous * field for field in (e01, y1, e12, z[2], e02, x0)]
        return fields + [z[2] + edge]

    steps = plane.shape[2] // CHUNK // 2
    for step in range(steps):
        put_lines(lines, step, fields_at(step), fields_at(step + steps))
    return transformed(lines, table)


def late_kernel(other, plane, row_one, row_two, strain, table, out, ready, lines):
    slopes_at = lambda cells: corrected(0, cells, row_one, row_two, strain)
    out[...] = stress_lines(slopes_at, other, plane, table, lines)
    for step in range(plane.shape[2] // CHUNK):
        cells = pl.ds(step * CHUNK, CHUNK)
        for i, field in enumerate(corrected(1, cells, row_one, row_two, strain)):
            ready[i, :, cells] = field


def last_kernel(
    planes, groups, capacity,
    other, plane, ready, table, earlier, spectra, factors, pick,
    out, lines, codes,
):
    rows = other.shape[1]
    padded_rows = rows + MARGIN
    gz = lax.axis_index("gz")
    first = jnp.where(gz == 0, 1.0, 0.0)
    last = jnp.where(gz == planes - 1, 1.0, 0.0)
    odd = gz % 2
    slopes_at = lambda cells: [ready[i, :, cells] for i in range(7)]
    totals = (earlier, stress_lines(slopes_at, other, plane, table, lines))
    parts = []
    for k in range(2):
        sign = jnp.where(odd == k, 1.0, -1.0)
        pieces = [totals[k][rows * i : rows * (i + 1)] for i in range(7)]
        for i in range(3):
            start = 3 * padded_rows + MARGIN * (3 * k + i)
            pieces[i] = jnp.concatenate([pieces[i], spectra[start : start + MARGIN, :]], axis=0)
        t01, p11, t12 = pieces[:3]
        s22, t02, s00, rise = [padded(piece) for piece in pieces[3:]]
        p11 = up(p11) + down(p11) - 2.0 * p11
        t01 = up(t01) - down(t01)
        t12 = 0.25 * (up(t12) - down(t12))
        flat = spectra[k * padded_rows : (k + 1) * padded_rows, :]
        s22, rise = sign * s22, sign * rise
        middle = p11 - 2.0 * s22 + 0.5 * (flat + rise)
        middle = middle + slope_of(factors, t01) + factors[1:2] * s00
        cross = sign * (t12 + slope_of(factors, t02))
        parts.append([s22 + cross, middle, s22 - cross])

    ghost = spectra[2 * padded_rows : 3 * padded_rows, :]
    lower = [jnp.where(odd == 1, p, q) for p, q in zip(*parts)]
    upper = [jnp.where(odd == 1, q, p) for p, q in zip(*parts)]
    spectrum = [
        lower[0],
        lower[1] + upper[0] + first * ghost,
        lower[2] + upper[1] + last * ghost,
        upper[2],
    ]
    count = len(spectrum)

    stacked = jnp.concatenate(spectrum, axis=0)
    if pick.dtype == jnp.bfloat16:
        selected = matmul(jnp.concatenate(split(stacked), axis=0), pick[...])
        size = count * padded_rows
        selected = selected[:size] + selected[size:]
    else:
        halves = []
        for start in range(0, pick.shape[1], 128):
            source = jnp.broadcast_to(pick[0:1, start : start + 128], stacked.shape)
            taken = jnp.take_along_axis(stacked, source, axis=1)
            halves.append(jnp.where(pick[1:2, start : start + 128] > 0, taken, 0.0))
        selected = jnp.concatenate(halves, axis=1)

    lane = lax.broadcasted_iota(jnp.int32, (padded_rows, 128), 1)
    empty_block = jnp.zeros((padded_rows, 128), jnp.float32)
    sub_lanes = lax.broadcasted_iota(jnp.int32, (8, 128), 0)
    share = 2 * capacity
    for half in range(groups * share // 128):
        pieces = [
            selected[padded_rows * j : padded_rows * (j + 1), 128 * half : 128 * (half + 1)]
            for j in range(count)
        ]
        for place in range(128 // share):
            block = empty_block
            for j in range(count):
                distance = (share * (j - place)) % 128
                moved = pltpu.roll(pieces[j], distance, 1) if distance else pieces[j]
                block = jnp.where(lane // share == j, moved, block)
            largest = jnp.max(jnp.abs(block), axis=0, keepdims=True)
            power = jnp.floor(jnp.log2(jnp.maximum(largest, 1e-30)) * STEPS) + 1.0
            block = jnp.floor(block * (CODES * jnp.exp2(power * (-1.0 / STEPS))) + 0.5)
            rim = pltpu.roll(block[rows:], 2, 0)
            rim = jnp.where(sub_lanes == 0, power, jnp.where(sub_lanes < 3, rim, 0.0))
            base = (half * (128 // share) + place) * (rows + 4)
            codes[base : base + 4, :] = rim[:4]
            codes[base + 4 : base + 4 + rows, :] = block[:rows]
    packed = codes[...].astype(jnp.int32).astype(jnp.int16)
    for side in range(planes):
        out[side * packed.shape[0] : (side + 1) * packed.shape[0], :] = packed


def solve_kernel(kyr, depth, capacity, reach, received, basis, green, out, codes):
    planes = green.shape[1]
    sources = received.shape[0] // reach
    codes[...] = received[...].astype(jnp.int32).astype(jnp.float32)
    power = codes[pl.ds(0, sources, stride=reach), :]
    scale = jnp.exp2(power * (1.0 / STEPS)) * (1.0 / CODES)
    row = lax.broadcasted_iota(jnp.int32, (2 * reach, 128), 0)
    values = []
    for pair in range(0, sources, 2):
        factor = jnp.where(row < reach, scale[pair : pair + 1], scale[pair + 1 : pair + 2])
        values.append(codes[pair * reach : (pair + 2) * reach, :] * factor)
    each = sources // planes // 2
    blocks = [jnp.concatenate(values[i * each : (i + 1) * each], axis=0) for i in range(planes)]
    high, low = split(jnp.concatenate(blocks, axis=1))
    product = matmul(basis[...], high)
    product = product[: 2 * kyr] + product[2 * kyr :] + matmul(basis[: 2 * kyr, :], low)
    cosine = [jnp.zeros((kyr, 128), jnp.float32) for _ in range(depth)]
    sine = [jnp.zeros((kyr, 128), jnp.float32) for _ in range(depth)]
    for block in range(planes):
        lanes = slice(block * 128, (block + 1) * 128)
        for k in range(depth):
            cosine[k] = cosine[k] + green[k, block] * product[:kyr, lanes]
            sine[k] = sine[k] + green[k, block] * product[kyr:, lanes]
    lane = lax.broadcasted_iota(jnp.int32, (kyr, 128), 1)
    share = 2 * capacity

    def gathered(fields):
        fields = [field + pltpu.roll(field, 64, 1) for field in fields]
        field = jnp.where(lane < 64, fields[0], fields[1])
        return field + pltpu.roll(field, share, 1)

    turned = gathered(sine)
    turned = jnp.where(lane % 2 == 0, pltpu.roll(turned, 127, 1), -pltpu.roll(turned, 1, 1))
    result = gathered(cosine) + turned
    flipped = result.T
    for k in range(depth):
        out[:, k, :] = flipped[64 * k + share : 64 * k + 2 * share]


def exchange(array, axis, size, shifted):
    pairs = [(i, i + 1) for i in range(shifted, size - 1, 2)]
    return lax.ppermute(array, axis, pairs + [(j, i) for i, j in pairs])


def in_hbm(array):
    return pltpu.with_memory_space_constraint(array, pltpu.HBM)


def per_device(groups, planes, velocity_x, velocity_y, velocity_z, owners, below, above, metric):
    depth, rows, width = velocity_x.shape
    kxr = owners.shape[0]
    kyr = 2 * kxr
    levels = below.shape[0]
    limit = pltpu.CompilerParams(vmem_limit_bytes=32 * 1024 * 1024)
    fields = (velocity_x, velocity_y, velocity_z)

    plane_shape = jax.ShapeDtypeStruct((3, rows, width), jnp.bfloat16)
    row_shape = jax.ShapeDtypeStruct((8, width), jnp.bfloat16)
    own_one, own_two = pl.pallas_call(
        pack_kernel,
        out_shape=(plane_shape, plane_shape),
        in_specs=[HBM] * 3,
        out_specs=(VMEM,) * 2,
        scratch_shapes=[pltpu.SemaphoreType.DMA((3, 2))],
        compiler_params=limit,
    )(*[in_hbm(field) for field in fields])
    plane_one = exchange(own_one, "gz", planes, 0)
    plane_two = exchange(own_two, "gz", planes, 1)
    row_one, row_two = pl.pallas_call(
        row_kernel,
        out_shape=(row_shape, row_shape),
        in_specs=[VMEM] * 2,
        out_specs=(VMEM,) * 2,
        compiler_params=limit,
    )(own_one, own_two)
    row_one = exchange(row_one, "gy", groups, 0)
    row_two = exchange(row_two, "gy", groups, 1)

    table, factors = [jnp.asarray(array) for array in x_tables(width, kxr, rows * groups)]
    if 2 * kxr == 128:
        pick_shape = jax.ShapeDtypeStruct((8, groups * CAP * 2), jnp.int32)
    else:
        pick_shape = jax.ShapeDtypeStruct((2 * kxr, groups * CAP * 2), jnp.bfloat16)
    pick, green, table, factors = pl.pallas_call(
        functools.partial(mode_kernel, groups, CAP, kyr, levels, depth),
        out_shape=(
            pick_shape,
            jax.ShapeDtypeStruct((depth, planes, kyr, 128), jnp.float32),
            jax.ShapeDtypeStruct(table.shape, table.dtype),
            jax.ShapeDtypeStruct(factors.shape, factors.dtype),
        ),
        in_specs=[HBM] * 6,
        out_specs=(VMEM,) * 4,
        scratch_shapes=[
            pltpu.VMEM((1, kxr), jnp.int32),
            pltpu.SMEM((3, levels), jnp.float32),
            pltpu.SemaphoreType.DMA((5,)),
            pltpu.SemaphoreType.DMA((4,)),
        ],
        compiler_params=limit,
    )(*map(in_hbm, (owners.reshape(1, kxr), below, above, metric, table, factors)))

    strain, spectra = pl.pallas_call(
        functools.partial(early_kernel, groups, planes),
        out_shape=(
            jax.ShapeDtypeStruct((depth, 5, rows, width), jnp.float32),
            jax.ShapeDtypeStruct((3 * (rows + MARGIN) + 6 * MARGIN, 2 * kxr), jnp.float32),
        ),
        in_specs=[VMEM] * 4,
        out_specs=(VMEM,) * 2,
        scratch_shapes=[pltpu.VMEM((2, PIECES * (5 * rows + 6 * MARGIN), width // 2), jnp.bfloat16)],
        compiler_params=limit,
    )(own_one, own_two, table, factors)

    reach = rows + 4
    held = pltpu.VMEM((2, PIECES * 7 * rows, width // 2), jnp.bfloat16)
    earlier, ready = pl.pallas_call(
        late_kernel,
        out_shape=(
            jax.ShapeDtypeStruct((7 * rows, 2 * kxr), jnp.float32),
            jax.ShapeDtypeStruct((7, rows, width), jnp.float32),
        ),
        in_specs=[VMEM] * 6,
        out_specs=(VMEM,) * 2,
        scratch_shapes=[held],
        compiler_params=limit,
    )(own_two, plane_one, row_one, row_two, strain, table)
    outgoing = pl.pallas_call(
        functools.partial(last_kernel, planes, groups, CAP),
        out_shape=jax.ShapeDtypeStruct((planes * groups * reach, 128), jnp.int16),
        in_specs=[VMEM] * 8,
        out_specs=VMEM,
        scratch_shapes=[held, pltpu.VMEM((groups * reach, 128), jnp.float32)],
        compiler_params=limit,
    )(own_one, plane_two, ready, table, earlier, spectra, factors, pick)
    outgoing = outgoing.reshape(planes * groups, reach // 2, 2, 128)
    received = lax.all_to_all(outgoing, ("gz", "gy"), split_axis=0, concat_axis=0, tiled=True)
    received = received.reshape(planes * groups * reach, 128)

    basis = jnp.asarray(y_tables(rows, groups, kyr))
    solved = pl.pallas_call(
        functools.partial(solve_kernel, kyr, depth, CAP, reach),
        out_shape=jax.ShapeDtypeStruct((CAP * 2, depth, kyr), jnp.float32),
        in_specs=[VMEM] * 3,
        out_specs=VMEM,
        scratch_shapes=[pltpu.VMEM(received.shape, jnp.float32)],
        compiler_params=limit,
    )(received, basis, green)
    return solved.reshape(1, CAP, 2, depth, kyr)


def solution(mesh):
    placed = (P("gz", "gy", None), P("gz", "gy", None), P("gz", "gy", None), P(), P(), P(), P())
    return jax.shard_map(
        functools.partial(per_device, mesh.shape["gy"], mesh.shape["gz"]),
        mesh=mesh,
        in_specs=placed,
        out_specs=P("gy", None, None, "gz", None),
        check_vma=False,
    )
```

```python
import functools
import math

import jax
import jax.numpy as jnp
import numpy as np
from jax import lax
from jax.experimental import pallas as pl
from jax.experimental.pallas import tpu as pltpu
from jax.sharding import PartitionSpec as P

CAP = 16
SMAG_COEF = 0.12
STRAIN_FLOOR = 0.01
BASE_SHIFT = 0.004
MODE_SHIFT = 0.02

CHUNK = 256
MARGIN = 8
CODES = 32000.0
STEPS = 32.0
PIECES = 3
VMEM = pl.BlockSpec(memory_space=pltpu.VMEM)
HBM = pl.BlockSpec(memory_space=pltpu.HBM)
SMEM = pl.BlockSpec(memory_space=pltpu.SMEM)


def split(value):
    high = value.astype(jnp.bfloat16)
    low = (value - high.astype(jnp.float32)).astype(jnp.bfloat16)
    return high, low


def split_table(table, parts):
    pieces = []
    for _ in range(parts):
        pieces.append(table.astype(jnp.bfloat16))
        table = table - pieces[-1].astype(np.float64)
    return pieces


def matmul(left, right):
    return jnp.dot(left, right, preferred_element_type=jnp.float32)


def mode_order(place, kxr):
    return 2 * place - (2 * place // kxr) * (kxr - 1)


def x_tables(width, kxr, grid_rows):
    norm = 1.0 / math.sqrt(width * grid_rows)
    modes = mode_order(np.arange(kxr), kxr)
    phase = (np.arange(width // 2)[:, None] * modes[None, :] % width) * (2.0 * np.pi / width)
    table = np.stack([np.cos(phase) * norm, -np.sin(phase) * norm], axis=2)
    table = table.reshape(width // 2, 2, kxr).transpose(1, 0, 2).reshape(width, kxr)
    angle = modes * (2.0 * np.pi / width)
    turn = np.stack([-np.sin(angle), np.sin(angle)], axis=1).reshape(2 * kxr) * 0.5
    second = np.repeat(-4.0 * np.sin(angle * 0.5) ** 2, 2)
    pieces = split_table(table, PIECES) + [np.zeros(table.shape, jnp.bfloat16)]
    return np.concatenate(pieces, axis=1), np.stack([turn, second]).astype(np.float32)


def y_tables(rows, groups, kyr):
    grid_rows = rows * groups
    nowhere = -grid_rows
    offset = np.concatenate([[nowhere, -1, rows, nowhere], np.arange(rows)])
    cells = (np.arange(groups)[:, None] * rows + offset[None, :]).reshape(-1)
    ky = np.arange(kyr) - kyr // 2
    phase = (ky[:, None] * cells[None, :] % grid_rows) * (2.0 * np.pi / grid_rows)
    valid = (cells >= 0) & (cells < grid_rows)
    table = np.concatenate([np.cos(phase), np.sin(phase)], axis=0) * valid[None, :]
    return np.concatenate(split_table(table, 2), axis=0)


def mode_kernel(
    groups, capacity, kyr, levels, depth,
    owners_hbm, below_hbm, above_hbm, metric_hbm, table_hbm, factors_hbm,
    pick, green, table, factors, owners, scalars, arrived, small,
):
    copies = [pltpu.make_async_copy(factors_hbm, factors, arrived.at[0])]
    share = table.shape[0] // (arrived.shape[0] - 1)
    for i in range(1, arrived.shape[0]):
        at = pl.ds((i - 1) * share, share)
        copies.append(pltpu.make_async_copy(table_hbm.at[at], table.at[at], arrived.at[i]))
    others = [pltpu.make_async_copy(owners_hbm, owners, small.at[3])]
    for i, array in enumerate((below_hbm, above_hbm, metric_hbm)):
        others.append(pltpu.make_async_copy(array, scalars.at[i], small.at[i]))
    for copy in others + copies:
        copy.start()
    for copy in others:
        copy.wait()
    kxr = owners.shape[1]
    below, above, metric = [[scalars[i, k] for k in range(levels)] for i in range(3)]
    places, gy = lax.axis_index("gz"), lax.axis_index("gy")
    shape = (2 * kxr, kxr)
    mode = mode_order(lax.broadcasted_iota(jnp.int32, shape, 0) // 2, kxr)
    other = lax.broadcasted_iota(jnp.int32, shape, 1)
    named = owners[...].astype(jnp.float32)
    owner = jnp.sum(jnp.where(mode == other, named, 0.0), axis=1, keepdims=True)
    rank = jnp.sum(
        jnp.where((named == owner) & (other < mode), 1.0, 0.0), axis=1, keepdims=True
    )
    slot = (owner * capacity + rank).astype(jnp.int32)
    part = lax.broadcasted_iota(jnp.int32, (2 * kxr, 1), 0) % 2
    column = lax.broadcasted_iota(jnp.int32, (2 * kxr, groups * capacity * 2), 1)
    chosen = jnp.where(slot * 2 + part == column, 1.0, 0.0)
    if pick.dtype == jnp.bfloat16:
        pick[...] = chosen.astype(jnp.bfloat16)
    else:
        place = lax.broadcasted_iota(jnp.int32, chosen.shape, 0).astype(jnp.float32)
        source = jnp.sum(chosen * place, axis=0, keepdims=True).astype(jnp.int32)
        filled = jnp.sum(chosen, axis=0, keepdims=True).astype(jnp.int32)
        pick[...] = jnp.concatenate([source, filled] + [source * 0] * 6, axis=0)

    lane = lax.broadcasted_iota(jnp.int32, (2 * kxr, 128), 1)
    here = gy * capacity + lane % (2 * capacity) // 2
    owned = (slot == here) & (part == 0)
    mode_id = mode_order(lax.broadcasted_iota(jnp.int32, (2 * kxr, 128), 0) // 2, kxr)
    mode_id = mode_id.astype(jnp.float32)
    kx = jnp.sum(jnp.where(owned, mode_id, 0.0), axis=0, keepdims=True)
    filled = jnp.sum(jnp.where(owned, 1.0, 0.0), axis=0, keepdims=True)

    size = 64
    at = lax.broadcasted_iota(jnp.int32, (size, 128), 1) // (2 * capacity)

    def turn(step, carry):
        start = pl.multiple_of(step * size, size)
        ky = lax.broadcasted_iota(jnp.int32, (size, 128), 0) + (start - kyr // 2)
        ky = ky.astype(jnp.float32)
        radius = kx * kx + ky * ky
        inside = jnp.where(radius <= float(kxr * kxr), filled, 0.0)
        shift = BASE_SHIFT + MODE_SHIFT * (radius / float(kxr * kxr))
        inverse = []
        for k in range(levels):
            pivot = -(below[k] + above[k] + metric[k] * shift)
            if k > 0:
                pivot = pivot - below[k] * above[k - 1] * inverse[-1]
            inverse.append(1.0 / pivot)
        for k in range(depth):
            target = places * depth + k
            forward = []
            for pos in range(levels):
                unit = jnp.where(target == pos, 1.0, 0.0)
                value = inside * unit
                if pos > 0:
                    value = value - above[pos - 1] * inverse[pos - 1] * forward[-1]
                forward.append(value)
            weights = [None] * levels
            for pos in range(levels - 1, -1, -1):
                value = forward[pos]
                if pos < levels - 1:
                    value = value - below[pos + 1] * weights[pos + 1]
                weights[pos] = value * inverse[pos]
            for block in range(levels // depth):
                total = jnp.zeros((size, 128), jnp.float32)
                for j in range(depth + 2):
                    pos = block * depth - 1 + j
                    if 0 <= pos < levels:
                        total = jnp.where(at == j, weights[pos], total)
                green[k, block, pl.ds(start, size), :] = total
        return carry

    lax.fori_loop(0, kyr // size, turn, 0)
    for copy in copies:
        copy.wait()


def pack_kernel(vx, vy, vz, own_one, own_two, arrived):
    odd = lax.axis_index("gz") % 2
    copies = []
    for k, plane in enumerate((own_one, own_two)):
        for i, field in enumerate((vx, vy, vz)):
            level = odd if k else 1 - odd
            copies.append(pltpu.make_async_copy(field.at[level], plane.at[i], arrived.at[i, k]))
    for copy in copies:
        copy.start()
    for copy in copies:
        copy.wait()


def row_kernel(own_one, own_two, row_one, row_two):
    rows, width = own_one.shape[1:]
    odd_row = lax.axis_index("gy") % 2
    sub = lax.broadcasted_iota(jnp.int32, (8, width), 0)
    bottom = jnp.zeros((8, width), jnp.float32)
    top = bottom
    for i in range(3):
        for k, plane in enumerate((own_one, own_two)):
            field = plane[i].astype(jnp.float32)
            bottom = jnp.where(sub == 2 * i + k, field[0:1], bottom)
            top = jnp.where(sub == 2 * i + k, field[rows - 1 : rows], top)
    row_one[...] = jnp.where(odd_row == 0, top, bottom).astype(jnp.bfloat16)
    row_two[...] = jnp.where(odd_row == 0, bottom, top).astype(jnp.bfloat16)


def up(field):
    return pltpu.roll(field, field.shape[0] - 1, 0)


def down(field):
    return pltpu.roll(field, 1, 0)


def padded(field):
    empty = jnp.zeros((MARGIN, field.shape[1]), field.dtype)
    return jnp.concatenate([field, empty], axis=0)


def magnitude(squared):
    return SMAG_COEF * (squared * lax.rsqrt(squared))


def put_lines(lines, step, near, far):
    cells = pl.ds(step * CHUNK, CHUNK)
    count = lines.shape[1] // PIECES
    start = 0
    for one, other in zip(near, far):
        size = one.shape[0]
        for parity, field in enumerate((one + other, one - other)):
            for piece in range(PIECES):
                at = piece * count + start
                part = field.astype(jnp.bfloat16)
                lines[parity, at : at + size, cells] = part
                field = field - part.astype(jnp.float32)
        start += size


def transformed(lines, table):
    count, half = lines.shape[1] // PIECES, lines.shape[2]
    modes = table.shape[1] // (PIECES + 1)
    totals = []
    for parity in range(2):
        product = matmul(lines[parity], table[parity * half : (parity + 1) * half, :])
        total = product[:count, : 2 * modes] + product[:count, 2 * modes :]
        for piece in range(1, PIECES):
            total = total + product[piece * count : (piece + 1) * count, : 2 * modes]
        totals.append(total + pltpu.roll(total, modes, 1))
    lane = lax.broadcasted_iota(jnp.int32, (1, 2 * modes), 1)
    return jnp.where(lane < modes, *totals)


def slope_of(factors, field):
    modes = field.shape[1]
    even = lax.broadcasted_iota(jnp.int32, (1, modes), 1) % 2 == 0
    moved = jnp.where(even, pltpu.roll(field, modes - 1, 1), pltpu.roll(field, 1, 1))
    return factors[0:1] * moved


def early_kernel(
    groups, planes,
    own_one, own_two, table, factors,
    strain, spectra, lines,
):
    rows, width = own_one.shape[1:]
    gz, gy = lax.axis_index("gz"), lax.axis_index("gy")
    first = jnp.where(gz == 0, 1.0, 0.0)
    last = jnp.where(gz == planes - 1, 1.0, 0.0)
    odd = gz % 2
    sub = lax.broadcasted_iota(jnp.int32, (8, CHUNK), 0)
    ghost_rows = jnp.where((sub == 0) & (gy == groups - 1) | (sub == 7) & (gy == 0), 1.0, 0.0)

    def fields_at(step):
        here = step * CHUNK
        before, after = (here - 128) % width, (here + CHUNK) % width
        cells = pl.ds(here, CHUNK)
        flat, rims = [], []
        for k, source in enumerate((own_one, own_two)):
            sign = jnp.where(odd == k, 1.0, -1.0)
            own = [source[i, :, cells].astype(jnp.float32) for i in range(3)]
            x, y, rim = [], [], []
            for i in range(3):
                window = jnp.concatenate(
                    [
                        source[i, :, pl.ds(before, 128)].astype(jnp.float32),
                        own[i],
                        source[i, :, pl.ds(after, 128)].astype(jnp.float32),
                    ],
                    axis=1,
                )
                difference = pltpu.roll(window, CHUNK + 255, 1) - pltpu.roll(window, 1, 1)
                x.append(difference[:, 128 : 128 + CHUNK])
                field = padded(own[i])
                difference = up(field) - down(field)
                y.append(difference[:rows])
                rim.append(difference[rows:])
            e01 = y[0] + x[1]
            strain[k, 0, :, cells] = x[0]
            strain[k, 1, :, cells] = y[1]
            strain[k, 2, :, cells] = e01
            strain[k, 3, :, cells] = sign * x[2]
            strain[k, 4, :, cells] = sign * y[2]
            squared = 0.5 * (rim[1] * rim[1]) + 0.25 * (rim[0] * rim[0] + rim[2] * rim[2])
            viscous = ghost_rows * magnitude(squared + STRAIN_FLOOR)
            rims += [viscous * rim[0], viscous * rim[1], viscous * (sign * rim[2])]
            flat.append(x[0] + y[1])

        ghost = [(first - last) * own_two[i, :, cells].astype(jnp.float32) for i in range(3)]
        squared = 0.5 * (ghost[2] * ghost[2])
        squared = squared + 0.25 * (ghost[0] * ghost[0] + ghost[1] * ghost[1])
        viscous = magnitude(squared + STRAIN_FLOOR)
        edge = [viscous * ghost[i] for i in range(3)]
        return flat + edge + [jnp.concatenate(rims, axis=0)]

    steps = width // CHUNK // 2
    for step in range(steps):
        put_lines(lines, step, fields_at(step), fields_at(step + steps))

    total = transformed(lines, table)
    pieces = [padded(total[rows * i : rows * (i + 1)]) for i in range(5)]
    t02, t12, s22 = pieces[2:]
    cross = 0.25 * (up(t12) - down(t12)) + slope_of(factors, t02)
    pieces = pieces[:2] + [s22 + (last - first) * cross]
    for i, piece in enumerate(pieces + [total[5 * rows :]]):
        start = (rows + MARGIN) * i
        spectra[start : start + piece.shape[0], :] = piece


def corrected(k, cells, row_one, row_two, strain):
    rows = strain.shape[2]
    odd_row = lax.axis_index("gy") % 2
    sign = jnp.where(lax.axis_index("gz") % 2 == k, 1.0, -1.0)
    row = lax.broadcasted_iota(jnp.int32, (rows, CHUNK), 0)
    ones = row_one[:, cells].astype(jnp.float32)
    twos = row_two[:, cells].astype(jnp.float32)
    lows = jnp.where(odd_row == 0, twos, ones)
    highs = jnp.where(odd_row == 0, ones, twos)

    def beyond(i):
        at = 2 * i + k
        inner = jnp.where(row == 0, -lows[at : at + 1], 0.0)
        return jnp.where(row == rows - 1, highs[at : at + 1], inner)

    x0, sx2 = strain[k, 0, :, cells], strain[k, 3, :, cells]
    edge = beyond(1)
    y1 = strain[k, 1, :, cells] + edge
    e01 = strain[k, 2, :, cells] + beyond(0)
    sy2 = strain[k, 4, :, cells] + sign * beyond(2)
    flat = 0.5 * (x0 * x0 + y1 * y1) + 0.25 * (e01 * e01) + STRAIN_FLOOR
    return x0, y1, e01, sx2, sy2, flat, sign * edge


def stress_lines(slopes_at, other, plane, table, lines):
    def fields_at(step):
        cells = pl.ds(step * CHUNK, CHUNK)
        x0, y1, e01, sx2, sy2, flat, edge = slopes_at(cells)
        z = [
            plane[i, :, cells].astype(jnp.float32) - other[i, :, cells].astype(jnp.float32)
            for i in range(3)
        ]
        e02, e12 = z[0] + sx2, z[1] + sy2
        squared = flat + 0.5 * (z[2] * z[2]) + 0.25 * (e02 * e02 + e12 * e12)
        viscous = magnitude(squared)
        fields = [viscous * field for field in (e01, y1, e12, z[2], e02, x0)]
        return fields + [z[2] + edge]

    steps = plane.shape[2] // CHUNK // 2
    for step in range(steps):
        put_lines(lines, step, fields_at(step), fields_at(step + steps))
    return transformed(lines, table)


def level_parts(k, total, spectra, factors):
    rows = total.shape[0] // 7
    padded_rows = rows + MARGIN
    odd = lax.axis_index("gz") % 2
    sign = jnp.where(odd == k, 1.0, -1.0)
    pieces = [total[rows * i : rows * (i + 1)] for i in range(7)]
    for i in range(3):
        start = 3 * padded_rows + MARGIN * (3 * k + i)
        pieces[i] = jnp.concatenate([pieces[i], spectra[start : start + MARGIN, :]], axis=0)
    t01, p11, t12 = pieces[:3]
    s22, t02, s00, rise = [padded(piece) for piece in pieces[3:]]
    p11 = up(p11) + down(p11) - 2.0 * p11
    t01 = up(t01) - down(t01)
    t12 = 0.25 * (up(t12) - down(t12))
    flat = spectra[k * padded_rows : (k + 1) * padded_rows, :]
    s22, rise = sign * s22, sign * rise
    middle = p11 - 2.0 * s22 + 0.5 * (flat + rise)
    middle = middle + slope_of(factors, t01) + factors[1:2] * s00
    cross = sign * (t12 + slope_of(factors, t02))
    return [s22 + cross, middle, s22 - cross]


def late_kernel(
    other, plane, row_one, row_two, strain, table, spectra, factors,
    out, ready, lines,
):
    slopes_at = lambda cells: corrected(0, cells, row_one, row_two, strain)
    total = stress_lines(slopes_at, other, plane, table, lines)
    out[...] = jnp.concatenate(level_parts(0, total, spectra, factors), axis=0)
    for step in range(plane.shape[2] // CHUNK):
        cells = pl.ds(step * CHUNK, CHUNK)
        for i, field in enumerate(corrected(1, cells, row_one, row_two, strain)):
            ready[i, :, cells] = field


def last_kernel(
    planes, groups, capacity,
    other, plane, ready, table, earlier, spectra, factors, pick,
    out, lines, codes,
):
    rows = other.shape[1]
    padded_rows = rows + MARGIN
    gz = lax.axis_index("gz")
    first = jnp.where(gz == 0, 1.0, 0.0)
    last = jnp.where(gz == planes - 1, 1.0, 0.0)
    odd = gz % 2
    slopes_at = lambda cells: [ready[i, :, cells] for i in range(7)]
    parts = [
        [earlier[padded_rows * i : padded_rows * (i + 1), :] for i in range(3)],
        level_parts(1, stress_lines(slopes_at, other, plane, table, lines), spectra, factors),
    ]
    ghost = spectra[2 * padded_rows : 3 * padded_rows, :]
    lower = [jnp.where(odd == 1, p, q) for p, q in zip(*parts)]
    upper = [jnp.where(odd == 1, q, p) for p, q in zip(*parts)]
    spectrum = [
        lower[0],
        lower[1] + upper[0] + first * ghost,
        lower[2] + upper[1] + last * ghost,
        upper[2],
    ]
    count = len(spectrum)

    stacked = jnp.concatenate(spectrum, axis=0)
    if pick.dtype == jnp.bfloat16:
        selected = matmul(jnp.concatenate(split(stacked), axis=0), pick[...])
        size = count * padded_rows
        selected = selected[:size] + selected[size:]
    else:
        halves = []
        for start in range(0, pick.shape[1], 128):
            source = jnp.broadcast_to(pick[0:1, start : start + 128], stacked.shape)
            taken = jnp.take_along_axis(stacked, source, axis=1)
            halves.append(jnp.where(pick[1:2, start : start + 128] > 0, taken, 0.0))
        selected = jnp.concatenate(halves, axis=1)

    lane = lax.broadcasted_iota(jnp.int32, (padded_rows, 128), 1)
    empty_block = jnp.zeros((padded_rows, 128), jnp.float32)
    sub_lanes = lax.broadcasted_iota(jnp.int32, (8, 128), 0)
    share = 2 * capacity
    for half in range(groups * share // 128):
        pieces = [
            selected[padded_rows * j : padded_rows * (j + 1), 128 * half : 128 * (half + 1)]
            for j in range(count)
        ]
        for place in range(128 // share):
            block = empty_block
            for j in range(count):
                distance = (share * (j - place)) % 128
                moved = pltpu.roll(pieces[j], distance, 1) if distance else pieces[j]
                block = jnp.where(lane // share == j, moved, block)
            largest = jnp.max(jnp.abs(block), axis=0, keepdims=True)
            power = jnp.floor(jnp.log2(jnp.maximum(largest, 1e-30)) * STEPS) + 1.0
            block = jnp.floor(block * (CODES * jnp.exp2(power * (-1.0 / STEPS))) + 0.5)
            rim = pltpu.roll(block[rows:], 2, 0)
            rim = jnp.where(sub_lanes == 0, power, jnp.where(sub_lanes < 3, rim, 0.0))
            base = (half * (128 // share) + place) * (rows + 4)
            codes[base : base + 4, :] = rim[:4]
            codes[base + 4 : base + 4 + rows, :] = block[:rows]
    packed = codes[...].astype(jnp.int32).astype(jnp.int16)
    for side in range(planes):
        out[side * packed.shape[0] : (side + 1) * packed.shape[0], :] = packed


def solve_kernel(kyr, depth, capacity, reach, received, basis, green, out, codes):
    planes = green.shape[1]
    sources = received.shape[0] // reach
    codes[...] = received[...].astype(jnp.int32).astype(jnp.float32)
    power = codes[pl.ds(0, sources, stride=reach), :]
    scale = jnp.exp2(power * (1.0 / STEPS)) * (1.0 / CODES)
    row = lax.broadcasted_iota(jnp.int32, (2 * reach, 128), 0)
    values = []
    for pair in range(0, sources, 2):
        factor = jnp.where(row < reach, scale[pair : pair + 1], scale[pair + 1 : pair + 2])
        values.append(codes[pair * reach : (pair + 2) * reach, :] * factor)
    each = sources // planes // 2
    blocks = [jnp.concatenate(values[i * each : (i + 1) * each], axis=0) for i in range(planes)]
    high, low = split(jnp.concatenate(blocks, axis=1))
    product = matmul(basis[...], high)
    product = product[: 2 * kyr] + product[2 * kyr :] + matmul(basis[: 2 * kyr, :], low)
    cosine = [jnp.zeros((kyr, 128), jnp.float32) for _ in range(depth)]
    sine = [jnp.zeros((kyr, 128), jnp.float32) for _ in range(depth)]
    for block in range(planes):
        lanes = slice(block * 128, (block + 1) * 128)
        for k in range(depth):
            cosine[k] = cosine[k] + green[k, block] * product[:kyr, lanes]
            sine[k] = sine[k] + green[k, block] * product[kyr:, lanes]
    lane = lax.broadcasted_iota(jnp.int32, (kyr, 128), 1)
    share = 2 * capacity

    def gathered(fields):
        fields = [field + pltpu.roll(field, 64, 1) for field in fields]
        field = jnp.where(lane < 64, fields[0], fields[1])
        return field + pltpu.roll(field, share, 1)

    turned = gathered(sine)
    turned = jnp.where(lane % 2 == 0, pltpu.roll(turned, 127, 1), -pltpu.roll(turned, 1, 1))
    result = gathered(cosine) + turned
    flipped = result.T
    for k in range(depth):
        out[:, k, :] = flipped[64 * k + share : 64 * k + 2 * share]


def exchange(array, axis, size, shifted):
    pairs = [(i, i + 1) for i in range(shifted, size - 1, 2)]
    return lax.ppermute(array, axis, pairs + [(j, i) for i, j in pairs])


def in_hbm(array):
    return pltpu.with_memory_space_constraint(array, pltpu.HBM)


def per_device(groups, planes, velocity_x, velocity_y, velocity_z, owners, below, above, metric):
    depth, rows, width = velocity_x.shape
    kxr = owners.shape[0]
    kyr = 2 * kxr
    levels = below.shape[0]
    limit = pltpu.CompilerParams(vmem_limit_bytes=32 * 1024 * 1024)
    fields = (velocity_x, velocity_y, velocity_z)

    plane_shape = jax.ShapeDtypeStruct((3, rows, width), jnp.bfloat16)
    row_shape = jax.ShapeDtypeStruct((8, width), jnp.bfloat16)
    own_one, own_two = pl.pallas_call(
        pack_kernel,
        out_shape=(plane_shape, plane_shape),
        in_specs=[HBM] * 3,
        out_specs=(VMEM,) * 2,
        scratch_shapes=[pltpu.SemaphoreType.DMA((3, 2))],
        compiler_params=limit,
    )(*[in_hbm(field) for field in fields])
    plane_one = exchange(own_one, "gz", planes, 0)
    plane_two = exchange(own_two, "gz", planes, 1)
    row_one, row_two = pl.pallas_call(
        row_kernel,
        out_shape=(row_shape, row_shape),
        in_specs=[VMEM] * 2,
        out_specs=(VMEM,) * 2,
        compiler_params=limit,
    )(own_one, own_two)
    row_one = exchange(row_one, "gy", groups, 0)
    row_two = exchange(row_two, "gy", groups, 1)

    table, factors = [jnp.asarray(array) for array in x_tables(width, kxr, rows * groups)]
    if 2 * kxr == 128:
        pick_shape = jax.ShapeDtypeStruct((8, groups * CAP * 2), jnp.int32)
    else:
        pick_shape = jax.ShapeDtypeStruct((2 * kxr, groups * CAP * 2), jnp.bfloat16)
    pick, green, table, factors = pl.pallas_call(
        functools.partial(mode_kernel, groups, CAP, kyr, levels, depth),
        out_shape=(
            pick_shape,
            jax.ShapeDtypeStruct((depth, planes, kyr, 128), jnp.float32),
            jax.ShapeDtypeStruct(table.shape, table.dtype),
            jax.ShapeDtypeStruct(factors.shape, factors.dtype),
        ),
        in_specs=[HBM] * 6,
        out_specs=(VMEM,) * 4,
        scratch_shapes=[
            pltpu.VMEM((1, kxr), jnp.int32),
            pltpu.SMEM((3, levels), jnp.float32),
            pltpu.SemaphoreType.DMA((5,)),
            pltpu.SemaphoreType.DMA((4,)),
        ],
        compiler_params=limit,
    )(*map(in_hbm, (owners.reshape(1, kxr), below, above, metric, table, factors)))

    strain, spectra = pl.pallas_call(
        functools.partial(early_kernel, groups, planes),
        out_shape=(
            jax.ShapeDtypeStruct((depth, 5, rows, width), jnp.float32),
            jax.ShapeDtypeStruct((3 * (rows + MARGIN) + 6 * MARGIN, 2 * kxr), jnp.float32),
        ),
        in_specs=[VMEM] * 4,
        out_specs=(VMEM,) * 2,
        scratch_shapes=[pltpu.VMEM((2, PIECES * (5 * rows + 6 * MARGIN), width // 2), jnp.bfloat16)],
        compiler_params=limit,
    )(own_one, own_two, table, factors)

    reach = rows + 4
    held = pltpu.VMEM((2, PIECES * 7 * rows, width // 2), jnp.bfloat16)
    earlier, ready = pl.pallas_call(
        late_kernel,
        out_shape=(
            jax.ShapeDtypeStruct((3 * (rows + MARGIN), 2 * kxr), jnp.float32),
            jax.ShapeDtypeStruct((7, rows, width), jnp.float32),
        ),
        in_specs=[VMEM] * 8,
        out_specs=(VMEM,) * 2,
        scratch_shapes=[held],
        compiler_params=limit,
    )(own_two, plane_one, row_one, row_two, strain, table, spectra, factors)
    outgoing = pl.pallas_call(
        functools.partial(last_kernel, planes, groups, CAP),
        out_shape=jax.ShapeDtypeStruct((planes * groups * reach, 128), jnp.int16),
        in_specs=[VMEM] * 8,
        out_specs=VMEM,
        scratch_shapes=[held, pltpu.VMEM((groups * reach, 128), jnp.float32)],
        compiler_params=limit,
    )(own_one, plane_two, ready, table, earlier, spectra, factors, pick)
    outgoing = outgoing.reshape(planes * groups, reach // 2, 2, 128)
    received = lax.all_to_all(outgoing, ("gz", "gy"), split_axis=0, concat_axis=0, tiled=True)
    received = received.reshape(planes * groups * reach, 128)

    basis = jnp.asarray(y_tables(rows, groups, kyr))
    solved = pl.pallas_call(
        functools.partial(solve_kernel, kyr, depth, CAP, reach),
        out_shape=jax.ShapeDtypeStruct((CAP * 2, depth, kyr), jnp.float32),
        in_specs=[VMEM] * 3,
        out_specs=VMEM,
        scratch_shapes=[pltpu.VMEM(received.shape, jnp.float32)],
        compiler_params=limit,
    )(received, basis, green)
    return solved.reshape(1, CAP, 2, depth, kyr)


def solution(mesh):
    placed = (P("gz", "gy", None), P("gz", "gy", None), P("gz", "gy", None), P(), P(), P(), P())
    return jax.shard_map(
        functools.partial(per_device, mesh.shape["gy"], mesh.shape["gz"]),
        mesh=mesh,
        in_specs=placed,
        out_specs=P("gy", None, None, "gz", None),
        check_vma=False,
    )
```

```python
import functools
import math

import jax
import jax.numpy as jnp
import numpy as np
from jax import lax
from jax.experimental import pallas as pl
from jax.experimental.pallas import tpu as pltpu
from jax.sharding import PartitionSpec as P

CAP = 16
SMAG_COEF = 0.12
STRAIN_FLOOR = 0.01
BASE_SHIFT = 0.004
MODE_SHIFT = 0.02

CHUNK = 256
MARGIN = 8
CODES = 32000.0
STEPS = 32.0
PIECES = 3
VMEM = pl.BlockSpec(memory_space=pltpu.VMEM)
HBM = pl.BlockSpec(memory_space=pltpu.HBM)
SMEM = pl.BlockSpec(memory_space=pltpu.SMEM)


def split(value):
    high = value.astype(jnp.bfloat16)
    low = (value - high.astype(jnp.float32)).astype(jnp.bfloat16)
    return high, low


def split_table(table, parts):
    pieces = []
    for _ in range(parts):
        pieces.append(table.astype(jnp.bfloat16))
        table = table - pieces[-1].astype(np.float64)
    return pieces


def matmul(left, right):
    return jnp.dot(left, right, preferred_element_type=jnp.float32)


def mode_order(place, kxr):
    return 2 * place - (2 * place // kxr) * (kxr - 1)


def x_tables(width, kxr, grid_rows):
    norm = 1.0 / math.sqrt(width * grid_rows)
    modes = mode_order(np.arange(kxr), kxr)
    phase = (np.arange(width // 2)[:, None] * modes[None, :] % width) * (2.0 * np.pi / width)
    table = np.stack([np.cos(phase) * norm, -np.sin(phase) * norm], axis=2)
    table = table.reshape(width // 2, 2, kxr).transpose(1, 0, 2).reshape(width, kxr)
    angle = modes * (2.0 * np.pi / width)
    turn = np.stack([-np.sin(angle), np.sin(angle)], axis=1).reshape(2 * kxr) * 0.5
    second = np.repeat(-4.0 * np.sin(angle * 0.5) ** 2, 2)
    pieces = split_table(table, PIECES) + [np.zeros(table.shape, jnp.bfloat16)]
    return np.concatenate(pieces, axis=1), np.stack([turn, second]).astype(np.float32)


def y_tables(rows, groups, kyr):
    grid_rows = rows * groups
    nowhere = -grid_rows
    offset = np.concatenate([[nowhere, -1, rows, nowhere], np.arange(rows)])
    cells = (np.arange(groups)[:, None] * rows + offset[None, :]).reshape(-1)
    ky = np.arange(kyr) - kyr // 2
    phase = (ky[:, None] * cells[None, :] % grid_rows) * (2.0 * np.pi / grid_rows)
    valid = (cells >= 0) & (cells < grid_rows)
    table = np.concatenate([np.cos(phase), np.sin(phase)], axis=0) * valid[None, :]
    return np.concatenate(split_table(table, 2), axis=0)


def mode_kernel(
    groups, capacity, kyr, levels, depth,
    owners_hbm, below_hbm, above_hbm, metric_hbm, table_hbm, factors_hbm,
    pick, green, table, factors, owners, scalars, arrived, small,
):
    copies = [pltpu.make_async_copy(factors_hbm, factors, arrived.at[0])]
    share = table.shape[0] // (arrived.shape[0] - 1)
    for i in range(1, arrived.shape[0]):
        at = pl.ds((i - 1) * share, share)
        copies.append(pltpu.make_async_copy(table_hbm.at[at], table.at[at], arrived.at[i]))
    others = [pltpu.make_async_copy(owners_hbm, owners, small.at[3])]
    for i, array in enumerate((below_hbm, above_hbm, metric_hbm)):
        others.append(pltpu.make_async_copy(array, scalars.at[i], small.at[i]))
    for copy in others + copies:
        copy.start()
    for copy in others:
        copy.wait()
    kxr = owners.shape[1]
    below, above, metric = [[scalars[i, k] for k in range(levels)] for i in range(3)]
    places, gy = lax.axis_index("gz"), lax.axis_index("gy")
    shape = (2 * kxr, kxr)
    mode = mode_order(lax.broadcasted_iota(jnp.int32, shape, 0) // 2, kxr)
    other = lax.broadcasted_iota(jnp.int32, shape, 1)
    named = owners[...].astype(jnp.float32)
    owner = jnp.sum(jnp.where(mode == other, named, 0.0), axis=1, keepdims=True)
    rank = jnp.sum(
        jnp.where((named == owner) & (other < mode), 1.0, 0.0), axis=1, keepdims=True
    )
    slot = (owner * capacity + rank).astype(jnp.int32)
    part = lax.broadcasted_iota(jnp.int32, (2 * kxr, 1), 0) % 2
    column = lax.broadcasted_iota(jnp.int32, (2 * kxr, groups * capacity * 2), 1)
    chosen = jnp.where(slot * 2 + part == column, 1.0, 0.0)
    if pick.dtype == jnp.bfloat16:
        pick[...] = chosen.astype(jnp.bfloat16)
    else:
        place = lax.broadcasted_iota(jnp.int32, chosen.shape, 0).astype(jnp.float32)
        source = jnp.sum(chosen * place, axis=0, keepdims=True).astype(jnp.int32)
        filled = jnp.sum(chosen, axis=0, keepdims=True).astype(jnp.int32)
        pick[...] = jnp.concatenate([source, filled] + [source * 0] * 6, axis=0)

    lane = lax.broadcasted_iota(jnp.int32, (2 * kxr, 128), 1)
    here = gy * capacity + lane % (2 * capacity) // 2
    owned = (slot == here) & (part == 0)
    mode_id = mode_order(lax.broadcasted_iota(jnp.int32, (2 * kxr, 128), 0) // 2, kxr)
    mode_id = mode_id.astype(jnp.float32)
    kx = jnp.sum(jnp.where(owned, mode_id, 0.0), axis=0, keepdims=True)
    filled = jnp.sum(jnp.where(owned, 1.0, 0.0), axis=0, keepdims=True)

    size = 64
    at = lax.broadcasted_iota(jnp.int32, (size, 128), 1) // (2 * capacity)

    def turn(step, carry):
        start = pl.multiple_of(step * size, size)
        ky = lax.broadcasted_iota(jnp.int32, (size, 128), 0) + (start - kyr // 2)
        ky = ky.astype(jnp.float32)
        radius = kx * kx + ky * ky
        inside = jnp.where(radius <= float(kxr * kxr), filled, 0.0)
        shift = BASE_SHIFT + MODE_SHIFT * (radius / float(kxr * kxr))
        inverse = []
        for k in range(levels):
            pivot = -(below[k] + above[k] + metric[k] * shift)
            if k > 0:
                pivot = pivot - below[k] * above[k - 1] * inverse[-1]
            inverse.append(1.0 / pivot)
        for k in range(depth):
            target = places * depth + k
            forward = []
            for pos in range(levels):
                unit = jnp.where(target == pos, 1.0, 0.0)
                value = inside * unit
                if pos > 0:
                    value = value - above[pos - 1] * inverse[pos - 1] * forward[-1]
                forward.append(value)
            weights = [None] * levels
            for pos in range(levels - 1, -1, -1):
                value = forward[pos]
                if pos < levels - 1:
                    value = value - below[pos + 1] * weights[pos + 1]
                weights[pos] = value * inverse[pos]
            for block in range(levels // depth):
                total = jnp.zeros((size, 128), jnp.float32)
                for j in range(depth + 2):
                    pos = block * depth - 1 + j
                    if 0 <= pos < levels:
                        total = jnp.where(at == j, weights[pos], total)
                green[k, block, pl.ds(start, size), :] = total
        return carry

    lax.fori_loop(0, kyr // size, turn, 0)
    for copy in copies:
        copy.wait()


def pack_kernel(vx, vy, vz, own_one, own_two, arrived):
    odd = lax.axis_index("gz") % 2
    copies = []
    for k, plane in enumerate((own_one, own_two)):
        for i, field in enumerate((vx, vy, vz)):
            level = odd if k else 1 - odd
            copies.append(pltpu.make_async_copy(field.at[level], plane.at[i], arrived.at[i, k]))
    for copy in copies:
        copy.start()
    for copy in copies:
        copy.wait()


def row_kernel(own_one, own_two, row_one, row_two):
    rows, width = own_one.shape[1:]
    odd_row = lax.axis_index("gy") % 2
    sub = lax.broadcasted_iota(jnp.int32, (8, width), 0)
    bottom = jnp.zeros((8, width), jnp.float32)
    top = bottom
    for i in range(3):
        for k, plane in enumerate((own_one, own_two)):
            field = plane[i].astype(jnp.float32)
            bottom = jnp.where(sub == 2 * i + k, field[0:1], bottom)
            top = jnp.where(sub == 2 * i + k, field[rows - 1 : rows], top)
    row_one[...] = jnp.where(odd_row == 0, top, bottom).astype(jnp.bfloat16)
    row_two[...] = jnp.where(odd_row == 0, bottom, top).astype(jnp.bfloat16)


def up(field):
    return pltpu.roll(field, field.shape[0] - 1, 0)


def down(field):
    return pltpu.roll(field, 1, 0)


def padded(field):
    empty = jnp.zeros((MARGIN, field.shape[1]), field.dtype)
    return jnp.concatenate([field, empty], axis=0)


def magnitude(squared):
    return SMAG_COEF * (squared * lax.rsqrt(squared))


def put_lines(lines, step, near, far):
    cells = pl.ds(step * CHUNK, CHUNK)
    count = lines.shape[1] // PIECES
    start = 0
    for one, other in zip(near, far):
        size = one.shape[0]
        for parity, field in enumerate((one + other, one - other)):
            for piece in range(PIECES):
                at = piece * count + start
                part = field.astype(jnp.bfloat16)
                lines[parity, at : at + size, cells] = part
                field = field - part.astype(jnp.float32)
        start += size


def transformed(lines, table):
    count, half = lines.shape[1] // PIECES, lines.shape[2]
    modes = table.shape[1] // (PIECES + 1)
    totals = []
    for parity in range(2):
        product = matmul(lines[parity], table[parity * half : (parity + 1) * half, :])
        total = product[:count, : 2 * modes] + product[:count, 2 * modes :]
        for piece in range(1, PIECES):
            total = total + product[piece * count : (piece + 1) * count, : 2 * modes]
        totals.append(total + pltpu.roll(total, modes, 1))
    lane = lax.broadcasted_iota(jnp.int32, (1, 2 * modes), 1)
    return jnp.where(lane < modes, *totals)


def slope_of(factors, field):
    modes = field.shape[1]
    even = lax.broadcasted_iota(jnp.int32, (1, modes), 1) % 2 == 0
    moved = jnp.where(even, pltpu.roll(field, modes - 1, 1), pltpu.roll(field, 1, 1))
    return factors[0:1] * moved


def early_kernel(
    groups, planes,
    own_one, own_two, table, factors,
    strain, spectra, lines,
):
    rows, width = own_one.shape[1:]
    gz, gy = lax.axis_index("gz"), lax.axis_index("gy")
    first = jnp.where(gz == 0, 1.0, 0.0)
    last = jnp.where(gz == planes - 1, 1.0, 0.0)
    odd = gz % 2
    sub = lax.broadcasted_iota(jnp.int32, (8, CHUNK), 0)
    ghost_rows = jnp.where((sub == 0) & (gy == groups - 1) | (sub == 7) & (gy == 0), 1.0, 0.0)

    def fields_at(step):
        here = step * CHUNK
        before, after = (here - 128) % width, (here + CHUNK) % width
        cells = pl.ds(here, CHUNK)
        flat, rims = [], []
        for k, source in enumerate((own_one, own_two)):
            sign = jnp.where(odd == k, 1.0, -1.0)
            own = [source[i, :, cells].astype(jnp.float32) for i in range(3)]
            x, y, rim = [], [], []
            for i in range(3):
                window = jnp.concatenate(
                    [
                        source[i, :, pl.ds(before, 128)].astype(jnp.float32),
                        own[i],
                        source[i, :, pl.ds(after, 128)].astype(jnp.float32),
                    ],
                    axis=1,
                )
                difference = pltpu.roll(window, CHUNK + 255, 1) - pltpu.roll(window, 1, 1)
                x.append(difference[:, 128 : 128 + CHUNK])
                field = padded(own[i])
                difference = up(field) - down(field)
                y.append(difference[:rows])
                rim.append(difference[rows:])
            e01 = y[0] + x[1]
            strain[k, 0, :, cells] = x[0]
            strain[k, 1, :, cells] = y[1]
            strain[k, 2, :, cells] = e01
            strain[k, 3, :, cells] = sign * x[2]
            strain[k, 4, :, cells] = sign * y[2]
            squared = 0.5 * (rim[1] * rim[1]) + 0.25 * (rim[0] * rim[0] + rim[2] * rim[2])
            viscous = ghost_rows * magnitude(squared + STRAIN_FLOOR)
            rims += [viscous * rim[0], viscous * rim[1], viscous * (sign * rim[2])]
            flat.append(x[0] + y[1])

        ghost = [(first - last) * own_two[i, :, cells].astype(jnp.float32) for i in range(3)]
        squared = 0.5 * (ghost[2] * ghost[2])
        squared = squared + 0.25 * (ghost[0] * ghost[0] + ghost[1] * ghost[1])
        viscous = magnitude(squared + STRAIN_FLOOR)
        edge = [viscous * ghost[i] for i in range(3)]
        return flat + edge + [jnp.concatenate(rims, axis=0)]

    steps = width // CHUNK // 2
    for step in range(steps):
        put_lines(lines, step, fields_at(step), fields_at(step + steps))

    total = transformed(lines, table)
    pieces = [padded(total[rows * i : rows * (i + 1)]) for i in range(5)]
    t02, t12, s22 = pieces[2:]
    cross = 0.25 * (up(t12) - down(t12)) + slope_of(factors, t02)
    pieces = pieces[:2] + [s22 + (last - first) * cross]
    for i, piece in enumerate(pieces + [total[5 * rows :]]):
        start = (rows + MARGIN) * i
        spectra[start : start + piece.shape[0], :] = piece


def corrected(k, cells, other, row_one, row_two, strain):
    rows = strain.shape[2]
    odd_row = lax.axis_index("gy") % 2
    sign = jnp.where(lax.axis_index("gz") % 2 == k, 1.0, -1.0)
    row = lax.broadcasted_iota(jnp.int32, (rows, CHUNK), 0)
    ones = row_one[:, cells].astype(jnp.float32)
    twos = row_two[:, cells].astype(jnp.float32)
    lows = jnp.where(odd_row == 0, twos, ones)
    highs = jnp.where(odd_row == 0, ones, twos)

    def beyond(i):
        at = 2 * i + k
        inner = jnp.where(row == 0, -lows[at : at + 1], 0.0)
        return jnp.where(row == rows - 1, highs[at : at + 1], inner)

    x0, sx2 = strain[k, 0, :, cells], strain[k, 3, :, cells]
    edge = beyond(1)
    y1 = strain[k, 1, :, cells] + edge
    e01 = strain[k, 2, :, cells] + beyond(0)
    sy2 = strain[k, 4, :, cells] + sign * beyond(2)
    flat = 0.5 * (x0 * x0 + y1 * y1) + 0.25 * (e01 * e01) + STRAIN_FLOOR
    across = [other[i, :, cells].astype(jnp.float32) for i in range(3)]
    return x0, y1, e01, sx2 - across[0], sy2 - across[1], flat, sign * edge, across[2]


def stress_lines(slopes_at, plane, table, lines):
    def fields_at(step):
        cells = pl.ds(step * CHUNK, CHUNK)
        x0, y1, e01, sx2, sy2, flat, edge, across = slopes_at(cells)
        near = [plane[i, :, cells].astype(jnp.float32) for i in range(3)]
        e02, e12, rise = near[0] + sx2, near[1] + sy2, near[2] - across
        squared = flat + 0.5 * (rise * rise) + 0.25 * (e02 * e02 + e12 * e12)
        viscous = magnitude(squared)
        fields = [viscous * field for field in (e01, y1, e12, rise, e02, x0)]
        return fields + [rise + edge]

    steps = plane.shape[2] // CHUNK // 2
    for step in range(steps):
        put_lines(lines, step, fields_at(step), fields_at(step + steps))
    return transformed(lines, table)


def level_parts(k, total, spectra, factors):
    rows = total.shape[0] // 7
    padded_rows = rows + MARGIN
    odd = lax.axis_index("gz") % 2
    sign = jnp.where(odd == k, 1.0, -1.0)
    pieces = [total[rows * i : rows * (i + 1)] for i in range(7)]
    for i in range(3):
        start = 3 * padded_rows + MARGIN * (3 * k + i)
        pieces[i] = jnp.concatenate([pieces[i], spectra[start : start + MARGIN, :]], axis=0)
    t01, p11, t12 = pieces[:3]
    s22, t02, s00, rise = [padded(piece) for piece in pieces[3:]]
    p11 = up(p11) + down(p11) - 2.0 * p11
    t01 = up(t01) - down(t01)
    t12 = 0.25 * (up(t12) - down(t12))
    flat = spectra[k * padded_rows : (k + 1) * padded_rows, :]
    s22, rise = sign * s22, sign * rise
    middle = p11 - 2.0 * s22 + 0.5 * (flat + rise)
    middle = middle + slope_of(factors, t01) + factors[1:2] * s00
    cross = sign * (t12 + slope_of(factors, t02))
    return [s22 + cross, middle, s22 - cross]


def late_kernel(
    own_one, own_two, plane, row_one, row_two, strain, table, spectra, factors,
    out, ready, lines,
):
    slopes_at = lambda cells: corrected(0, cells, own_two, row_one, row_two, strain)
    total = stress_lines(slopes_at, plane, table, lines)
    out[...] = jnp.concatenate(level_parts(0, total, spectra, factors), axis=0)
    for step in range(plane.shape[2] // CHUNK):
        cells = pl.ds(step * CHUNK, CHUNK)
        for i, field in enumerate(corrected(1, cells, own_one, row_one, row_two, strain)):
            ready[i, :, cells] = field


def last_kernel(
    planes, groups, capacity,
    plane, ready, table, earlier, spectra, factors, pick,
    out, lines, codes,
):
    rows = plane.shape[1]
    padded_rows = rows + MARGIN
    gz = lax.axis_index("gz")
    first = jnp.where(gz == 0, 1.0, 0.0)
    last = jnp.where(gz == planes - 1, 1.0, 0.0)
    odd = gz % 2
    slopes_at = lambda cells: [ready[i, :, cells] for i in range(8)]
    parts = [
        [earlier[padded_rows * i : padded_rows * (i + 1), :] for i in range(3)],
        level_parts(1, stress_lines(slopes_at, plane, table, lines), spectra, factors),
    ]
    ghost = spectra[2 * padded_rows : 3 * padded_rows, :]
    lower = [jnp.where(odd == 1, p, q) for p, q in zip(*parts)]
    upper = [jnp.where(odd == 1, q, p) for p, q in zip(*parts)]
    spectrum = [
        lower[0],
        lower[1] + upper[0] + first * ghost,
        lower[2] + upper[1] + last * ghost,
        upper[2],
    ]
    count = len(spectrum)

    stacked = jnp.concatenate(spectrum, axis=0)
    if pick.dtype == jnp.bfloat16:
        selected = matmul(jnp.concatenate(split(stacked), axis=0), pick[...])
        size = count * padded_rows
        selected = selected[:size] + selected[size:]
    else:
        halves = []
        for start in range(0, pick.shape[1], 128):
            source = jnp.broadcast_to(pick[0:1, start : start + 128], stacked.shape)
            taken = jnp.take_along_axis(stacked, source, axis=1)
            halves.append(jnp.where(pick[1:2, start : start + 128] > 0, taken, 0.0))
        selected = jnp.concatenate(halves, axis=1)

    lane = lax.broadcasted_iota(jnp.int32, (padded_rows, 128), 1)
    empty_block = jnp.zeros((padded_rows, 128), jnp.float32)
    sub_lanes = lax.broadcasted_iota(jnp.int32, (8, 128), 0)
    share = 2 * capacity
    for half in range(groups * share // 128):
        pieces = [
            selected[padded_rows * j : padded_rows * (j + 1), 128 * half : 128 * (half + 1)]
            for j in range(count)
        ]
        for place in range(128 // share):
            block = empty_block
            for j in range(count):
                distance = (share * (j - place)) % 128
                moved = pltpu.roll(pieces[j], distance, 1) if distance else pieces[j]
                block = jnp.where(lane // share == j, moved, block)
            largest = jnp.max(jnp.abs(block), axis=0, keepdims=True)
            power = jnp.floor(jnp.log2(jnp.maximum(largest, 1e-30)) * STEPS) + 1.0
            block = jnp.floor(block * (CODES * jnp.exp2(power * (-1.0 / STEPS))) + 0.5)
            rim = pltpu.roll(block[rows:], 2, 0)
            rim = jnp.where(sub_lanes == 0, power, jnp.where(sub_lanes < 3, rim, 0.0))
            base = (half * (128 // share) + place) * (rows + 4)
            codes[base : base + 4, :] = rim[:4]
            codes[base + 4 : base + 4 + rows, :] = block[:rows]
    packed = codes[...].astype(jnp.int32).astype(jnp.int16)
    for side in range(planes):
        out[side * packed.shape[0] : (side + 1) * packed.shape[0], :] = packed


def solve_kernel(kyr, depth, capacity, reach, received, basis, green, out, codes):
    planes = green.shape[1]
    sources = received.shape[0] // reach
    codes[...] = received[...].astype(jnp.int32).astype(jnp.float32)
    power = codes[pl.ds(0, sources, stride=reach), :]
    scale = jnp.exp2(power * (1.0 / STEPS)) * (1.0 / CODES)
    row = lax.broadcasted_iota(jnp.int32, (2 * reach, 128), 0)
    values = []
    for pair in range(0, sources, 2):
        factor = jnp.where(row < reach, scale[pair : pair + 1], scale[pair + 1 : pair + 2])
        values.append(codes[pair * reach : (pair + 2) * reach, :] * factor)
    each = sources // planes // 2
    blocks = [jnp.concatenate(values[i * each : (i + 1) * each], axis=0) for i in range(planes)]
    high, low = split(jnp.concatenate(blocks, axis=1))
    product = matmul(basis[...], high)
    product = product[: 2 * kyr] + product[2 * kyr :] + matmul(basis[: 2 * kyr, :], low)
    cosine = [jnp.zeros((kyr, 128), jnp.float32) for _ in range(depth)]
    sine = [jnp.zeros((kyr, 128), jnp.float32) for _ in range(depth)]
    for block in range(planes):
        lanes = slice(block * 128, (block + 1) * 128)
        for k in range(depth):
            cosine[k] = cosine[k] + green[k, block] * product[:kyr, lanes]
            sine[k] = sine[k] + green[k, block] * product[kyr:, lanes]
    lane = lax.broadcasted_iota(jnp.int32, (kyr, 128), 1)
    share = 2 * capacity

    def gathered(fields):
        fields = [field + pltpu.roll(field, 64, 1) for field in fields]
        field = jnp.where(lane < 64, fields[0], fields[1])
        return field + pltpu.roll(field, share, 1)

    turned = gathered(sine)
    turned = jnp.where(lane % 2 == 0, pltpu.roll(turned, 127, 1), -pltpu.roll(turned, 1, 1))
    result = gathered(cosine) + turned
    flipped = result.T
    for k in range(depth):
        out[:, k, :] = flipped[64 * k + share : 64 * k + 2 * share]


def exchange(array, axis, size, shifted):
    pairs = [(i, i + 1) for i in range(shifted, size - 1, 2)]
    return lax.ppermute(array, axis, pairs + [(j, i) for i, j in pairs])


def in_hbm(array):
    return pltpu.with_memory_space_constraint(array, pltpu.HBM)


def per_device(groups, planes, velocity_x, velocity_y, velocity_z, owners, below, above, metric):
    depth, rows, width = velocity_x.shape
    kxr = owners.shape[0]
    kyr = 2 * kxr
    levels = below.shape[0]
    limit = pltpu.CompilerParams(vmem_limit_bytes=32 * 1024 * 1024)
    fields = (velocity_x, velocity_y, velocity_z)

    plane_shape = jax.ShapeDtypeStruct((3, rows, width), jnp.bfloat16)
    row_shape = jax.ShapeDtypeStruct((8, width), jnp.bfloat16)
    own_one, own_two = pl.pallas_call(
        pack_kernel,
        out_shape=(plane_shape, plane_shape),
        in_specs=[HBM] * 3,
        out_specs=(VMEM,) * 2,
        scratch_shapes=[pltpu.SemaphoreType.DMA((3, 2))],
        compiler_params=limit,
    )(*[in_hbm(field) for field in fields])
    plane_one = exchange(own_one, "gz", planes, 0)
    plane_two = exchange(own_two, "gz", planes, 1)
    row_one, row_two = pl.pallas_call(
        row_kernel,
        out_shape=(row_shape, row_shape),
        in_specs=[VMEM] * 2,
        out_specs=(VMEM,) * 2,
        compiler_params=limit,
    )(own_one, own_two)
    row_one = exchange(row_one, "gy", groups, 0)
    row_two = exchange(row_two, "gy", groups, 1)

    table, factors = [jnp.asarray(array) for array in x_tables(width, kxr, rows * groups)]
    if 2 * kxr == 128:
        pick_shape = jax.ShapeDtypeStruct((8, groups * CAP * 2), jnp.int32)
    else:
        pick_shape = jax.ShapeDtypeStruct((2 * kxr, groups * CAP * 2), jnp.bfloat16)
    pick, green, table, factors = pl.pallas_call(
        functools.partial(mode_kernel, groups, CAP, kyr, levels, depth),
        out_shape=(
            pick_shape,
            jax.ShapeDtypeStruct((depth, planes, kyr, 128), jnp.float32),
            jax.ShapeDtypeStruct(table.shape, table.dtype),
            jax.ShapeDtypeStruct(factors.shape, factors.dtype),
        ),
        in_specs=[HBM] * 6,
        out_specs=(VMEM,) * 4,
        scratch_shapes=[
            pltpu.VMEM((1, kxr), jnp.int32),
            pltpu.SMEM((3, levels), jnp.float32),
            pltpu.SemaphoreType.DMA((5,)),
            pltpu.SemaphoreType.DMA((4,)),
        ],
        compiler_params=limit,
    )(*map(in_hbm, (owners.reshape(1, kxr), below, above, metric, table, factors)))

    strain, spectra = pl.pallas_call(
        functools.partial(early_kernel, groups, planes),
        out_shape=(
            jax.ShapeDtypeStruct((depth, 5, rows, width), jnp.float32),
            jax.ShapeDtypeStruct((3 * (rows + MARGIN) + 6 * MARGIN, 2 * kxr), jnp.float32),
        ),
        in_specs=[VMEM] * 4,
        out_specs=(VMEM,) * 2,
        scratch_shapes=[pltpu.VMEM((2, PIECES * (5 * rows + 6 * MARGIN), width // 2), jnp.bfloat16)],
        compiler_params=limit,
    )(own_one, own_two, table, factors)

    reach = rows + 4
    held = pltpu.VMEM((2, PIECES * 7 * rows, width // 2), jnp.bfloat16)
    earlier, ready = pl.pallas_call(
        late_kernel,
        out_shape=(
            jax.ShapeDtypeStruct((3 * (rows + MARGIN), 2 * kxr), jnp.float32),
            jax.ShapeDtypeStruct((8, rows, width), jnp.float32),
        ),
        in_specs=[VMEM] * 9,
        out_specs=(VMEM,) * 2,
        scratch_shapes=[held],
        compiler_params=limit,
    )(own_one, own_two, plane_one, row_one, row_two, strain, table, spectra, factors)
    outgoing = pl.pallas_call(
        functools.partial(last_kernel, planes, groups, CAP),
        out_shape=jax.ShapeDtypeStruct((planes * groups * reach, 128), jnp.int16),
        in_specs=[VMEM] * 7,
        out_specs=VMEM,
        scratch_shapes=[held, pltpu.VMEM((groups * reach, 128), jnp.float32)],
        compiler_params=limit,
    )(plane_two, ready, table, earlier, spectra, factors, pick)
    outgoing = outgoing.reshape(planes * groups, reach // 2, 2, 128)
    received = lax.all_to_all(outgoing, ("gz", "gy"), split_axis=0, concat_axis=0, tiled=True)
    received = received.reshape(planes * groups * reach, 128)

    basis = jnp.asarray(y_tables(rows, groups, kyr))
    solved = pl.pallas_call(
        functools.partial(solve_kernel, kyr, depth, CAP, reach),
        out_shape=jax.ShapeDtypeStruct((CAP * 2, depth, kyr), jnp.float32),
        in_specs=[VMEM] * 3,
        out_specs=VMEM,
        scratch_shapes=[pltpu.VMEM(received.shape, jnp.float32)],
        compiler_params=limit,
    )(received, basis, green)
    return solved.reshape(1, CAP, 2, depth, kyr)


def solution(mesh):
    placed = (P("gz", "gy", None), P("gz", "gy", None), P("gz", "gy", None), P(), P(), P(), P())
    return jax.shard_map(
        functools.partial(per_device, mesh.shape["gy"], mesh.shape["gz"]),
        mesh=mesh,
        in_specs=placed,
        out_specs=P("gy", None, None, "gz", None),
        check_vma=False,
    )
```
